32 devices in a mesh: row: 8 (over y, x, core), col: 4 (over z).
Axes of the slice: x: 2, y: 2, z: 4, core: 2. Of those that a mesh axis runs over, the one named last changes fastest.
Arguments:
- cached_inverse: float32 [4, 8, 128, 8, 4, 128], P(None, 'row', None, None, 'col'), may hold values from -6 to 6
- parent_panel: float32 [256, 24, 128], P('col', 'row'), may hold values from -0.09375 to 0.09375
- parent_blocks: int32 [24], P('row'), may hold values from -1 to 31, as said below
- parent_sizes: int32 [24], P('row'), may hold values from 0 to 128, as said below
- parent_diagonal: float32 [256, 256], P('col'), may hold values from -6 to 6
- child_panel: float32 [256, 24, 128], P('col', 'row'), may hold values from -0.09375 to 0.09375
- child_top: float32 [256, 256], P('col'), may hold values from -0.375 to 0.375
- child_blocks: int32 [24], P('row'), may hold values from -1 to 31, as said below
- child_sizes: int32 [24], P('row'), may hold values from 0 to 128, as said below
- child_diagonal: float32 [256, 256], P('col'), may hold values from -6 to 6
Outputs:
- parent_rows: float32 [4, 8, 128, 256], P(None, 'row', 'col')
- parent_diag: float32 [256, 256], P('col')
- child_rows: float32 [4, 8, 128, 256], P(None, 'row', 'col')
- child_upper: float32 [256, 256], P('col')
- child_diag: float32 [256, 256], P('col')
The draws below stay inside these ranges and needn't reach their ends.
Inputs may be any that keep to these rules, and one draw needn't show every extreme that they name: `parent_blocks`: slots p*3 to p*3 + 2 belong to index p of row; their live slots come first, name distinct block numbers congruent to p modulo the size of row, and the rest hold -1. Some index of row has 3 live slots. `parent_sizes`: 0 exactly for the slots that hold -1 in parent_blocks. `child_blocks`: slot k holds either parent_blocks[k] (a live parent slot) or -1. `child_sizes`: 0 exactly for the slots that hold -1 in child_blocks, else at most parent_sizes of the same slot.
All inputs are finite; a program needn't handle non-finite values.
Results may differ from the reference program's by a relative error of at most 0.000096.
Values sent between devices are 32-bit elements; how exact they have to be, the bound alone decides.
No kernel may reach another device: no remote copies, remote signals or barrier semaphores. Data moves between devices by JAX's collectives and lax.ppermute only.
A program may use at most 64 MiB of HBM per device.

```python
import jax
import jax.numpy as jnp
from jax import lax

W = 256
B = 128
RC = 4
RPD = 3
NB = 32
M = 4096
CC = 8
SLOTS = 24
N_ROW = 8
N_COL = 4


def structure(key):
    rows_total = NB // RC
    key_list = jax.random.split(jax.random.fold_in(key, 11), 5)
    counts = jax.random.randint(key_list[0], (rows_total,), 1, RPD + 1)
    counts = counts.at[0].set(RPD).at[1].set(1)
    scores = jax.random.randint(key_list[1], (rows_total, RC), 0, 1 << 20) * RC + jnp.arange(RC, dtype=jnp.int32)[None, :]
    scores = scores.at[rows_total - 1, RC - 1].set(-1)
    ranking = jnp.argsort(scores, axis=1, stable=True)[:, :RPD].astype(jnp.int32)
    slot_index = jnp.arange(RPD, dtype=jnp.int32)
    is_live = slot_index[None, :] < counts[:, None]
    owner_row = jnp.arange(rows_total, dtype=jnp.int32)[:, None]
    blocks = jnp.where(is_live, ranking * rows_total + owner_row, -1)
    block_sizes = jnp.where(is_live, jax.random.randint(key_list[2], (rows_total, RPD), 1, B + 1), 0)
    block_sizes = block_sizes.at[0, 0].set(B)
    retained = jax.random.randint(key_list[3], (rows_total, RPD), 0, 5) < 3
    retained = retained.at[0, 0].set(True).at[rows_total - 1, 0].set(True)
    child_live = is_live & retained
    child_blocks = jnp.where(child_live, blocks, -1)
    child_sizes = jnp.where(child_live, jax.random.randint(key_list[4], (rows_total, RPD), 1, jnp.maximum(block_sizes, 1) + 1), 0)
    child_sizes = child_sizes.at[0, 0].set(B)
    return (blocks.reshape(-1).astype(jnp.int32), block_sizes.reshape(-1).astype(jnp.int32), child_blocks.reshape(-1).astype(jnp.int32), child_sizes.reshape(-1).astype(jnp.int32))


def draw_parent_blocks(key, part):
    return structure(key)[0]


def draw_parent_sizes(key, part):
    return structure(key)[1]


def draw_child_blocks(key, part):
    return structure(key)[2]


def draw_child_sizes(key, part):
    return structure(key)[3]


def block_scale(rng, shape, cuts, smallest, top_value):
    loudness, own = 1.0, jax.random.fold_in(rng, 6)
    for axis_at, blocks in cuts:
        draws = jnp.exp(jax.random.uniform(jax.random.fold_in(own, axis_at), (blocks,), jnp.float32, smallest / len(cuts), top_value / len(cuts)))
        loudness = loudness * jnp.repeat(draws, shape[axis_at] // blocks).reshape([-1 if axis == axis_at else 1 for axis in range(len(shape))])
    return loudness


def gaussian(own_key, extent, width, limit, cuts=(), kind=jnp.bfloat16):
    result = width * jax.random.normal(own_key, extent, jnp.float32)
    if cuts:
        result = result * block_scale(own_key, extent, cuts, -0.22, 0.18)
    return jnp.clip(result, -limit, limit).astype(kind)


def setup_inputs(seed: int = 0) -> dict:
    arg_keys = jax.random.split(jax.random.key(seed), 11)
    return {
        "cached_inverse": gaussian(arg_keys[0], (RC, N_ROW, B, CC, N_COL, B), 1.0, 6.0, ((1, 8), (4, 4)), jnp.float32),
        "parent_panel": gaussian(arg_keys[1], (W, SLOTS, B), M ** -0.5, 0.09375, ((0, 4), (1, 8)), jnp.float32),
        "parent_blocks": draw_parent_blocks(jax.random.fold_in(arg_keys[10], 71), 0),
        "parent_sizes": draw_parent_sizes(jax.random.fold_in(arg_keys[10], 71), 0),
        "parent_diagonal": gaussian(arg_keys[4], (W, W), 1.0, 6.0, ((0, 4),), jnp.float32),
        "child_panel": gaussian(arg_keys[5], (W, SLOTS, B), M ** -0.5, 0.09375, ((0, 4), (1, 8)), jnp.float32),
        "child_top": gaussian(arg_keys[6], (W, W), W ** -0.5, 0.375, ((0, 4),), jnp.float32),
        "child_blocks": draw_child_blocks(jax.random.fold_in(arg_keys[10], 71), 0),
        "child_sizes": draw_child_sizes(jax.random.fold_in(arg_keys[10], 71), 0),
        "child_diagonal": gaussian(arg_keys[9], (W, W), 1.0, 6.0, ((0, 4),), jnp.float32),
    }


highest = lax.Precision.HIGHEST


def dense_panel(panel, blocks, sizes):
    row_live = (jnp.arange(B, dtype=jnp.int32)[None, :] < sizes[:, None]).astype(jnp.float32)
    onehot = (blocks[None, :] == jnp.arange(NB, dtype=jnp.int32)[:, None]).astype(jnp.float32)
    masked = panel * row_live[None, :, :]
    dense = jnp.einsum("nk,wkb->nbw", onehot, masked, precision=highest).reshape(M, W)
    row_mask = jnp.einsum("nk,kb->nb", onehot, row_live, precision=highest).reshape(M)
    return dense, row_mask


def reference(cached_inverse, parent_panel, parent_blocks, parent_sizes, parent_diagonal, child_panel, child_top, child_blocks, child_sizes, child_diagonal):
    matrix = cached_inverse.reshape(M, M)
    parent_dense, parent_mask = dense_panel(parent_panel, parent_blocks, parent_sizes)
    parent_rows = -jnp.dot(matrix, parent_dense, precision=highest, preferred_element_type=jnp.float32) * parent_mask[:, None]
    parent_diag = parent_diagonal - jnp.dot(parent_dense.T, parent_rows, precision=highest, preferred_element_type=jnp.float32)
    child_dense, child_mask = dense_panel(child_panel, child_blocks, child_sizes)
    child_rows = -(jnp.dot(matrix, child_dense, precision=highest, preferred_element_type=jnp.float32) + jnp.dot(parent_rows, child_top, precision=highest, preferred_element_type=jnp.float32)) * child_mask[:, None]
    child_upper = -(jnp.dot(parent_diag, child_top, precision=highest, preferred_element_type=jnp.float32) + jnp.dot(parent_rows.T, child_dense, precision=highest, preferred_element_type=jnp.float32))
    child_diag = child_diagonal - jnp.dot(child_top.T, child_upper, precision=highest, preferred_element_type=jnp.float32) - jnp.dot(child_dense.T, child_rows, precision=highest, preferred_element_type=jnp.float32)
    return (parent_rows.reshape(RC, N_ROW, B, W), parent_diag, child_rows.reshape(RC, N_ROW, B, W), child_upper, child_diag)
```

```python
import functools

import jax
import jax.numpy as jnp
from jax import lax
from jax.experimental import pallas as pl
from jax.experimental.pallas import tpu as pltpu
from jax.sharding import PartitionSpec as P

f32 = jnp.float32
bf16 = jnp.bfloat16

NN = (((1,), (0,)), ((), ()))
NT = (((1,), (1,)), ((), ()))
TN = (((0,), (0,)), ((), ()))


def split(value):
    high = value.astype(bf16)
    return high, (value - high.astype(f32)).astype(bf16)


def dot3(left, right, dims):
    (lh, ll), (rh, rl) = left, right
    dot = functools.partial(lax.dot_general, dimension_numbers=dims, preferred_element_type=f32)
    return dot(lh, rh) + (dot(lh, rl) + dot(ll, rh))


def vmem(count):
    return [pl.BlockSpec(memory_space=pltpu.VMEM)] * count


def smem(count):
    return [pl.BlockSpec(memory_space=pltpu.SMEM)] * count


def call(kernel, scalars, arrays, outs, scratch=(), flops=0):
    nbytes = sum(a.size * 4 for a in arrays) + sum(4 * o[0] * o[1] for o in outs)
    return pl.pallas_call(
        kernel,
        out_shape=[jax.ShapeDtypeStruct(o, f32) for o in outs],
        in_specs=smem(len(scalars)) + vmem(len(arrays)),
        out_specs=vmem(len(outs)),
        scratch_shapes=list(scratch),
        compiler_params=pltpu.CompilerParams(vmem_limit_bytes=48 * 1024 * 1024),
        cost_estimate=pl.CostEstimate(flops=flops, bytes_accessed=nbytes, transcendentals=0),
    )(*scalars, *arrays)


def exchange(value, mask, row_total):
    return lax.ppermute(value, "row", [(i, i ^ mask) for i in range(row_total)])


def shift(value, step, col_total):
    return lax.ppermute(value, "col", [(i, (i + step) % col_total) for i in range(col_total)])


class Shape:
    def __init__(self, rows, cols, panel, cached, width):
        self.R, self.C = rows, cols
        self.ws, self.slots, self.B = panel.shape
        self.W = width
        self.RC = cached.shape[0]
        self.CC = cached.shape[3]
        self.Q = rows // cols
        self.payload = self.slots * 2 * self.ws
        self.piece = self.payload // cols
        self.chunk = self.ws // 2
        self.share = self.B // cols
        self.chips = rows // 2
        self.eight = self.ws // rows


def pack(s, blocks, psize, csize, parent, child, top, *outs):
    sends, payload = outs[: s.C], outs[s.C]
    col = lax.axis_index("col")
    lane = lax.broadcasted_iota(jnp.int32, (s.ws, s.B), 1)
    for slot in range(s.slots):
        base = slot * 2 * s.ws
        for which, panel, sizes in ((0, parent, psize), (1, child, csize)):
            live = jnp.where(lane < sizes[slot], panel[:, slot, :], 0.0)
            payload[base + which * s.ws : base + (which + 1) * s.ws, :] = live
    half = s.W // s.B
    for part in range(half):
        start = s.payload + part * s.ws
        payload[start : start + s.ws, :] = top[:, part * s.B : (part + 1) * s.B]
    row8 = lax.broadcasted_iota(jnp.int32, (8, s.B), 0)
    ids = jnp.zeros((8, s.B), f32)
    for slot in range(s.slots):
        ids = jnp.where(row8 == slot, blocks[slot].astype(f32), ids)
    for turn in range(s.C):
        start = pl.multiple_of(lax.rem(turn - col + s.C, s.C) * s.piece, s.piece)
        sends[turn][: s.piece, :] = payload[pl.ds(start, s.piece), :]
        sends[turn][s.piece :, :] = ids


def join(s, *refs):
    pieces, out = refs[: s.C], refs[s.C]
    part = lax.rem(lax.axis_index("row"), s.C)
    for turn in range(s.C):
        start = pl.multiple_of(lax.rem(turn - part + s.C, s.C) * s.piece, s.piece)
        out[pl.ds(start, s.piece), :] = pieces[turn][: s.piece, :]
    out[s.payload :, :] = pieces[0][s.piece :, :]


def main(s, blocks, cached, pd, *refs):
    panels, refs = refs[: s.R], refs[s.R :]
    owned, refs = refs[: s.C], refs[s.C :]
    shares, refs = refs[: s.C], refs[s.C :]
    keep, send, base, top, refs = refs[0], refs[1], refs[2], refs[3], refs[4:]
    xh, xl, ph, plo, sh, sl, total, both = refs
    row, col = lax.axis_index("row"), lax.axis_index("col")
    per = s.piece // s.chunk
    for mask in range(s.R):
        part = lax.rem(jnp.bitwise_xor(row, mask), s.C)
        for i in range(per):
            at = part * per + i
            group, off = lax.div(at, 2), lax.rem(at, 2) * s.chunk
            slot, which = lax.div(group, 2), lax.rem(group, 2)
            for source in range(s.C):
                start = source * s.piece + i * s.chunk
                high, low = split(panels[mask][start : start + s.chunk, :])
                dest = pl.multiple_of(which * s.W + source * s.ws + off, s.chunk)
                lead = (mask // s.C) * s.slots + slot
                xh[lead, pl.ds(dest, s.chunk), :] = high
                xl[lead, pl.ds(dest, s.chunk), :] = low
    for step in range(s.C):
        source = lax.rem(col - step + s.C, s.C)
        for slot in range(s.slots):
            for which in range(2):
                start = (slot * 2 + which) * s.ws
                high, low = split(owned[step][start : start + s.ws, :])
                dest = pl.multiple_of(which * s.W + source * s.ws, s.ws)
                ph[slot, pl.ds(dest, s.ws), :] = high
                plo[slot, pl.ds(dest, s.ws), :] = low
        for part in range(s.W // s.B):
            start = s.payload + part * s.ws
            dest = pl.multiple_of(source * s.ws, s.ws)
            top[pl.ds(dest, s.ws), part * s.B : (part + 1) * s.B] = owned[step][
                start : start + s.ws, :
            ]
    for slot in range(s.slots):
        p = lax.div(jnp.maximum(blocks[slot], 0), s.R)
        for other in range(s.Q):
            for k in range(s.slots):
                at = s.payload + k
                number = jnp.max(panels[other * s.C][at : at + 1, :]).astype(jnp.int32)
                m = lax.div(jnp.maximum(number, 0), s.C)
                start = p * (s.B * s.CC) + m
                high, low = split(cached[pl.ds(start, s.B, stride=s.CC), :])
                lead = (other * s.slots + k) * s.B
                sh[slot * s.B : (slot + 1) * s.B, lead : lead + s.B] = high
                sl[slot * s.B : (slot + 1) * s.B, lead : lead + s.B] = low
    wide = s.Q * s.slots
    right = tuple(jnp.concatenate([x[i] for i in range(wide)], axis=1) for x in (xh, xl))
    total[...] = dot3((sh[...], sl[...]), right, NT)
    for step in range(s.C):
        target = lax.rem(col + step, s.C)
        for slot in range(s.slots):
            start = pl.multiple_of(slot * s.B + target * s.share, s.share)
            shares[step][slot * s.share : (slot + 1) * s.share, :] = total[pl.ds(start, s.share), :]
    left = tuple(jnp.concatenate([x[i] for i in range(s.slots)], axis=1) for x in (ph, plo))
    lower = tuple(x[s.W :, :] for x in left)
    ab = dot3(left, split(total[:, : s.W]), NN)
    a, b = ab[: s.W], ab[s.W :]
    d = dot3(lower, split(total[:, s.W :]), NN)
    top_full = split(top[...])
    u = b.T - dot3(split(a), top_full, NN)
    parts = [owned[0][s.payload + i * s.ws : s.payload + (i + 1) * s.ws, :] for i in range(s.W // s.B)]
    top_own = split(jnp.concatenate(parts, axis=1))
    lead = dot3(split(pd[...]), top_full, NN)
    base[...] = -lead
    cd = d - dot3(split(b), top_full, NN) - dot3(top_full, split(u), TN)
    cd = cd + dot3(top_own, split(lead * (1.0 / s.R)), TN)
    both[0 : s.W, :] = a
    both[s.W : 2 * s.W, :] = u
    both[2 * s.W :, :] = cd
    core = lax.rem(row, 2)
    n = s.eight
    for out, flip in ((keep, 0), (send, 1)):
        offset = jnp.bitwise_xor(core, flip) * (s.ws // 2)
        for chip in range(s.chips):
            for source in range(s.C):
                for kind in range(3):
                    at = pl.multiple_of(kind * s.W + source * s.ws + chip * n + offset, n)
                    to = ((chip * s.C + source) * 3 + kind) * n
                    out[to : to + n, :] = both[pl.ds(at, n), :]


def add_chips(s, kept, got, *outs):
    size = s.C * 3 * s.eight
    chip = lax.div(lax.axis_index("row"), 2)
    for mask in range(s.chips):
        rows = pl.ds(pl.multiple_of(jnp.bitwise_xor(chip, mask) * size, size), size)
        outs[mask][...] = kept[rows, :] + got[rows, :]


def add_cols(s, *refs):
    terms, outs, total = refs[: s.chips], refs[s.chips : -1], refs[-1]
    size = 3 * s.eight
    col = lax.axis_index("col")
    value = terms[0][...]
    for term in terms[1:]:
        value = value + term[...]
    total[...] = value
    for step in range(s.C):
        rows = pl.ds(pl.multiple_of(lax.rem(col + step, s.C) * size, size), size)
        outs[step][...] = total[rows, :]


def add_all(s, *refs):
    value = refs[0][...]
    for term in refs[1:-1]:
        value = value + term[...]
    refs[-1][...] = value


def finish(s, pd, cd, base, *refs):
    parts, outs = refs[: s.R], refs[s.R :]
    row = lax.axis_index("row")
    n = s.eight
    starts = (pd, base, cd)
    for mask in range(s.R):
        source = jnp.bitwise_xor(row, mask)
        at = lax.rem(source, 2) * (s.ws // 2) + lax.div(source, 2) * n
        rows = pl.ds(pl.multiple_of(at, n), n)
        for kind in range(3):
            outs[kind][rows, :] = starts[kind][rows, :] + parts[mask][kind * n : (kind + 1) * n, :]


def rows_out(s, blocks, psize, csize, top, *refs):
    terms, (parent, child) = refs[: s.C], refs[s.C :]
    first = lax.axis_index("col") * s.share
    value = terms[0][...]
    for term in terms[1:]:
        value = value + term[...]
    index = lax.broadcasted_iota(jnp.int32, (s.share, s.W), 0) + first
    plive = jnp.concatenate([index < psize[k] for k in range(s.slots)], axis=0)
    clive = jnp.concatenate([index < csize[k] for k in range(s.slots)], axis=0)
    y = jnp.where(plive, -value[:, : s.W], 0.0)
    carried = dot3(split(y), split(top[...]), NN)
    z = jnp.where(clive, -(value[:, s.W :] + carried), 0.0)
    parent[...] = jnp.zeros_like(parent)
    child[...] = jnp.zeros_like(child)
    for slot in range(s.slots):
        @pl.when(blocks[slot] >= 0)
        def _():
            at = lax.div(blocks[slot], s.R) * s.share
            rows = pl.ds(pl.multiple_of(at, s.share), s.share)
            parent[rows, :] = y[slot * s.share : (slot + 1) * s.share, :]
            child[rows, :] = z[slot * s.share : (slot + 1) * s.share, :]


def scatter_perm(s, turn):
    return [
        ((q * s.C + a) * s.C + c, (q * s.C + (turn - c) % s.C) * s.C + a)
        for q in range(s.Q)
        for a in range(s.C)
        for c in range(s.C)
    ]


def fast_body(
    cached_inverse,
    parent_panel,
    parent_blocks,
    parent_sizes,
    parent_diagonal,
    child_panel,
    child_top,
    child_blocks,
    child_sizes,
    child_diagonal,
):
    R, C = lax.axis_size("row"), lax.axis_size("col")
    B = cached_inverse.shape[2]
    s = Shape(R, C, parent_panel, cached_inverse, parent_diagonal.shape[1])
    cached = cached_inverse.reshape(-1, B)
    bind = lambda kernel: functools.partial(kernel, s)
    sent = (s.piece + 8, B)
    whole = (s.payload + (s.W // B) * s.ws, B)
    with jax.named_scope("pack"):
        *sends, payload = call(
            bind(pack),
            (parent_blocks, parent_sizes, child_sizes),
            (parent_panel, child_panel, child_top),
            [sent] * C + [whole],
        )
    with jax.named_scope("scatter"):
        pieces = [
            lax.ppermute(sends[t], ("row", "col"), scatter_perm(s, t)) for t in range(C)
        ]
    with jax.named_scope("join"):
        (own,) = call(bind(join), (), pieces, [(s.payload + 8, B)])
    with jax.named_scope("panels"):
        panels = {0: own}
        for mask in range(2, R, 2):
            panels[mask] = exchange(own, mask, R)
        for mask in range(0, R, 2):
            panels[mask + 1] = exchange(panels[mask], 1, R)
    with jax.named_scope("owned"):
        owned = [payload] + [shift(payload, k, C) for k in range(1, C)]
    W, ws = s.W, s.ws
    D = 3 * W
    wide = s.Q * s.slots
    live = s.slots * B
    scratch = [
        pltpu.VMEM((wide, 2 * W, B), bf16),
        pltpu.VMEM((wide, 2 * W, B), bf16),
        pltpu.VMEM((s.slots, 2 * W, B), bf16),
        pltpu.VMEM((s.slots, 2 * W, B), bf16),
        pltpu.VMEM((live, wide * B), bf16),
        pltpu.VMEM((live, wide * B), bf16),
        pltpu.VMEM((live, 2 * W), f32),
        pltpu.VMEM((D, W), f32),
    ]
    outs = [(s.slots * s.share, 2 * W)] * C + [(D // 2, W), (D // 2, W), (ws, W), (W, W)]
    with jax.named_scope("products"):
        out = call(
            bind(main),
            (parent_blocks,),
            (cached, parent_diagonal, *[panels[m] for m in range(R)], *owned),
            outs,
            scratch,
            flops=2 * live * wide * B * 2 * W * 3,
        )
    shares, (keep, send, base, top) = out[:C], out[C:]
    with jax.named_scope("sum_core"):
        got = exchange(send, 1, R)
    with jax.named_scope("sum_shares"):
        rows = [shares[0]] + [shift(shares[k], k, C) for k in range(1, C)]
    with jax.named_scope("sum_chips"):
        mine = call(bind(add_chips), (), (keep, got), [(C * 3 * s.eight, W)] * s.chips)
        mine = [mine[0]] + [exchange(mine[m], 2 * m, R) for m in range(1, s.chips)]
    with jax.named_scope("sum_cols"):
        scr = [pltpu.VMEM((C * 3 * s.eight, W), f32)]
        cols = call(bind(add_cols), (), mine, [(3 * s.eight, W)] * C, scr)
        cols = [cols[0]] + [shift(cols[k], k, C) for k in range(1, C)]
    with jax.named_scope("spread"):
        (done,) = call(bind(add_all), (), cols, [(3 * s.eight, W)])
        parts = {0: done}
        for mask in range(2, R, 2):
            parts[mask] = exchange(done, mask, R)
        for mask in range(0, R, 2):
            parts[mask + 1] = exchange(parts[mask], 1, R)
    with jax.named_scope("rows_out"):
        parent_rows, child_rows = call(
            bind(rows_out),
            (parent_blocks, parent_sizes, child_sizes),
            (top, *rows),
            [(s.RC * s.share, W)] * 2,
        )
    with jax.named_scope("finish"):
        parent_diag, child_upper, child_diag = call(
            bind(finish),
            (),
            (parent_diagonal, child_diagonal, base, *[parts[m] for m in range(R)]),
            [(ws, W)] * 3,
        )
    shape = (s.RC, 1, s.share, W)
    return (
        parent_rows.reshape(shape),
        parent_diag,
        child_rows.reshape(shape),
        child_upper,
        child_diag,
    )


highest = lax.Precision.HIGHEST


def from_root(value, axis, source):
    kept = jnp.where(lax.axis_index(axis) == source, value, 0).astype(value.dtype)
    return lax.psum(kept, axis)


def live_rows(sizes, block_rows):
    return (jnp.arange(block_rows, dtype=jnp.int32)[None, :] < sizes[:, None]).astype(jnp.float32)


def own_share(widened, blocks, row_live, row_index, row_total, col_index, row_share, local_rows):
    wanted = jnp.arange(local_rows, dtype=jnp.int32) * row_total + row_index
    onehot = (blocks[None, :] == wanted[:, None]).astype(jnp.float32)
    sliced = lax.dynamic_slice_in_dim(widened, col_index * row_share, row_share, 2)
    own_rows = jnp.einsum("rk,wkb->rbw", onehot, sliced, precision=highest)
    live_part = lax.dynamic_slice_in_dim(row_live, col_index * row_share, row_share, 1)
    row_alive = jnp.einsum("rk,kb->rb", onehot, live_part, precision=highest)
    return (own_rows, row_alive)


def add_columns(column_dense, widened, blocks, col_index, col_total):
    wanted = jnp.arange(column_dense.shape[0], dtype=jnp.int32) * col_total + col_index
    onehot = (blocks[None, :] == wanted[:, None]).astype(jnp.float32)
    return column_dense + jnp.einsum("ck,wky->cwy", onehot, widened, precision=highest)


def column_panel(widened, blocks, col_index, col_total, row_total, col_blocks):
    column_dense = jnp.zeros((col_blocks, widened.shape[0], widened.shape[2]), jnp.float32)
    for repeat in range(row_total // col_total):
        sender = col_index + repeat * col_total
        heard_panel, heard_blocks = (
            from_root(widened, "row", sender),
            from_root(blocks, "row", sender),
        )
        column_dense = add_columns(column_dense, heard_panel, heard_blocks, col_index, col_total)
    return column_dense


def child_panels(
    child_panel, child_top, child_live, child_blocks, col_index, col_total, row_total, col_blocks
):
    wide_child, top_full = (
        lax.all_gather(child_panel, "col", axis=0, tiled=True),
        lax.all_gather(child_top, "col", axis=0, tiled=True),
    )
    child_full = wide_child * child_live[None, :, :]
    child_dense = column_panel(
        child_full, child_blocks, col_index, col_total, row_total, col_blocks
    )
    return (child_full, child_dense, top_full)


def apply_inverse(cached, column_dense):
    summed = lax.psum_scatter(
        jnp.einsum(
            "rxcy,cwy->xrw",
            cached,
            column_dense,
            precision=highest,
            preferred_element_type=jnp.float32,
        ),
        "col",
        scatter_dimension=0,
        tiled=True,
    )
    return jnp.transpose(summed, (1, 0, 2))


def diagonal_sum(partial_rows, panel_width, col_share, col_index):
    entire = lax.psum(partial_rows(0, panel_width), ("row", "col"))
    return lax.dynamic_slice_in_dim(entire, col_index * col_share, col_share, 0)


def body(
    cached_inverse,
    parent_panel,
    parent_blocks,
    parent_sizes,
    parent_diagonal,
    child_panel,
    child_top,
    child_blocks,
    child_sizes,
    child_diagonal,
):
    row_total = lax.axis_size("row")
    col_total = lax.axis_size("col")
    row_index = lax.axis_index("row")
    col_index = lax.axis_index("col")
    local_rows = cached_inverse.shape[0]
    block_rows = cached_inverse.shape[2]
    col_blocks = cached_inverse.shape[3]
    cached = cached_inverse.reshape(local_rows, block_rows, col_blocks, block_rows)
    panel_width = parent_diagonal.shape[1]
    row_share = block_rows // col_total
    col_share = panel_width // col_total
    parent_live = live_rows(parent_sizes, block_rows)
    child_live = live_rows(child_sizes, block_rows)
    wide_parent = lax.all_gather(parent_panel, "col", axis=0, tiled=True)
    parent_full = wide_parent * parent_live[None, :, :]
    parent_dense = column_panel(
        parent_full, parent_blocks, col_index, col_total, row_total, col_blocks
    )
    child_full, child_dense, top_full = child_panels(
        child_panel,
        child_top,
        child_live,
        child_blocks,
        col_index,
        col_total,
        row_total,
        col_blocks,
    )
    parent_own, parent_alive = own_share(
        parent_full,
        parent_blocks,
        parent_live,
        row_index,
        row_total,
        col_index,
        row_share,
        local_rows,
    )
    both_local = apply_inverse(cached, jnp.concatenate([parent_dense, child_dense], axis=1))
    parent_local = -both_local[:, :, :panel_width] * parent_alive[:, :, None]
    child_own, child_alive = own_share(
        child_full, child_blocks, child_live, row_index, row_total, col_index, row_share, local_rows
    )
    carried = jnp.einsum("rbw,wv->rbv", parent_local, top_full, precision=highest)
    child_local = -(both_local[:, :, panel_width:] + carried) * child_alive[:, :, None]

    def stacked_terms(offset, amount):
        first_part = jnp.einsum("rbw,rbv->wv", parent_own, parent_local, precision=highest)
        second_part = jnp.einsum("rbw,rbv->wv", parent_local, child_own, precision=highest)
        third_part = jnp.einsum("rbc,rbv->cv", child_own, child_local, precision=highest)
        return jnp.concatenate([first_part, second_part, third_part], axis=1)

    stacked_sum = diagonal_sum(stacked_terms, panel_width, col_share, col_index)
    parent_diag = parent_diagonal - stacked_sum[:, :panel_width]
    child_upper = -(
        jnp.dot(parent_diag, top_full, precision=highest, preferred_element_type=jnp.float32)
        + stacked_sum[:, panel_width : 2 * panel_width]
    )
    upper_whole = lax.all_gather(child_upper, "col", axis=0, tiled=True)
    top_columns = lax.dynamic_slice_in_dim(top_full, col_index * col_share, col_share, 1)
    child_diag = (
        child_diagonal
        - jnp.dot(top_columns.T, upper_whole, precision=highest, preferred_element_type=jnp.float32)
        - stacked_sum[:, 2 * panel_width :]
    )
    return (
        parent_local[:, None, :, :],
        parent_diag,
        child_local[:, None, :, :],
        child_upper,
        child_diag,
    )


def fits(rows, cols, panel, cached, width):
    s = Shape(rows, cols, panel, cached, width)
    return (
        rows & (rows - 1) == 0
        and rows % cols == 0
        and s.payload % cols == 0
        and s.chunk % 16 == 0
        and s.piece % s.chunk == 0
        and s.share % 16 == 0
        and s.ws % rows == 0
        and s.eight % 8 == 0
        and width % s.B == 0
    )


def chosen(*args):
    sizes = lax.axis_size("row"), lax.axis_size("col")
    ok = fits(*sizes, args[1], args[0], args[4].shape[1])
    return (fast_body if ok else body)(*args)


def solution(mesh):
    in_specs = (
        P(None, "row", None, None, "col", None),
        P("col", "row", None),
        P("row"),
        P("row"),
        P("col", None),
        P("col", "row", None),
        P("col", None),
        P("row"),
        P("row"),
        P("col", None),
    )
    out_specs = (
        P(None, "row", "col", None),
        P("col", None),
        P(None, "row", "col", None),
        P("col", None),
        P("col", None),
    )
    return jax.shard_map(chosen, mesh=mesh, in_specs=in_specs, out_specs=out_specs, check_vma=False)
```

```python
import functools

import jax
import jax.numpy as jnp
from jax import lax
from jax.experimental import pallas as pl
from jax.experimental.pallas import tpu as pltpu
from jax.sharding import PartitionSpec as P

f32 = jnp.float32
bf16 = jnp.bfloat16

NN = (((1,), (0,)), ((), ()))
NT = (((1,), (1,)), ((), ()))
TN = (((0,), (0,)), ((), ()))


def split(value):
    high = value.astype(bf16)
    return high, (value - high.astype(f32)).astype(bf16)


def dot3(left, right, dims):
    (lh, ll), (rh, rl) = left, right
    on_left, on_right = dims[0][0][0], dims[0][1][0]
    return lax.dot_general(
        jnp.concatenate([lh, lh, ll], axis=on_left),
        jnp.concatenate([rh, rl, rh], axis=on_right),
        dims,
        preferred_element_type=f32,
    )


def call(kernel, inputs, outs, scratch=(), flops=0, limit=40, alias=None):
    arrays = [a for _, a in inputs]
    shapes = [jax.ShapeDtypeStruct(*(o if isinstance(o[0], tuple) else (o, f32))) for o in outs]
    nbytes = sum(a.size * a.dtype.itemsize for a in arrays + shapes)
    return pl.pallas_call(
        kernel,
        out_shape=shapes,
        in_specs=[pl.BlockSpec(memory_space=space) for space, _ in inputs],
        out_specs=[pl.BlockSpec(memory_space=pltpu.VMEM)] * len(outs),
        scratch_shapes=list(scratch),
        input_output_aliases=alias or {},
        compiler_params=pltpu.CompilerParams(vmem_limit_bytes=limit and limit * 1024 * 1024),
        cost_estimate=pl.CostEstimate(flops=flops, bytes_accessed=nbytes, transcendentals=0),
    )(*arrays)


def vmem(*arrays):
    return [(pltpu.VMEM, a) for a in arrays]


def smem(*arrays):
    return [(pltpu.SMEM, a) for a in arrays]


def hbm(*arrays):
    return [(pltpu.HBM, a) for a in arrays]


def fetch(sources, targets, sems):
    copies = [
        pltpu.make_async_copy(a, b, sems.at[i]) for i, (a, b) in enumerate(zip(sources, targets))
    ]
    for copy in copies:
        copy.start()
    return copies


def exchange(value, mask, row_total):
    return lax.ppermute(value, "row", [(i, i ^ mask) for i in range(row_total)])


def flip(value, mask, col_total):
    return lax.ppermute(value, "col", [(i, i ^ mask) for i in range(col_total)])


class Shape:
    def __init__(self, rows, cols, panel, cached, width):
        self.R, self.C = rows, cols
        self.ws, self.slots, self.B = panel.shape
        self.W = width
        self.RC = cached.shape[0]
        self.CC = cached.shape[3]
        self.Q = rows // cols
        self.payload = self.slots * 2 * self.ws
        self.piece = self.payload // cols
        self.chunk = self.ws // 2
        self.share = self.B // cols
        self.chips = rows // 2
        self.eight = self.ws // rows
        self.live = self.slots * self.B
        self.parts = self.W // self.B
        self.block = self.payload + 8


def pack(s, *refs):
    sources, refs = refs[:6], refs[6:]
    sends, payload, refs = refs[: s.C], refs[s.C], refs[s.C + 1 :]
    targets, sems = refs[:6], refs[6]
    for copy in fetch(sources, targets, sems):
        copy.wait()
    blocks, psize, csize, parent, child, top = targets
    col = lax.axis_index("col")
    lane = lax.broadcasted_iota(jnp.int32, (s.ws, s.B), 1)
    for slot in range(s.slots):
        base = slot * 2 * s.ws
        for which, panel, sizes in ((0, parent, psize), (1, child, csize)):
            live = jnp.where(lane < sizes[slot], panel[slot], 0.0)
            payload[base + which * s.ws : base + (which + 1) * s.ws, :] = live
    wide = s.W // 2
    mine = lax.rem(lax.axis_index("row"), 2) * wide
    payload[s.payload :, :] = top[:, pl.ds(pl.multiple_of(mine, wide), wide)]
    row8 = lax.broadcasted_iota(jnp.int32, (8, s.B), 0)
    ids = jnp.zeros((8, s.B), f32)
    for slot in range(s.slots):
        ids = jnp.where(row8 == slot, blocks[slot].astype(f32), ids)
    for turn in range(s.C):
        start = pl.multiple_of(lax.rem(turn - col + s.C, s.C) * s.piece, s.piece)
        sends[turn][: s.piece, :] = payload[pl.ds(start, s.piece), :]
        sends[turn][s.piece :, :] = ids


def split_live(s, cached, blocks, high, low, held, numbers, sems):
    copy = pltpu.make_async_copy(blocks, numbers, sems.at[0])
    copy.start()
    copy.wait()
    size = s.B * s.CC
    copies = []
    for slot in range(s.slots):
        p = lax.div(jnp.maximum(numbers[slot], 0), s.R)
        source = cached.at[pl.ds(pl.multiple_of(p * size, size), size), :]
        copy = pltpu.make_async_copy(source, held.at[pl.ds(slot * size, size), :], sems.at[1 + slot])
        copy.start()
        copies.append(copy)
    for slot in range(s.slots):
        copies[slot].wait()
        rows = slice(slot * s.B, (slot + 1) * s.B)
        for m in range(s.CC):
            h, l = split(held[pl.ds(slot * size + m, s.B, stride=s.CC), :])
            high[rows, m * s.B : (m + 1) * s.B] = h
            low[rows, m * s.B : (m + 1) * s.B] = l


def join(s, *refs):
    pieces, out = refs[: s.C], refs[s.C + 2]
    part = lax.rem(lax.axis_index("row"), s.C)
    for turn in range(s.C):
        start = pl.multiple_of(lax.rem(turn - part + s.C, s.C) * s.piece, s.piece)
        out[pl.ds(start, s.piece), :] = pieces[turn][: s.piece, :]
    out[s.payload :, :] = pieces[0][s.piece :, :]


def collect(s, *refs):
    owned, (lh, ll, half, panel) = refs[: s.C], refs[s.C :]
    col = lax.axis_index("col")
    for mask in range(s.C):
        source = jnp.bitwise_xor(col, mask)
        for slot in range(s.slots):
            for which in range(2):
                start = (slot * 2 + which) * s.ws
                dest = pl.multiple_of(which * s.W + source * s.ws, s.ws)
                panel[pl.ds(dest, s.ws), slot * s.B : (slot + 1) * s.B] = owned[mask][
                    start : start + s.ws, :
                ]
        dest = pl.multiple_of(source * s.ws, s.ws)
        half[pl.ds(dest, s.ws), :] = owned[mask][s.payload :, :]
    lh[...], ll[...] = split(panel[...])


def own_panels(s, pd, lh, ll, mine, theirs, vh, vl, th, tl, base, extra, top):
    row, col = lax.axis_index("row"), lax.axis_index("col")
    wide = s.W // 2
    core = lax.rem(row, 2)
    top[:, pl.ds(pl.multiple_of(core * wide, wide), wide)] = mine[...]
    top[:, pl.ds(pl.multiple_of((1 - core) * wide, wide), wide)] = theirs[...]
    th[...], tl[...] = split(top[...])
    full = (th[...], tl[...])
    vh[...], vl[...] = split(dot3(split(top[...].T), (lh[: s.W, :], ll[: s.W, :]), NN))
    lead = dot3(split(pd[...]), full, NN)
    base[...] = -lead
    own = top[pl.ds(pl.multiple_of(col * s.ws, s.ws), s.ws), :]
    extra[...] = dot3(split(own), split(lead * (1.0 / s.R)), TN)


def products(s, sh, sl, lh, ll, vh, vl, th, tl, extra, *refs):
    panels, (stay, leave, keep, send, xh, xl, total, both) = refs[: s.R], refs[s.R :]
    row = lax.axis_index("row")
    core = lax.rem(row, 2)
    places = []
    for owner in range(s.Q):
        for slot in range(s.slots):
            at = s.payload + slot
            number = jnp.max(panels[owner * s.C][at : at + 1, :]).astype(jnp.int32)
            places.append(jnp.where(number < 0, s.CC, lax.div(jnp.maximum(number, 0), s.C)))
    for m in range(s.CC):
        taken = places[0] == m
        for place in places[1:]:
            taken = jnp.logical_or(taken, place == m)

        @pl.when(jnp.logical_not(taken))
        def _():
            xh[m] = jnp.zeros((2 * s.W, s.B), bf16)
            xl[m] = jnp.zeros((2 * s.W, s.B), bf16)

    per = s.piece // s.chunk
    for mask in range(s.R):
        owner = mask // s.C
        part = lax.rem(jnp.bitwise_xor(row, mask), s.C)
        for i in range(per):
            at = part * per + i
            group, off = lax.div(at, 2), lax.rem(at, 2) * s.chunk
            slot, which = lax.div(group, 2), lax.rem(group, 2)
            place = places[owner * s.slots]
            for k in range(1, s.slots):
                place = jnp.where(slot == k, places[owner * s.slots + k], place)
            for source in range(s.C):
                start = source * s.piece + i * s.chunk
                high, low = split(panels[mask][start : start + s.chunk, :])
                dest = pl.multiple_of(which * s.W + source * s.ws + off, s.chunk)
                xh[place, pl.ds(dest, s.chunk), :] = high
                xl[place, pl.ds(dest, s.chunk), :] = low
    right = tuple(jnp.concatenate([x[i] for i in range(s.CC)], axis=1) for x in (xh, xl))
    total[...] = dot3((sh[...], sl[...]), right, NT)
    col = lax.axis_index("col")
    for mask in range(s.C):
        out = leave if mask % 2 else stay
        target = jnp.bitwise_xor(col, mask)
        for slot in range(s.slots):
            start = pl.multiple_of(slot * s.B + target * s.share, s.share)
            to = (mask // 2 * s.slots + slot) * s.share
            out[to : to + s.share, :] = total[pl.ds(start, s.share), :]
    W = s.W
    left = tuple(jnp.concatenate([x[...], y[...]], axis=0) for x, y in ((lh, vh), (ll, vl)))
    first = dot3(left, split(total[:, :W]), NN)
    d = dot3((lh[W:, :], ll[W:, :]), split(total[:, W:]), NN)
    second = dot3(split(first), (th[...], tl[...]), NN)
    both[0:W, :] = first[:W]
    both[W : 2 * W, :] = first[W : 2 * W].T - second[:W]
    cross = second[W : 2 * W]
    both[2 * W :, :] = d - cross - cross.T + second[2 * W :] + extra[...]
    n = s.eight
    for out, swap in ((keep, 0), (send, 1)):
        offset = jnp.bitwise_xor(core, swap) * (s.ws // 2)
        for chip in range(s.chips):
            for source in range(s.C):
                for kind in range(3):
                    at = pl.multiple_of(kind * W + source * s.ws + chip * n + offset, n)
                    to = ((chip * s.C + source) * 3 + kind) * n
                    out[to : to + n, :] = both[pl.ds(at, n), :]


def add_chips(s, kept, got, *outs):
    size = s.C * 3 * s.eight
    chip = lax.div(lax.axis_index("row"), 2)
    for mask in range(s.chips):
        rows = pl.ds(pl.multiple_of(jnp.bitwise_xor(chip, mask) * size, size), size)
        outs[mask][...] = kept[rows, :] + got[rows, :]


def add_cols(s, *refs):
    terms, (kept, got), refs = refs[: s.chips], refs[s.chips : s.chips + 2], refs[s.chips + 2 :]
    outs, (stay, leave, total) = refs[: s.C], refs[s.C :]
    size = 3 * s.eight
    col = lax.axis_index("col")
    value = terms[0][...]
    for term in terms[1:]:
        value = value + term[...]
    total[...] = value
    for mask in range(s.C):
        rows = pl.ds(pl.multiple_of(jnp.bitwise_xor(col, mask) * size, size), size)
        outs[mask][...] = total[rows, :]
    halve(s, kept, got, stay, leave)


def halve(s, kept, got, stay, leave):
    size = s.slots * s.share
    for i in range(kept.shape[0] // size):
        out, at = (leave if i % 2 else stay), i // 2 * size
        rows = slice(i * size, (i + 1) * size)
        out[at : at + size, :] = kept[rows, :] + got[rows, :]


def add_all(s, *refs):
    value = refs[0][...]
    for term in refs[1:-1]:
        value = value + term[...]
    refs[-1][...] = value


def finish(s, pd, cd, base, *refs):
    parts, outs = refs[: s.R], refs[s.R :]
    row = lax.axis_index("row")
    n = s.eight
    starts = (pd, base, cd)
    for mask in range(s.R):
        source = jnp.bitwise_xor(row, mask)
        at = lax.rem(source, 2) * (s.ws // 2) + lax.div(source, 2) * n
        rows = pl.ds(pl.multiple_of(at, n), n)
        for kind in range(3):
            outs[kind][rows, :] = starts[kind][rows, :] + parts[mask][kind * n : (kind + 1) * n, :]


def rows_out(s, blocks, psize, csize, th, tl, kept, got, parent, child):
    value = kept[...] + got[...]
    first = lax.axis_index("col") * s.share
    index = lax.broadcasted_iota(jnp.int32, (s.share, s.W), 0) + first
    plive = jnp.concatenate([index < psize[k] for k in range(s.slots)], axis=0)
    clive = jnp.concatenate([index < csize[k] for k in range(s.slots)], axis=0)
    y = jnp.where(plive, -value[:, : s.W], 0.0)
    carried = dot3(split(y), (th[...], tl[...]), NN)
    z = jnp.where(clive, -(value[:, s.W :] + carried), 0.0)
    parent[...] = jnp.zeros_like(parent)
    child[...] = jnp.zeros_like(child)
    for slot in range(s.slots):

        @pl.when(blocks[slot] >= 0)
        def _():
            at = lax.div(blocks[slot], s.R) * s.share
            rows = pl.ds(pl.multiple_of(at, s.share), s.share)
            parent[rows, :] = y[slot * s.share : (slot + 1) * s.share, :]
            child[rows, :] = z[slot * s.share : (slot + 1) * s.share, :]


def scatter_perm(s, turn):
    return [
        ((q * s.C + a) * s.C + c, (q * s.C + (turn - c) % s.C) * s.C + a)
        for q in range(s.Q)
        for a in range(s.C)
        for c in range(s.C)
    ]


def fast_body(
    cached_inverse,
    parent_panel,
    parent_blocks,
    parent_sizes,
    parent_diagonal,
    child_panel,
    child_top,
    child_blocks,
    child_sizes,
    child_diagonal,
):
    R, C = lax.axis_size("row"), lax.axis_size("col")
    B = cached_inverse.shape[2]
    s = Shape(R, C, parent_panel, cached_inverse, parent_diagonal.shape[1])
    W, ws, live = s.W, s.ws, s.live
    cached = cached_inverse.reshape(-1, B)
    bind = lambda kernel: functools.partial(kernel, s)
    numbers = pltpu.SMEM((s.slots,), jnp.int32)
    by_slot = (s.slots, ws, B)
    with jax.named_scope("pack"):
        *sends, payload = call(
            bind(pack),
            hbm(
                parent_blocks,
                parent_sizes,
                child_sizes,
                jnp.transpose(parent_panel, (1, 0, 2)),
                jnp.transpose(child_panel, (1, 0, 2)),
                child_top,
            ),
            [(s.piece + 8, B)] * C + [(s.payload + ws, B)],
            [numbers] * 3
            + [pltpu.VMEM(by_slot, f32)] * 2
            + [pltpu.VMEM((ws, W), f32), pltpu.SemaphoreType.DMA((6,))],
            limit=None,
        )
    with jax.named_scope("scatter"):
        pieces = [lax.ppermute(sends[t], ("row", "col"), scatter_perm(s, t)) for t in range(C)]
    with jax.named_scope("owned"):
        owned = {0: payload}
        mask = C // 2
        while mask:
            owned.update({m ^ mask: flip(owned[m], mask, C) for m in list(owned)})
            mask //= 2
    with jax.named_scope("split_live"):
        sh, sl = call(
            bind(split_live),
            hbm(cached, parent_blocks),
            [((live, s.CC * B), bf16)] * 2,
            [pltpu.VMEM((s.slots * B * s.CC, B), f32), numbers]
            + [pltpu.SemaphoreType.DMA((1 + s.slots,))],
        )
    with jax.named_scope("join"):
        own, sh, sl = call(
            bind(join),
            vmem(*pieces, sh, sl),
            [(s.block, B), (sh.shape, bf16), (sl.shape, bf16)],
            alias={C: 1, C + 1: 2},
        )
    with jax.named_scope("panels"):
        panels = {0: own}
        for mask in range(2, R, 2):
            panels[mask] = exchange(own, mask, R)
        for mask in range(0, R, 2):
            panels[mask + 1] = exchange(panels[mask], 1, R)
    with jax.named_scope("collect"):
        lh, ll, half = call(
            bind(collect),
            vmem(*[owned[m] for m in range(C)]),
            [((2 * W, live), bf16)] * 2 + [(W, W // 2)],
            [pltpu.VMEM((2 * W, live), f32)],
        )
        theirs = exchange(half, 1, R)
    with jax.named_scope("own_panels"):
        vh, vl, th, tl, base, extra = call(
            bind(own_panels),
            vmem(parent_diagonal, lh, ll, half, theirs),
            [((W, live), bf16)] * 2 + [((W, W), bf16)] * 2 + [(ws, W), (W, W)],
            [pltpu.VMEM((W, W), f32)],
        )
    with jax.named_scope("products"):
        half = C // 2 * s.slots * s.share
        stay, leave, keep, send = call(
            bind(products),
            vmem(sh, sl, lh, ll, vh, vl, th, tl, extra, *[panels[m] for m in range(R)]),
            [(half, 2 * W), (half, 2 * W), (3 * W // 2, W), (3 * W // 2, W)],
            [pltpu.VMEM((s.CC + 1, 2 * W, B), bf16)] * 2
            + [pltpu.VMEM((live, 2 * W), f32), pltpu.VMEM((3 * W, W), f32)],
            flops=2 * live * s.CC * B * 2 * W * 3,
        )
    with jax.named_scope("sum_core"):
        got = exchange(send, 1, R)
    with jax.named_scope("sum_shares"):
        got_rows = flip(leave, 1, C)
    with jax.named_scope("sum_chips"):
        mine = call(bind(add_chips), vmem(keep, got), [(C * 3 * s.eight, W)] * s.chips)
        mine = [mine[0]] + [exchange(mine[m], 2 * m, R) for m in range(1, s.chips)]
    with jax.named_scope("sum_cols"):
        scr = [pltpu.VMEM((C * 3 * s.eight, W), f32)]
        half //= 2
        *cols, stay, leave = call(
            bind(add_cols),
            vmem(*mine, stay, got_rows),
            [(3 * s.eight, W)] * C + [(half, 2 * W)] * 2,
            scr,
        )
        cols = [cols[0]] + [flip(cols[m], m, C) for m in range(1, C)]
        got_rows = flip(leave, 2, C)
        mask = 4
        while mask < C:
            half //= 2
            stay, leave = call(bind(halve), vmem(stay, got_rows), [(half, 2 * W)] * 2)
            got_rows = flip(leave, mask, C)
            mask *= 2
    with jax.named_scope("spread"):
        (done,) = call(bind(add_all), vmem(*cols), [(3 * s.eight, W)])
        parts = {0: done}
        for mask in range(2, R, 2):
            parts[mask] = exchange(done, mask, R)
        for mask in range(0, R, 2):
            parts[mask + 1] = exchange(parts[mask], 1, R)
    with jax.named_scope("rows_out"):
        parent_rows, child_rows = call(
            bind(rows_out),
            smem(parent_blocks, parent_sizes, child_sizes) + vmem(th, tl, stay, got_rows),
            [(s.RC * s.share, W)] * 2,
        )
    with jax.named_scope("finish"):
        parent_diag, child_upper, child_diag = call(
            bind(finish),
            vmem(parent_diagonal, child_diagonal, base, *[parts[m] for m in range(R)]),
            [(ws, W)] * 3,
        )
    shape = (s.RC, 1, s.share, W)
    return (
        parent_rows.reshape(shape),
        parent_diag,
        child_rows.reshape(shape),
        child_upper,
        child_diag,
    )


highest = lax.Precision.HIGHEST


def from_root(value, axis, source):
    kept = jnp.where(lax.axis_index(axis) == source, value, 0).astype(value.dtype)
    return lax.psum(kept, axis)


def live_rows(sizes, block_rows):
    return (jnp.arange(block_rows, dtype=jnp.int32)[None, :] < sizes[:, None]).astype(jnp.float32)


def own_share(widened, blocks, row_live, row_index, row_total, col_index, row_share, local_rows):
    wanted = jnp.arange(local_rows, dtype=jnp.int32) * row_total + row_index
    onehot = (blocks[None, :] == wanted[:, None]).astype(jnp.float32)
    sliced = lax.dynamic_slice_in_dim(widened, col_index * row_share, row_share, 2)
    own_rows = jnp.einsum("rk,wkb->rbw", onehot, sliced, precision=highest)
    live_part = lax.dynamic_slice_in_dim(row_live, col_index * row_share, row_share, 1)
    row_alive = jnp.einsum("rk,kb->rb", onehot, live_part, precision=highest)
    return (own_rows, row_alive)


def add_columns(column_dense, widened, blocks, col_index, col_total):
    wanted = jnp.arange(column_dense.shape[0], dtype=jnp.int32) * col_total + col_index
    onehot = (blocks[None, :] == wanted[:, None]).astype(jnp.float32)
    return column_dense + jnp.einsum("ck,wky->cwy", onehot, widened, precision=highest)


def column_panel(widened, blocks, col_index, col_total, row_total, col_blocks):
    column_dense = jnp.zeros((col_blocks, widened.shape[0], widened.shape[2]), jnp.float32)
    for repeat in range(row_total // col_total):
        sender = col_index + repeat * col_total
        heard_panel, heard_blocks = (
            from_root(widened, "row", sender),
            from_root(blocks, "row", sender),
        )
        column_dense = add_columns(column_dense, heard_panel, heard_blocks, col_index, col_total)
    return column_dense


def child_panels(
    child_panel, child_top, child_live, child_blocks, col_index, col_total, row_total, col_blocks
):
    wide_child, top_full = (
        lax.all_gather(child_panel, "col", axis=0, tiled=True),
        lax.all_gather(child_top, "col", axis=0, tiled=True),
    )
    child_full = wide_child * child_live[None, :, :]
    child_dense = column_panel(
        child_full, child_blocks, col_index, col_total, row_total, col_blocks
    )
    return (child_full, child_dense, top_full)


def apply_inverse(cached, column_dense):
    summed = lax.psum_scatter(
        jnp.einsum(
            "rxcy,cwy->xrw",
            cached,
            column_dense,
            precision=highest,
            preferred_element_type=jnp.float32,
        ),
        "col",
        scatter_dimension=0,
        tiled=True,
    )
    return jnp.transpose(summed, (1, 0, 2))


def diagonal_sum(partial_rows, panel_width, col_share, col_index):
    entire = lax.psum(partial_rows(0, panel_width), ("row", "col"))
    return lax.dynamic_slice_in_dim(entire, col_index * col_share, col_share, 0)


def body(
    cached_inverse,
    parent_panel,
    parent_blocks,
    parent_sizes,
    parent_diagonal,
    child_panel,
    child_top,
    child_blocks,
    child_sizes,
    child_diagonal,
):
    row_total = lax.axis_size("row")
    col_total = lax.axis_size("col")
    row_index = lax.axis_index("row")
    col_index = lax.axis_index("col")
    local_rows = cached_inverse.shape[0]
    block_rows = cached_inverse.shape[2]
    col_blocks = cached_inverse.shape[3]
    cached = cached_inverse.reshape(local_rows, block_rows, col_blocks, block_rows)
    panel_width = parent_diagonal.shape[1]
    row_share = block_rows // col_total
    col_share = panel_width // col_total
    parent_live = live_rows(parent_sizes, block_rows)
    child_live = live_rows(child_sizes, block_rows)
    wide_parent = lax.all_gather(parent_panel, "col", axis=0, tiled=True)
    parent_full = wide_parent * parent_live[None, :, :]
    parent_dense = column_panel(
        parent_full, parent_blocks, col_index, col_total, row_total, col_blocks
    )
    child_full, child_dense, top_full = child_panels(
        child_panel,
        child_top,
        child_live,
        child_blocks,
        col_index,
        col_total,
        row_total,
        col_blocks,
    )
    parent_own, parent_alive = own_share(
        parent_full,
        parent_blocks,
        parent_live,
        row_index,
        row_total,
        col_index,
        row_share,
        local_rows,
    )
    both_local = apply_inverse(cached, jnp.concatenate([parent_dense, child_dense], axis=1))
    parent_local = -both_local[:, :, :panel_width] * parent_alive[:, :, None]
    child_own, child_alive = own_share(
        child_full, child_blocks, child_live, row_index, row_total, col_index, row_share, local_rows
    )
    carried = jnp.einsum("rbw,wv->rbv", parent_local, top_full, precision=highest)
    child_local = -(both_local[:, :, panel_width:] + carried) * child_alive[:, :, None]

    def stacked_terms(offset, amount):
        first_part = jnp.einsum("rbw,rbv->wv", parent_own, parent_local, precision=highest)
        second_part = jnp.einsum("rbw,rbv->wv", parent_local, child_own, precision=highest)
        third_part = jnp.einsum("rbc,rbv->cv", child_own, child_local, precision=highest)
        return jnp.concatenate([first_part, second_part, third_part], axis=1)

    stacked_sum = diagonal_sum(stacked_terms, panel_width, col_share, col_index)
    parent_diag = parent_diagonal - stacked_sum[:, :panel_width]
    child_upper = -(
        jnp.dot(parent_diag, top_full, precision=highest, preferred_element_type=jnp.float32)
        + stacked_sum[:, panel_width : 2 * panel_width]
    )
    upper_whole = lax.all_gather(child_upper, "col", axis=0, tiled=True)
    top_columns = lax.dynamic_slice_in_dim(top_full, col_index * col_share, col_share, 1)
    child_diag = (
        child_diagonal
        - jnp.dot(top_columns.T, upper_whole, precision=highest, preferred_element_type=jnp.float32)
        - stacked_sum[:, 2 * panel_width :]
    )
    return (
        parent_local[:, None, :, :],
        parent_diag,
        child_local[:, None, :, :],
        child_upper,
        child_diag,
    )


def fits(rows, cols, panel, cached, width):
    s = Shape(rows, cols, panel, cached, width)
    return (
        rows & (rows - 1) == 0
        and cols & (cols - 1) == 0
        and rows % cols == 0
        and cols > 2
        and width == 2 * s.B
        and s.payload % cols == 0
        and s.chunk % 16 == 0
        and s.piece % s.chunk == 0
        and s.share % 16 == 0
        and s.ws % rows == 0
        and s.eight % 8 == 0
        and width % s.B == 0
    )


def chosen(*args):
    sizes = lax.axis_size("row"), lax.axis_size("col")
    ok = fits(*sizes, args[1], args[0], args[4].shape[1])
    return (fast_body if ok else body)(*args)


def solution(mesh):
    in_specs = (
        P(None, "row", None, None, "col", None),
        P("col", "row", None),
        P("row"),
        P("row"),
        P("col", None),
        P("col", "row", None),
        P("col", None),
        P("row"),
        P("row"),
        P("col", None),
    )
    out_specs = (
        P(None, "row", "col", None),
        P("col", None),
        P(None, "row", "col", None),
        P("col", None),
        P("col", None),
    )
    return jax.shard_map(chosen, mesh=mesh, in_specs=in_specs, out_specs=out_specs, check_vma=False)
```

```python
import functools

import jax
import jax.numpy as jnp
from jax import lax
from jax.experimental import pallas as pl
from jax.experimental.pallas import tpu as pltpu
from jax.sharding import PartitionSpec as P

f32 = jnp.float32
bf16 = jnp.bfloat16

NN = (((1,), (0,)), ((), ()))
NT = (((1,), (1,)), ((), ()))
TN = (((0,), (0,)), ((), ()))


def split(value):
    high = value.astype(bf16)
    return high, (value - high.astype(f32)).astype(bf16)


def dot3(left, right, dims):
    (lh, ll), (rh, rl) = left, right
    on_left, on_right = dims[0][0][0], dims[0][1][0]
    return lax.dot_general(
        jnp.concatenate([lh, lh, ll], axis=on_left),
        jnp.concatenate([rh, rl, rh], axis=on_right),
        dims,
        preferred_element_type=f32,
    )


def call(kernel, inputs, outs, scratch=(), flops=0, limit=40, passed=()):
    alias = {len(inputs) + i: len(outs) + i for i in range(len(passed))}
    spaces = [pltpu.VMEM] * len(outs) + [pl.ANY] * len(passed)
    inputs = list(inputs) + [(pl.ANY, a) for a in passed]
    outs = list(outs) + [(a.shape, a.dtype) for a in passed]
    arrays = [a for _, a in inputs]
    shapes = [jax.ShapeDtypeStruct(*(o if isinstance(o[0], tuple) else (o, f32))) for o in outs]
    nbytes = sum(a.size * a.dtype.itemsize for a in arrays + shapes)
    return pl.pallas_call(
        kernel,
        out_shape=shapes,
        in_specs=[pl.BlockSpec(memory_space=space) for space, _ in inputs],
        out_specs=[pl.BlockSpec(memory_space=space) for space in spaces],
        scratch_shapes=list(scratch),
        input_output_aliases=alias,
        compiler_params=pltpu.CompilerParams(vmem_limit_bytes=limit and limit * 1024 * 1024),
        cost_estimate=pl.CostEstimate(flops=flops, bytes_accessed=nbytes, transcendentals=0),
    )(*arrays)


def vmem(*arrays):
    return [(pltpu.VMEM, a) for a in arrays]


def smem(*arrays):
    return [(pltpu.SMEM, a) for a in arrays]


def hbm(*arrays):
    return [(pltpu.HBM, a) for a in arrays]


def fetch(sources, targets, sems):
    copies = [
        pltpu.make_async_copy(a, b, sems.at[i]) for i, (a, b) in enumerate(zip(sources, targets))
    ]
    for copy in copies:
        copy.start()
    return copies


def exchange(value, mask, row_total):
    return lax.ppermute(value, "row", [(i, i ^ mask) for i in range(row_total)])


def flip(value, mask, col_total):
    return lax.ppermute(value, "col", [(i, i ^ mask) for i in range(col_total)])


class Shape:
    def __init__(self, rows, cols, panel, cached, width):
        self.R, self.C = rows, cols
        self.ws, self.slots, self.B = panel.shape
        self.W = width
        self.RC = cached.shape[0]
        self.CC = cached.shape[3]
        self.Q = rows // cols
        self.payload = self.slots * 2 * self.ws
        self.piece = self.payload // cols
        self.chunk = self.ws // 2
        self.share = self.B // cols
        self.chips = rows // 2
        self.eight = self.ws // rows
        self.live = self.slots * self.B
        self.parts = self.W // self.B
        self.block = self.payload + 8


def pack(s, *refs):
    sources, refs = refs[:6], refs[6:]
    sends, payload, refs = refs[: s.C], refs[s.C], refs[s.C + 1 :]
    targets, sems = refs[:6], refs[6]
    for copy in fetch(sources, targets, sems):
        copy.wait()
    blocks, psize, csize, parent, child, top = targets
    col = lax.axis_index("col")
    lane = lax.broadcasted_iota(jnp.int32, (s.ws, s.B), 1)
    for slot in range(s.slots):
        base = slot * 2 * s.ws
        for which, panel, sizes in ((0, parent, psize), (1, child, csize)):
            live = jnp.where(lane < sizes[slot], panel[slot], 0.0)
            payload[base + which * s.ws : base + (which + 1) * s.ws, :] = live
    wide = s.W // 2
    mine = lax.rem(lax.axis_index("row"), 2) * wide
    payload[s.payload :, :] = top[:, pl.ds(pl.multiple_of(mine, wide), wide)]
    row8 = lax.broadcasted_iota(jnp.int32, (8, s.B), 0)
    ids = jnp.zeros((8, s.B), f32)
    for slot in range(s.slots):
        ids = jnp.where(row8 == slot, blocks[slot].astype(f32), ids)
    for turn in range(s.C):
        start = pl.multiple_of(lax.rem(turn - col + s.C, s.C) * s.piece, s.piece)
        sends[turn][: s.piece, :] = payload[pl.ds(start, s.piece), :]
        sends[turn][s.piece :, :] = ids


def split_live(s, cached, blocks, high, low, held, numbers, sems):
    copy = pltpu.make_async_copy(blocks, numbers, sems.at[0])
    copy.start()
    copy.wait()
    size = s.B * s.CC
    copies = []
    for slot in range(s.slots):
        p = lax.div(jnp.maximum(numbers[slot], 0), s.R)
        source = cached.at[pl.ds(pl.multiple_of(p * size, size), size), :]
        copy = pltpu.make_async_copy(source, held.at[pl.ds(slot * size, size), :], sems.at[1 + slot])
        copy.start()
        copies.append(copy)
    for slot in range(s.slots):
        copies[slot].wait()
        rows = slice(slot * s.B, (slot + 1) * s.B)
        for m in range(s.CC):
            h, l = split(held[pl.ds(slot * size + m, s.B, stride=s.CC), :])
            high[rows, m * s.B : (m + 1) * s.B] = h
            low[rows, m * s.B : (m + 1) * s.B] = l


def join(s, *refs):
    pieces, out = refs[: s.C], refs[s.C + 2]
    part = lax.rem(lax.axis_index("row"), s.C)
    for turn in range(s.C):
        start = pl.multiple_of(lax.rem(turn - part + s.C, s.C) * s.piece, s.piece)
        out[pl.ds(start, s.piece), :] = pieces[turn][: s.piece, :]
    out[s.payload :, :] = pieces[0][s.piece :, :]


def collect(s, *refs):
    owned, (lh, ll, half, panel) = refs[: s.C], refs[s.C :]
    col = lax.axis_index("col")
    for mask in range(s.C):
        source = jnp.bitwise_xor(col, mask)
        for slot in range(s.slots):
            for which in range(2):
                start = (slot * 2 + which) * s.ws
                dest = pl.multiple_of(which * s.W + source * s.ws, s.ws)
                panel[pl.ds(dest, s.ws), slot * s.B : (slot + 1) * s.B] = owned[mask][
                    start : start + s.ws, :
                ]
        dest = pl.multiple_of(source * s.ws, s.ws)
        half[pl.ds(dest, s.ws), :] = owned[mask][s.payload :, :]
    lh[...], ll[...] = split(panel[...])


def own_panels(s, pd, lh, ll, mine, theirs, vh, vl, th, tl, base, extra, top):
    row, col = lax.axis_index("row"), lax.axis_index("col")
    wide = s.W // 2
    core = lax.rem(row, 2)
    top[:, pl.ds(pl.multiple_of(core * wide, wide), wide)] = mine[...]
    top[:, pl.ds(pl.multiple_of((1 - core) * wide, wide), wide)] = theirs[...]
    th[...], tl[...] = split(top[...])
    full = (th[...], tl[...])
    vh[...], vl[...] = split(dot3(split(top[...].T), (lh[: s.W, :], ll[: s.W, :]), NN))
    lead = dot3(split(pd[...]), full, NN)
    base[...] = -lead
    own = top[pl.ds(pl.multiple_of(col * s.ws, s.ws), s.ws), :]
    extra[...] = dot3(split(own), split(lead * (1.0 / s.R)), TN)


def products(s, sh, sl, lh, ll, vh, vl, th, tl, extra, *refs):
    panels, (stay, leave, keep, send, xh, xl, total, both) = refs[: s.R], refs[s.R :]
    row = lax.axis_index("row")
    core = lax.rem(row, 2)
    places = []
    for owner in range(s.Q):
        for slot in range(s.slots):
            at = s.payload + slot
            number = jnp.max(panels[owner * s.C][at : at + 1, :]).astype(jnp.int32)
            places.append(jnp.where(number < 0, s.CC, lax.div(jnp.maximum(number, 0), s.C)))
    for m in range(s.CC):
        taken = places[0] == m
        for place in places[1:]:
            taken = jnp.logical_or(taken, place == m)

        @pl.when(jnp.logical_not(taken))
        def _():
            xh[m] = jnp.zeros((2 * s.W, s.B), bf16)
            xl[m] = jnp.zeros((2 * s.W, s.B), bf16)

    per = s.piece // s.chunk
    for mask in range(s.R):
        owner = mask // s.C
        part = lax.rem(jnp.bitwise_xor(row, mask), s.C)
        for i in range(per):
            at = part * per + i
            group, off = lax.div(at, 2), lax.rem(at, 2) * s.chunk
            slot, which = lax.div(group, 2), lax.rem(group, 2)
            place = places[owner * s.slots]
            for k in range(1, s.slots):
                place = jnp.where(slot == k, places[owner * s.slots + k], place)
            for source in range(s.C):
                start = source * s.piece + i * s.chunk
                high, low = split(panels[mask][start : start + s.chunk, :])
                dest = pl.multiple_of(which * s.W + source * s.ws + off, s.chunk)
                xh[place, pl.ds(dest, s.chunk), :] = high
                xl[place, pl.ds(dest, s.chunk), :] = low
    right = tuple(jnp.concatenate([x[i] for i in range(s.CC)], axis=1) for x in (xh, xl))
    total[...] = dot3((sh[...], sl[...]), right, NT)
    col = lax.axis_index("col")
    for mask in range(s.C):
        out = leave if mask % 2 else stay
        target = jnp.bitwise_xor(col, mask)
        for slot in range(s.slots):
            start = pl.multiple_of(slot * s.B + target * s.share, s.share)
            to = (mask // 2 * s.slots + slot) * s.share
            out[to : to + s.share, :] = total[pl.ds(start, s.share), :]
    W = s.W
    left = tuple(jnp.concatenate([x[...], y[...]], axis=0) for x, y in ((lh, vh), (ll, vl)))
    first = dot3(left, split(total[:, :W]), NN)
    d = dot3((lh[W:, :], ll[W:, :]), split(total[:, W:]), NN)
    second = dot3(split(first), (th[...], tl[...]), NN)
    both[0:W, :] = first[:W]
    both[W : 2 * W, :] = first[W : 2 * W].T - second[:W]
    cross = second[W : 2 * W]
    both[2 * W :, :] = d - cross - cross.T + second[2 * W :] + extra[...]
    n = s.eight
    for out, swap in ((keep, 0), (send, 1)):
        offset = jnp.bitwise_xor(core, swap) * (s.ws // 2)
        for chip in range(s.chips):
            for source in range(s.C):
                for kind in range(3):
                    at = pl.multiple_of(kind * W + source * s.ws + chip * n + offset, n)
                    to = ((chip * s.C + source) * 3 + kind) * n
                    out[to : to + n, :] = both[pl.ds(at, n), :]


def add_chips(s, kept, got, *outs):
    size = s.C * 3 * s.eight
    chip = lax.div(lax.axis_index("row"), 2)
    for mask in range(s.chips):
        rows = pl.ds(pl.multiple_of(jnp.bitwise_xor(chip, mask) * size, size), size)
        outs[mask][...] = kept[rows, :] + got[rows, :]


def add_cols(s, *refs):
    terms, outs, total = refs[: s.chips], refs[s.chips : -1], refs[-1]
    size = 3 * s.eight
    col = lax.axis_index("col")
    value = terms[0][...]
    for term in terms[1:]:
        value = value + term[...]
    total[...] = value
    for mask in range(s.C):
        rows = pl.ds(pl.multiple_of(jnp.bitwise_xor(col, mask) * size, size), size)
        outs[mask][...] = total[rows, :]


def halve(s, kept, got, stay, leave):
    size = s.slots * s.share
    for i in range(kept.shape[0] // size):
        out, at = (leave if i % 2 else stay), i // 2 * size
        rows = slice(i * size, (i + 1) * size)
        out[at : at + size, :] = kept[rows, :] + got[rows, :]


def add_all(s, *refs):
    terms, (kept, got, out, stay, leave) = refs[: s.C], refs[s.C :]
    value = terms[0][...]
    for term in terms[1:]:
        value = value + term[...]
    out[...] = value
    halve(s, kept, got, stay, leave)


def finish(s, pd, cd, base, *refs):
    parts, outs = refs[: s.R], refs[s.R + 2 : s.R + 5]
    row = lax.axis_index("row")
    n = s.eight
    starts = (pd, base, cd)
    for mask in range(s.R):
        source = jnp.bitwise_xor(row, mask)
        at = lax.rem(source, 2) * (s.ws // 2) + lax.div(source, 2) * n
        rows = pl.ds(pl.multiple_of(at, n), n)
        for kind in range(3):
            outs[kind][rows, :] = starts[kind][rows, :] + parts[mask][kind * n : (kind + 1) * n, :]


def rows_out(s, blocks, psize, csize, th, tl, kept, got, parent, child):
    value = kept[...] + got[...]
    first = lax.axis_index("col") * s.share
    index = lax.broadcasted_iota(jnp.int32, (s.share, s.W), 0) + first
    plive = jnp.concatenate([index < psize[k] for k in range(s.slots)], axis=0)
    clive = jnp.concatenate([index < csize[k] for k in range(s.slots)], axis=0)
    y = jnp.where(plive, -value[:, : s.W], 0.0)
    carried = dot3(split(y), (th[...], tl[...]), NN)
    z = jnp.where(clive, -(value[:, s.W :] + carried), 0.0)
    parent[...] = jnp.zeros_like(parent)
    child[...] = jnp.zeros_like(child)
    for slot in range(s.slots):

        @pl.when(blocks[slot] >= 0)
        def _():
            at = lax.div(blocks[slot], s.R) * s.share
            rows = pl.ds(pl.multiple_of(at, s.share), s.share)
            parent[rows, :] = y[slot * s.share : (slot + 1) * s.share, :]
            child[rows, :] = z[slot * s.share : (slot + 1) * s.share, :]


def scatter_perm(s, turn):
    return [
        ((q * s.C + a) * s.C + c, (q * s.C + (turn - c) % s.C) * s.C + a)
        for q in range(s.Q)
        for a in range(s.C)
        for c in range(s.C)
    ]


def fast_body(
    cached_inverse,
    parent_panel,
    parent_blocks,
    parent_sizes,
    parent_diagonal,
    child_panel,
    child_top,
    child_blocks,
    child_sizes,
    child_diagonal,
):
    R, C = lax.axis_size("row"), lax.axis_size("col")
    B = cached_inverse.shape[2]
    s = Shape(R, C, parent_panel, cached_inverse, parent_diagonal.shape[1])
    W, ws, live = s.W, s.ws, s.live
    cached = cached_inverse.reshape(-1, B)
    bind = lambda kernel: functools.partial(kernel, s)
    numbers = pltpu.SMEM((s.slots,), jnp.int32)
    by_slot = (s.slots, ws, B)
    with jax.named_scope("pack"):
        *sends, payload = call(
            bind(pack),
            hbm(
                parent_blocks,
                parent_sizes,
                child_sizes,
                jnp.transpose(parent_panel, (1, 0, 2)),
                jnp.transpose(child_panel, (1, 0, 2)),
                child_top,
            ),
            [(s.piece + 8, B)] * C + [(s.payload + ws, B)],
            [numbers] * 3
            + [pltpu.VMEM(by_slot, f32)] * 2
            + [pltpu.VMEM((ws, W), f32), pltpu.SemaphoreType.DMA((6,))],
            limit=None,
        )
    with jax.named_scope("scatter"):
        pieces = [lax.ppermute(sends[t], ("row", "col"), scatter_perm(s, t)) for t in range(C)]
    with jax.named_scope("owned"):
        owned = {0: payload}
        mask = C // 2
        while mask:
            owned.update({m ^ mask: flip(owned[m], mask, C) for m in list(owned)})
            mask //= 2
    with jax.named_scope("split_live"):
        sh, sl = call(
            bind(split_live),
            hbm(cached, parent_blocks),
            [((live, s.CC * B), bf16)] * 2,
            [pltpu.VMEM((s.slots * B * s.CC, B), f32), numbers]
            + [pltpu.SemaphoreType.DMA((1 + s.slots,))],
        )
    with jax.named_scope("join"):
        own, sh, sl = call(
            bind(join),
            vmem(*pieces),
            [(s.block, B)],
            passed=(sh, sl),
        )
    with jax.named_scope("panels"):
        panels = {0: own}
        for mask in range(2, R, 2):
            panels[mask] = exchange(own, mask, R)
        for mask in range(0, R, 2):
            panels[mask + 1] = exchange(panels[mask], 1, R)
    with jax.named_scope("collect"):
        lh, ll, half = call(
            bind(collect),
            vmem(*[owned[m] for m in range(C)]),
            [((2 * W, live), bf16)] * 2 + [(W, W // 2)],
            [pltpu.VMEM((2 * W, live), f32)],
        )
        theirs = exchange(half, 1, R)
    with jax.named_scope("own_panels"):
        vh, vl, th, tl, base, extra = call(
            bind(own_panels),
            vmem(parent_diagonal, lh, ll, half, theirs),
            [((W, live), bf16)] * 2 + [((W, W), bf16)] * 2 + [(ws, W), (W, W)],
            [pltpu.VMEM((W, W), f32)],
        )
    with jax.named_scope("products"):
        half = C // 2 * s.slots * s.share
        stay, leave, keep, send = call(
            bind(products),
            vmem(sh, sl, lh, ll, vh, vl, th, tl, extra, *[panels[m] for m in range(R)]),
            [(half, 2 * W), (half, 2 * W), (3 * W // 2, W), (3 * W // 2, W)],
            [pltpu.VMEM((s.CC + 1, 2 * W, B), bf16)] * 2
            + [pltpu.VMEM((live, 2 * W), f32), pltpu.VMEM((3 * W, W), f32)],
            flops=2 * live * s.CC * B * 2 * W * 3,
        )
    with jax.named_scope("sum_core"):
        got = exchange(send, 1, R)
    with jax.named_scope("sum_shares"):
        got_rows = flip(leave, 1, C)
    with jax.named_scope("sum_chips"):
        mine = call(bind(add_chips), vmem(keep, got), [(C * 3 * s.eight, W)] * s.chips)
        mine = [mine[0]] + [exchange(mine[m], 2 * m, R) for m in range(1, s.chips)]
    with jax.named_scope("sum_cols"):
        scr = [pltpu.VMEM((C * 3 * s.eight, W), f32)]
        cols = call(bind(add_cols), vmem(*mine), [(3 * s.eight, W)] * C, scr)
        cols = [cols[0]] + [flip(cols[m], m, C) for m in range(1, C)]
    with jax.named_scope("spread"):
        half //= 2
        done, stay, leave = call(
            bind(add_all),
            vmem(*cols, stay, got_rows),
            [(3 * s.eight, W)] + [(half, 2 * W)] * 2,
        )
        got_rows = flip(leave, 2, C)
        mask = 4
        while mask < C:
            half //= 2
            stay, leave = call(bind(halve), vmem(stay, got_rows), [(half, 2 * W)] * 2)
            got_rows = flip(leave, mask, C)
            mask *= 2
        parts = {0: done}
        for mask in range(2, R, 2):
            parts[mask] = exchange(done, mask, R)
        for mask in range(0, R, 2):
            parts[mask + 1] = exchange(parts[mask], 1, R)
    with jax.named_scope("rows_out"):
        parent_rows, child_rows = call(
            bind(rows_out),
            smem(parent_blocks, parent_sizes, child_sizes) + vmem(th, tl, stay, got_rows),
            [(s.RC * s.share, W)] * 2,
        )
    with jax.named_scope("finish"):
        parent_diag, child_upper, child_diag, parent_rows, child_rows = call(
            bind(finish),
            vmem(parent_diagonal, child_diagonal, base, *[parts[m] for m in range(R)]),
            [(ws, W)] * 3,
            passed=(parent_rows, child_rows),
        )
    shape = (s.RC, 1, s.share, W)
    return (
        parent_rows.reshape(shape),
        parent_diag,
        child_rows.reshape(shape),
        child_upper,
        child_diag,
    )


highest = lax.Precision.HIGHEST


def from_root(value, axis, source):
    kept = jnp.where(lax.axis_index(axis) == source, value, 0).astype(value.dtype)
    return lax.psum(kept, axis)


def live_rows(sizes, block_rows):
    return (jnp.arange(block_rows, dtype=jnp.int32)[None, :] < sizes[:, None]).astype(jnp.float32)


def own_share(widened, blocks, row_live, row_index, row_total, col_index, row_share, local_rows):
    wanted = jnp.arange(local_rows, dtype=jnp.int32) * row_total + row_index
    onehot = (blocks[None, :] == wanted[:, None]).astype(jnp.float32)
    sliced = lax.dynamic_slice_in_dim(widened, col_index * row_share, row_share, 2)
    own_rows = jnp.einsum("rk,wkb->rbw", onehot, sliced, precision=highest)
    live_part = lax.dynamic_slice_in_dim(row_live, col_index * row_share, row_share, 1)
    row_alive = jnp.einsum("rk,kb->rb", onehot, live_part, precision=highest)
    return (own_rows, row_alive)


def add_columns(column_dense, widened, blocks, col_index, col_total):
    wanted = jnp.arange(column_dense.shape[0], dtype=jnp.int32) * col_total + col_index
    onehot = (blocks[None, :] == wanted[:, None]).astype(jnp.float32)
    return column_dense + jnp.einsum("ck,wky->cwy", onehot, widened, precision=highest)


def column_panel(widened, blocks, col_index, col_total, row_total, col_blocks):
    column_dense = jnp.zeros((col_blocks, widened.shape[0], widened.shape[2]), jnp.float32)
    for repeat in range(row_total // col_total):
        sender = col_index + repeat * col_total
        heard_panel, heard_blocks = (
            from_root(widened, "row", sender),
            from_root(blocks, "row", sender),
        )
        column_dense = add_columns(column_dense, heard_panel, heard_blocks, col_index, col_total)
    return column_dense


def child_panels(
    child_panel, child_top, child_live, child_blocks, col_index, col_total, row_total, col_blocks
):
    wide_child, top_full = (
        lax.all_gather(child_panel, "col", axis=0, tiled=True),
        lax.all_gather(child_top, "col", axis=0, tiled=True),
    )
    child_full = wide_child * child_live[None, :, :]
    child_dense = column_panel(
        child_full, child_blocks, col_index, col_total, row_total, col_blocks
    )
    return (child_full, child_dense, top_full)


def apply_inverse(cached, column_dense):
    summed = lax.psum_scatter(
        jnp.einsum(
            "rxcy,cwy->xrw",
            cached,
            column_dense,
            precision=highest,
            preferred_element_type=jnp.float32,
        ),
        "col",
        scatter_dimension=0,
        tiled=True,
    )
    return jnp.transpose(summed, (1, 0, 2))


def diagonal_sum(partial_rows, panel_width, col_share, col_index):
    entire = lax.psum(partial_rows(0, panel_width), ("row", "col"))
    return lax.dynamic_slice_in_dim(entire, col_index * col_share, col_share, 0)


def body(
    cached_inverse,
    parent_panel,
    parent_blocks,
    parent_sizes,
    parent_diagonal,
    child_panel,
    child_top,
    child_blocks,
    child_sizes,
    child_diagonal,
):
    row_total = lax.axis_size("row")
    col_total = lax.axis_size("col")
    row_index = lax.axis_index("row")
    col_index = lax.axis_index("col")
    local_rows = cached_inverse.shape[0]
    block_rows = cached_inverse.shape[2]
    col_blocks = cached_inverse.shape[3]
    cached = cached_inverse.reshape(local_rows, block_rows, col_blocks, block_rows)
    panel_width = parent_diagonal.shape[1]
    row_share = block_rows // col_total
    col_share = panel_width // col_total
    parent_live = live_rows(parent_sizes, block_rows)
    child_live = live_rows(child_sizes, block_rows)
    wide_parent = lax.all_gather(parent_panel, "col", axis=0, tiled=True)
    parent_full = wide_parent * parent_live[None, :, :]
    parent_dense = column_panel(
        parent_full, parent_blocks, col_index, col_total, row_total, col_blocks
    )
    child_full, child_dense, top_full = child_panels(
        child_panel,
        child_top,
        child_live,
        child_blocks,
        col_index,
        col_total,
        row_total,
        col_blocks,
    )
    parent_own, parent_alive = own_share(
        parent_full,
        parent_blocks,
        parent_live,
        row_index,
        row_total,
        col_index,
        row_share,
        local_rows,
    )
    both_local = apply_inverse(cached, jnp.concatenate([parent_dense, child_dense], axis=1))
    parent_local = -both_local[:, :, :panel_width] * parent_alive[:, :, None]
    child_own, child_alive = own_share(
        child_full, child_blocks, child_live, row_index, row_total, col_index, row_share, local_rows
    )
    carried = jnp.einsum("rbw,wv->rbv", parent_local, top_full, precision=highest)
    child_local = -(both_local[:, :, panel_width:] + carried) * child_alive[:, :, None]

    def stacked_terms(offset, amount):
        first_part = jnp.einsum("rbw,rbv->wv", parent_own, parent_local, precision=highest)
        second_part = jnp.einsum("rbw,rbv->wv", parent_local, child_own, precision=highest)
        third_part = jnp.einsum("rbc,rbv->cv", child_own, child_local, precision=highest)
        return jnp.concatenate([first_part, second_part, third_part], axis=1)

    stacked_sum = diagonal_sum(stacked_terms, panel_width, col_share, col_index)
    parent_diag = parent_diagonal - stacked_sum[:, :panel_width]
    child_upper = -(
        jnp.dot(parent_diag, top_full, precision=highest, preferred_element_type=jnp.float32)
        + stacked_sum[:, panel_width : 2 * panel_width]
    )
    upper_whole = lax.all_gather(child_upper, "col", axis=0, tiled=True)
    top_columns = lax.dynamic_slice_in_dim(top_full, col_index * col_share, col_share, 1)
    child_diag = (
        child_diagonal
        - jnp.dot(top_columns.T, upper_whole, precision=highest, preferred_element_type=jnp.float32)
        - stacked_sum[:, 2 * panel_width :]
    )
    return (
        parent_local[:, None, :, :],
        parent_diag,
        child_local[:, None, :, :],
        child_upper,
        child_diag,
    )


def fits(rows, cols, panel, cached, width):
    s = Shape(rows, cols, panel, cached, width)
    return (
        rows & (rows - 1) == 0
        and cols & (cols - 1) == 0
        and rows % cols == 0
        and cols > 2
        and width == 2 * s.B
        and s.payload % cols == 0
        and s.chunk % 16 == 0
        and s.piece % s.chunk == 0
        and s.share % 16 == 0
        and s.ws % rows == 0
        and s.eight % 8 == 0
        and width % s.B == 0
    )


def chosen(*args):
    sizes = lax.axis_size("row"), lax.axis_size("col")
    ok = fits(*sizes, args[1], args[0], args[4].shape[1])
    return (fast_body if ok else body)(*args)


def solution(mesh):
    in_specs = (
        P(None, "row", None, None, "col", None),
        P("col", "row", None),
        P("row"),
        P("row"),
        P("col", None),
        P("col", "row", None),
        P("col", None),
        P("row"),
        P("row"),
        P("col", None),
    )
    out_specs = (
        P(None, "row", "col", None),
        P("col", None),
        P(None, "row", "col", None),
        P("col", None),
        P("col", None),
    )
    return jax.shard_map(chosen, mesh=mesh, in_specs=in_specs, out_specs=out_specs, check_vma=False)
```

```python
import functools

import jax
import jax.numpy as jnp
from jax import lax
from jax.experimental import pallas as pl
from jax.experimental.pallas import tpu as pltpu
from jax.sharding import PartitionSpec as P

f32 = jnp.float32
bf16 = jnp.bfloat16

NN = (((1,), (0,)), ((), ()))
NT = (((1,), (1,)), ((), ()))
TN = (((0,), (0,)), ((), ()))


def split(value):
    high = value.astype(bf16)
    return high, (value - high.astype(f32)).astype(bf16)


def dot3(left, right, dims):
    (lh, ll), (rh, rl) = left, right
    on_left, on_right = dims[0][0][0], dims[0][1][0]
    return lax.dot_general(
        jnp.concatenate([lh, lh, ll], axis=on_left),
        jnp.concatenate([rh, rl, rh], axis=on_right),
        dims,
        preferred_element_type=f32,
    )


def call(kernel, inputs, outs, scratch=(), ahead=0, limit=40, passed=()):
    alias = {len(inputs) + i: len(outs) + i for i in range(len(passed))}
    spaces = [pltpu.VMEM] * len(outs) + [pl.ANY] * len(passed)
    inputs = list(inputs) + [(pl.ANY, a) for a in passed]
    outs = list(outs) + [(a.shape, a.dtype) for a in passed]
    arrays = [a for _, a in inputs]
    shapes = [jax.ShapeDtypeStruct(*(o if isinstance(o[0], tuple) else (o, f32))) for o in outs]
    nbytes = sum(a.size * a.dtype.itemsize for a in arrays + shapes)
    return pl.pallas_call(
        kernel,
        out_shape=shapes,
        in_specs=[pl.BlockSpec(memory_space=space) for space, _ in inputs],
        out_specs=[pl.BlockSpec(memory_space=space) for space in spaces],
        scratch_shapes=list(scratch),
        input_output_aliases=alias,
        compiler_params=pltpu.CompilerParams(vmem_limit_bytes=limit and limit * 1024 * 1024),
        cost_estimate=pl.CostEstimate(flops=int(ahead), bytes_accessed=nbytes, transcendentals=0),
    )(*arrays)


def vmem(*arrays):
    return [(pltpu.VMEM, a) for a in arrays]


def smem(*arrays):
    return [(pltpu.SMEM, a) for a in arrays]


def hbm(*arrays):
    return [(pltpu.HBM, a) for a in arrays]


def fetch(sources, targets, sems):
    copies = [
        pltpu.make_async_copy(a, b, sems.at[i]) for i, (a, b) in enumerate(zip(sources, targets))
    ]
    for copy in copies:
        copy.start()
    return copies


def exchange(value, mask, row_total):
    return lax.ppermute(value, "row", [(i, i ^ mask) for i in range(row_total)])


def flip(value, mask, col_total):
    return lax.ppermute(value, "col", [(i, i ^ mask) for i in range(col_total)])


class Shape:
    def __init__(self, rows, cols, panel, cached, width):
        self.R, self.C = rows, cols
        self.ws, self.slots, self.B = panel.shape
        self.W = width
        self.RC = cached.shape[0]
        self.CC = cached.shape[3]
        self.Q = rows // cols
        self.payload = self.slots * 2 * self.ws
        self.share = self.B // cols
        self.chips = rows // 2
        self.eight = self.ws // rows
        self.live = self.slots * self.B
        self.parts = self.W // self.B
        self.block = self.payload + self.ws + 8


def pack(s, *refs):
    sources, (sent, mine, *targets, sems) = refs[:6], refs[6:]
    for copy in fetch(sources, targets, sems):
        copy.wait()
    blocks, psize, csize, parent, child, top = targets
    lane = lax.broadcasted_iota(jnp.int32, (s.ws, s.B), 1)
    for slot in range(s.slots):
        base = slot * 2 * s.ws
        for which, panel, sizes in ((0, parent, psize), (1, child, csize)):
            live = jnp.where(lane < sizes[slot], panel[slot], 0.0)
            rows = slice(base + which * s.ws, base + (which + 1) * s.ws)
            mine[rows, :] = live
            sent[rows, :] = live
    half = lax.div(lax.axis_index("row"), s.C) * s.B
    sent[s.payload : s.payload + s.ws, :] = top[:, pl.ds(pl.multiple_of(half, s.B), s.B)]
    row8 = lax.broadcasted_iota(jnp.int32, (8, s.B), 0)
    ids = jnp.zeros((8, s.B), f32)
    for slot in range(s.slots):
        ids = jnp.where(row8 == slot, blocks[slot].astype(f32), ids)
    sent[s.payload + s.ws :, :] = ids


def order(s, *refs):
    pass


def split_live(s, cached, blocks, high, low, held, numbers, sems):
    copy = pltpu.make_async_copy(blocks, numbers, sems.at[0])
    copy.start()
    copy.wait()
    size = s.B * s.CC
    copies = []
    for slot in range(s.slots):
        p = lax.div(jnp.maximum(numbers[slot], 0), s.R)
        source = cached.at[pl.ds(pl.multiple_of(p * size, size), size), :]
        copy = pltpu.make_async_copy(source, held.at[pl.ds(slot * size, size), :], sems.at[1 + slot])
        copy.start()
        copies.append(copy)
    for slot in range(s.slots):
        copies[slot].wait()
        rows = slice(slot * s.B, (slot + 1) * s.B)
        for m in range(s.CC):
            h, l = split(held[pl.ds(slot * size + m, s.B, stride=s.CC), :])
            high[rows, m * s.B : (m + 1) * s.B] = h
            low[rows, m * s.B : (m + 1) * s.B] = l


def shares_of(s, pd, sh, sl, *refs):
    panels, refs = refs[: s.R], refs[s.R :]
    shares, refs = refs[: s.C], refs[s.C :]
    gh, gl, th, tl, ih, il, base, extra, xh, xl, total, top = refs
    row, col = lax.axis_index("row"), lax.axis_index("col")
    places = []
    for owner in range(s.Q):
        for slot in range(s.slots):
            at = s.payload + s.ws + slot
            number = jnp.max(panels[owner * s.C][at : at + 1, :]).astype(jnp.int32)
            places.append(jnp.where(number < 0, s.CC, lax.div(jnp.maximum(number, 0), s.C)))
    for m in range(s.CC):
        taken = places[0] == m
        for place in places[1:]:
            taken = jnp.logical_or(taken, place == m)

        @pl.when(jnp.logical_not(taken))
        def _():
            xh[m] = jnp.zeros((2 * s.W, s.B), bf16)
            xl[m] = jnp.zeros((2 * s.W, s.B), bf16)

    for mask in range(s.R):
        sender = jnp.bitwise_xor(row, mask)
        first = pl.multiple_of(lax.rem(sender, s.C) * s.ws, s.ws)
        for slot in range(s.slots):
            place = places[mask // s.C * s.slots + slot]
            for which in range(2):
                start = (slot * 2 + which) * s.ws
                high, low = split(panels[mask][start : start + s.ws, :])
                rows = pl.ds(pl.multiple_of(which * s.W + first, s.ws), s.ws)
                xh[place, rows, :] = high
                xl[place, rows, :] = low
        half = pl.multiple_of(lax.div(sender, s.C) * s.B, s.B)
        top[pl.ds(first, s.ws), pl.ds(half, s.B)] = panels[mask][s.payload : s.payload + s.ws, :]
    right = tuple(jnp.concatenate([x[i] for i in range(s.CC)], axis=1) for x in (xh, xl))
    total[...] = dot3((sh[...], sl[...]), right, NT)
    gh[...], gl[...] = split(total[...])
    for mask in range(s.C):
        target = jnp.bitwise_xor(col, mask)
        for slot in range(s.slots):
            start = pl.multiple_of(slot * s.B + target * s.share, s.share)
            rows = slice(slot * s.share, (slot + 1) * s.share)
            shares[mask][rows, :] = total[pl.ds(start, s.share), :]
    th[...], tl[...] = split(top[...])
    ih[...], il[...] = split(top[...].T)
    lead = dot3(split(pd[...]), (th[...], tl[...]), NN)
    base[...] = -lead
    own = top[pl.ds(pl.multiple_of(col * s.ws, s.ws), s.ws), :]
    extra[...] = dot3(split(own), split(lead * (1.0 / s.R)), TN)


def collect(s, *refs):
    owned, (lh, ll) = refs[: s.C], refs[s.C + 2 : s.C + 4]
    col = lax.axis_index("col")
    for mask in range(s.C):
        source = jnp.bitwise_xor(col, mask)
        for slot in range(s.slots):
            for which in range(2):
                start = (slot * 2 + which) * s.ws
                rows = pl.ds(pl.multiple_of(which * s.W + source * s.ws, s.ws), s.ws)
                lanes = slice(slot * s.B, (slot + 1) * s.B)
                lh[rows, lanes], ll[rows, lanes] = split(owned[mask][start : start + s.ws, :])


def products(s, gh, gl, th, tl, ih, il, extra, lh, ll, keep, send, both):
    core = lax.rem(lax.axis_index("row"), 2)
    W = s.W
    first = dot3((lh[...], ll[...]), (gh[:, :W], gl[:, :W]), NN)
    d = dot3((lh[W:, :], ll[W:, :]), (gh[:, W:], gl[:, W:]), NN)
    second = dot3(split(first), (th[...], tl[...]), NN)
    third = dot3((ih[...], il[...]), split(second[:W]), NN)
    both[0:W, :] = first[:W]
    both[W : 2 * W, :] = first[W:].T - second[:W]
    cross = second[W:]
    both[2 * W :, :] = d - cross - cross.T + third + extra[...]
    n = s.eight
    for out, swap in ((keep, 0), (send, 1)):
        offset = jnp.bitwise_xor(core, swap) * (s.ws // 2)
        for chip in range(s.chips):
            for source in range(s.C):
                for kind in range(3):
                    at = pl.multiple_of(kind * W + source * s.ws + chip * n + offset, n)
                    to = ((chip * s.C + source) * 3 + kind) * n
                    out[to : to + n, :] = both[pl.ds(at, n), :]


def add_chips(s, kept, got, share, *outs):
    outs = outs[: s.chips]
    size = s.C * 3 * s.eight
    chip = lax.div(lax.axis_index("row"), 2)
    for mask in range(s.chips):
        rows = pl.ds(pl.multiple_of(jnp.bitwise_xor(chip, mask) * size, size), size)
        outs[mask][...] = kept[rows, :] + got[rows, :]


def add_cols(s, *refs):
    terms, outs, total = refs[: s.chips], refs[s.chips : -1], refs[-1]
    size = 3 * s.eight
    col = lax.axis_index("col")
    value = terms[0][...]
    for term in terms[1:]:
        value = value + term[...]
    total[...] = value
    for mask in range(s.C):
        rows = pl.ds(pl.multiple_of(jnp.bitwise_xor(col, mask) * size, size), size)
        outs[mask][...] = total[rows, :]


def plus(s, *refs):
    count = len(refs) // 3
    for one, two, out in zip(refs[:count], refs[count : 2 * count], refs[2 * count :]):
        out[...] = one[...] + two[...]


def add_all(s, *refs):
    terms, out = refs[: s.C], refs[s.C + 2]
    value = terms[0][...]
    for term in terms[1:]:
        value = value + term[...]
    out[...] = value


def finish(s, pd, cd, base, *refs):
    parts, outs = refs[: s.R], refs[s.R :]
    row = lax.axis_index("row")
    n = s.eight
    starts = (pd, base, cd)
    for mask in range(s.R):
        source = jnp.bitwise_xor(row, mask)
        at = lax.rem(source, 2) * (s.ws // 2) + lax.div(source, 2) * n
        rows = pl.ds(pl.multiple_of(at, n), n)
        for kind in range(3):
            outs[kind][rows, :] = starts[kind][rows, :] + parts[mask][kind * n : (kind + 1) * n, :]


def rows_out(s, blocks, psize, csize, th, tl, *refs):
    terms, (parent, child) = refs[:-2], refs[-2:]
    value = terms[0][...]
    for term in terms[1:]:
        value = value + term[...]
    first = lax.axis_index("col") * s.share
    index = lax.broadcasted_iota(jnp.int32, (s.share, s.W), 0) + first
    plive = jnp.concatenate([index < psize[k] for k in range(s.slots)], axis=0)
    clive = jnp.concatenate([index < csize[k] for k in range(s.slots)], axis=0)
    y = jnp.where(plive, -value[:, : s.W], 0.0)
    carried = dot3(split(y), (th[...], tl[...]), NN)
    z = jnp.where(clive, -(value[:, s.W :] + carried), 0.0)
    parent[...] = jnp.zeros_like(parent)
    child[...] = jnp.zeros_like(child)
    for slot in range(s.slots):

        @pl.when(blocks[slot] >= 0)
        def _():
            at = lax.div(blocks[slot], s.R) * s.share
            rows = pl.ds(pl.multiple_of(at, s.share), s.share)
            parent[rows, :] = y[slot * s.share : (slot + 1) * s.share, :]
            child[rows, :] = z[slot * s.share : (slot + 1) * s.share, :]


def swap_perm(s):
    return [
        ((q * s.C + a) * s.C + c, (q * s.C + c) * s.C + a)
        for q in range(s.Q)
        for a in range(s.C)
        for c in range(s.C)
    ]


def fast_body(
    cached_inverse,
    parent_panel,
    parent_blocks,
    parent_sizes,
    parent_diagonal,
    child_panel,
    child_top,
    child_blocks,
    child_sizes,
    child_diagonal,
):
    R, C = lax.axis_size("row"), lax.axis_size("col")
    B = cached_inverse.shape[2]
    s = Shape(R, C, parent_panel, cached_inverse, parent_diagonal.shape[1])
    W, ws, live = s.W, s.ws, s.live
    cached = cached_inverse.reshape(-1, B)
    bind = lambda kernel: functools.partial(kernel, s)
    numbers = pltpu.SMEM((s.slots,), jnp.int32)
    by_slot = (s.slots, ws, B)
    with jax.named_scope("pack"):
        sent, mine = call(
            bind(pack),
            hbm(
                parent_blocks,
                parent_sizes,
                child_sizes,
                jnp.transpose(parent_panel, (1, 0, 2)),
                jnp.transpose(child_panel, (1, 0, 2)),
                child_top,
            ),
            [(s.block, B), (s.payload, B)],
            [numbers] * 3
            + [pltpu.VMEM(by_slot, f32)] * 2
            + [pltpu.VMEM((ws, W), f32), pltpu.SemaphoreType.DMA((6,))],
            limit=None,
        )
    with jax.named_scope("swap"):
        own = lax.ppermute(sent, ("row", "col"), swap_perm(s))
    with jax.named_scope("split_live"):
        sh, sl = call(
            bind(split_live),
            hbm(cached, parent_blocks),
            [((live, s.CC * B), bf16)] * 2,
            [pltpu.VMEM((s.slots * B * s.CC, B), f32), numbers]
            + [pltpu.SemaphoreType.DMA((1 + s.slots,))],
        )
    with jax.named_scope("owned"):
        owned = {0: mine, 1: flip(mine, 1, C)}
        mask = C // 2
        while mask > 1:
            owned.update({m ^ mask: flip(owned[m], mask, C) for m in owned if m != 1})
            mask //= 2
        owned.update({m ^ 1: flip(owned[m], 1, C) for m in list(owned) if m > 1})
    with jax.named_scope("order"):
        own, owned[1], sh, sl = call(bind(order), (), (), passed=(own, owned[1], sh, sl))
    with jax.named_scope("panels"):
        panels = {0: own}
        for mask in range(2, R, 2):
            panels[mask] = exchange(own, mask, R)
        for mask in range(0, R, 2):
            panels[mask + 1] = exchange(panels[mask], 1, R)
    with jax.named_scope("shares_of"):
        pair = lambda rows, cols: [((rows, cols), bf16)] * 2
        *shares, gh, gl, th, tl, ih, il, base, extra = call(
            bind(shares_of),
            vmem(parent_diagonal, sh, sl, *[panels[m] for m in range(R)]),
            [(s.slots * s.share, 2 * W)] * C
            + pair(live, 2 * W)
            + pair(W, W)
            + pair(W, W)
            + [(ws, W), (W, W)],
            [pltpu.VMEM((s.CC + 1, 2 * W, B), bf16)] * 2
            + [pltpu.VMEM((live, 2 * W), f32), pltpu.VMEM((W, W), f32)],
        )
    with jax.named_scope("products"):
        lh, ll, gh, gl = call(
            bind(collect),
            vmem(*[owned[m] for m in range(C)]),
            pair(2 * W, live),
            ahead=3e9,
            passed=(gh, gl),
        )
        keep, send = call(
            bind(products),
            vmem(gh, gl, th, tl, ih, il, extra, lh, ll),
            [(3 * W // 2, W)] * 2,
            [pltpu.VMEM((3 * W, W), f32)],
        )
    with jax.named_scope("sum_core"):
        got = exchange(send, 1, R)
    with jax.named_scope("sum_shares"):
        arrived, mask = [shares[0]], 1
        while mask < C:
            far = list(range(3 * mask, C, 2 * mask))
            if far:
                come = [flip(shares[m], mask, C) for m in far]
                to = [m ^ mask for m in far]
                added = call(
                    bind(plus),
                    vmem(*[shares[m] for m in to], *come),
                    [shares[0].shape] * len(far),
                    ahead=6e9,
                )
                for m, value in zip(to, added):
                    shares[m] = value
            mask *= 2
    with jax.named_scope("sum_chips"):
        *mine, shares[2] = call(
            bind(add_chips),
            vmem(keep, got),
            [(C * 3 * s.eight, W)] * s.chips,
            passed=(shares[2],),
        )
        mine = [mine[0]] + [exchange(mine[m], 2 * m, R) for m in range(1, s.chips)]
    with jax.named_scope("sum_shares"):
        mask = 1
        while mask < C:
            arrived.append(flip(shares[mask], mask, C))
            mask *= 2
    with jax.named_scope("sum_cols"):
        scr = [pltpu.VMEM((C * 3 * s.eight, W), f32)]
        cols = call(bind(add_cols), vmem(*mine), [(3 * s.eight, W)] * C, scr)
        cols = [cols[0]] + [flip(cols[m], m, C) for m in range(1, C)]
    with jax.named_scope("rows_out"):
        parent_rows, child_rows = call(
            bind(rows_out),
            smem(parent_blocks, parent_sizes, child_sizes) + vmem(th, tl, *arrived),
            [(s.RC * s.share, W)] * 2,
        )
    with jax.named_scope("spread"):
        done, parent_rows, child_rows = call(
            bind(add_all), vmem(*cols), [(3 * s.eight, W)], passed=(parent_rows, child_rows)
        )
        parts = {0: done}
        for mask in range(2, R, 2):
            parts[mask] = exchange(done, mask, R)
        for mask in range(0, R, 2):
            parts[mask + 1] = exchange(parts[mask], 1, R)
    with jax.named_scope("finish"):
        parent_diag, child_upper, child_diag = call(
            bind(finish),
            vmem(parent_diagonal, child_diagonal, base, *[parts[m] for m in range(R)]),
            [(ws, W)] * 3,
        )
    shape = (s.RC, 1, s.share, W)
    return (
        parent_rows.reshape(shape),
        parent_diag,
        child_rows.reshape(shape),
        child_upper,
        child_diag,
    )


highest = lax.Precision.HIGHEST


def from_root(value, axis, source):
    kept = jnp.where(lax.axis_index(axis) == source, value, 0).astype(value.dtype)
    return lax.psum(kept, axis)


def live_rows(sizes, block_rows):
    return (jnp.arange(block_rows, dtype=jnp.int32)[None, :] < sizes[:, None]).astype(jnp.float32)


def own_share(widened, blocks, row_live, row_index, row_total, col_index, row_share, local_rows):
    wanted = jnp.arange(local_rows, dtype=jnp.int32) * row_total + row_index
    onehot = (blocks[None, :] == wanted[:, None]).astype(jnp.float32)
    sliced = lax.dynamic_slice_in_dim(widened, col_index * row_share, row_share, 2)
    own_rows = jnp.einsum("rk,wkb->rbw", onehot, sliced, precision=highest)
    live_part = lax.dynamic_slice_in_dim(row_live, col_index * row_share, row_share, 1)
    row_alive = jnp.einsum("rk,kb->rb", onehot, live_part, precision=highest)
    return (own_rows, row_alive)


def add_columns(column_dense, widened, blocks, col_index, col_total):
    wanted = jnp.arange(column_dense.shape[0], dtype=jnp.int32) * col_total + col_index
    onehot = (blocks[None, :] == wanted[:, None]).astype(jnp.float32)
    return column_dense + jnp.einsum("ck,wky->cwy", onehot, widened, precision=highest)


def column_panel(widened, blocks, col_index, col_total, row_total, col_blocks):
    column_dense = jnp.zeros((col_blocks, widened.shape[0], widened.shape[2]), jnp.float32)
    for repeat in range(row_total // col_total):
        sender = col_index + repeat * col_total
        heard_panel, heard_blocks = (
            from_root(widened, "row", sender),
            from_root(blocks, "row", sender),
        )
        column_dense = add_columns(column_dense, heard_panel, heard_blocks, col_index, col_total)
    return column_dense


def child_panels(
    child_panel, child_top, child_live, child_blocks, col_index, col_total, row_total, col_blocks
):
    wide_child, top_full = (
        lax.all_gather(child_panel, "col", axis=0, tiled=True),
        lax.all_gather(child_top, "col", axis=0, tiled=True),
    )
    child_full = wide_child * child_live[None, :, :]
    child_dense = column_panel(
        child_full, child_blocks, col_index, col_total, row_total, col_blocks
    )
    return (child_full, child_dense, top_full)


def apply_inverse(cached, column_dense):
    summed = lax.psum_scatter(
        jnp.einsum(
            "rxcy,cwy->xrw",
            cached,
            column_dense,
            precision=highest,
            preferred_element_type=jnp.float32,
        ),
        "col",
        scatter_dimension=0,
        tiled=True,
    )
    return jnp.transpose(summed, (1, 0, 2))


def diagonal_sum(partial_rows, panel_width, col_share, col_index):
    entire = lax.psum(partial_rows(0, panel_width), ("row", "col"))
    return lax.dynamic_slice_in_dim(entire, col_index * col_share, col_share, 0)


def body(
    cached_inverse,
    parent_panel,
    parent_blocks,
    parent_sizes,
    parent_diagonal,
    child_panel,
    child_top,
    child_blocks,
    child_sizes,
    child_diagonal,
):
    row_total = lax.axis_size("row")
    col_total = lax.axis_size("col")
    row_index = lax.axis_index("row")
    col_index = lax.axis_index("col")
    local_rows = cached_inverse.shape[0]
    block_rows = cached_inverse.shape[2]
    col_blocks = cached_inverse.shape[3]
    cached = cached_inverse.reshape(local_rows, block_rows, col_blocks, block_rows)
    panel_width = parent_diagonal.shape[1]
    row_share = block_rows // col_total
    col_share = panel_width // col_total
    parent_live = live_rows(parent_sizes, block_rows)
    child_live = live_rows(child_sizes, block_rows)
    wide_parent = lax.all_gather(parent_panel, "col", axis=0, tiled=True)
    parent_full = wide_parent * parent_live[None, :, :]
    parent_dense = column_panel(
        parent_full, parent_blocks, col_index, col_total, row_total, col_blocks
    )
    child_full, child_dense, top_full = child_panels(
        child_panel,
        child_top,
        child_live,
        child_blocks,
        col_index,
        col_total,
        row_total,
        col_blocks,
    )
    parent_own, parent_alive = own_share(
        parent_full,
        parent_blocks,
        parent_live,
        row_index,
        row_total,
        col_index,
        row_share,
        local_rows,
    )
    both_local = apply_inverse(cached, jnp.concatenate([parent_dense, child_dense], axis=1))
    parent_local = -both_local[:, :, :panel_width] * parent_alive[:, :, None]
    child_own, child_alive = own_share(
        child_full, child_blocks, child_live, row_index, row_total, col_index, row_share, local_rows
    )
    carried = jnp.einsum("rbw,wv->rbv", parent_local, top_full, precision=highest)
    child_local = -(both_local[:, :, panel_width:] + carried) * child_alive[:, :, None]

    def stacked_terms(offset, amount):
        first_part = jnp.einsum("rbw,rbv->wv", parent_own, parent_local, precision=highest)
        second_part = jnp.einsum("rbw,rbv->wv", parent_local, child_own, precision=highest)
        third_part = jnp.einsum("rbc,rbv->cv", child_own, child_local, precision=highest)
        return jnp.concatenate([first_part, second_part, third_part], axis=1)

    stacked_sum = diagonal_sum(stacked_terms, panel_width, col_share, col_index)
    parent_diag = parent_diagonal - stacked_sum[:, :panel_width]
    child_upper = -(
        jnp.dot(parent_diag, top_full, precision=highest, preferred_element_type=jnp.float32)
        + stacked_sum[:, panel_width : 2 * panel_width]
    )
    upper_whole = lax.all_gather(child_upper, "col", axis=0, tiled=True)
    top_columns = lax.dynamic_slice_in_dim(top_full, col_index * col_share, col_share, 1)
    child_diag = (
        child_diagonal
        - jnp.dot(top_columns.T, upper_whole, precision=highest, preferred_element_type=jnp.float32)
        - stacked_sum[:, 2 * panel_width :]
    )
    return (
        parent_local[:, None, :, :],
        parent_diag,
        child_local[:, None, :, :],
        child_upper,
        child_diag,
    )


def fits(rows, cols, panel, cached, width):
    s = Shape(rows, cols, panel, cached, width)
    return (
        rows & (rows - 1) == 0
        and cols & (cols - 1) == 0
        and rows % cols == 0
        and cols > 2
        and s.Q == 2
        and width == 2 * s.B
        and s.ws % 16 == 0
        and s.share % 16 == 0
        and s.ws % rows == 0
        and s.eight % 8 == 0
        and width % s.B == 0
    )


def chosen(*args):
    sizes = lax.axis_size("row"), lax.axis_size("col")
    ok = fits(*sizes, args[1], args[0], args[4].shape[1])
    return (fast_body if ok else body)(*args)


def solution(mesh):
    in_specs = (
        P(None, "row", None, None, "col", None),
        P("col", "row", None),
        P("row"),
        P("row"),
        P("col", None),
        P("col", "row", None),
        P("col", None),
        P("row"),
        P("row"),
        P("col", None),
    )
    out_specs = (
        P(None, "row", "col", None),
        P("col", None),
        P(None, "row", "col", None),
        P("col", None),
        P("col", None),
    )
    return jax.shard_map(chosen, mesh=mesh, in_specs=in_specs, out_specs=out_specs, check_vma=False)
```

```python
import functools

import jax
import jax.numpy as jnp
from jax import lax
from jax.experimental import pallas as pl
from jax.experimental.pallas import tpu as pltpu
from jax.sharding import PartitionSpec as P

f32 = jnp.float32
bf16 = jnp.bfloat16

NN = (((1,), (0,)), ((), ()))
NT = (((1,), (1,)), ((), ()))
TN = (((0,), (0,)), ((), ()))


def split(value):
    high = value.astype(bf16)
    return high, (value - high.astype(f32)).astype(bf16)


def dot3(left, right, dims):
    (lh, ll), (rh, rl) = left, right
    on_left, on_right = dims[0][0][0], dims[0][1][0]
    return lax.dot_general(
        jnp.concatenate([lh, lh, ll], axis=on_left),
        jnp.concatenate([rh, rl, rh], axis=on_right),
        dims,
        preferred_element_type=f32,
    )


def call(kernel, inputs, outs, scratch=(), ahead=0, limit=40, passed=()):
    alias = {len(inputs) + i: len(outs) + i for i in range(len(passed))}
    spaces = [pltpu.VMEM] * len(outs) + [pl.ANY] * len(passed)
    inputs = list(inputs) + [(pl.ANY, a) for a in passed]
    outs = list(outs) + [(a.shape, a.dtype) for a in passed]
    arrays = [a for _, a in inputs]
    shapes = [jax.ShapeDtypeStruct(*(o if isinstance(o[0], tuple) else (o, f32))) for o in outs]
    nbytes = sum(a.size * a.dtype.itemsize for a in arrays + shapes)
    return pl.pallas_call(
        kernel,
        out_shape=shapes,
        in_specs=[pl.BlockSpec(memory_space=space) for space, _ in inputs],
        out_specs=[pl.BlockSpec(memory_space=space) for space in spaces],
        scratch_shapes=list(scratch),
        input_output_aliases=alias,
        compiler_params=pltpu.CompilerParams(vmem_limit_bytes=limit and limit * 1024 * 1024),
        cost_estimate=pl.CostEstimate(flops=int(ahead), bytes_accessed=nbytes, transcendentals=0),
    )(*arrays)


def vmem(*arrays):
    return [(pltpu.VMEM, a) for a in arrays]


def smem(*arrays):
    return [(pltpu.SMEM, a) for a in arrays]


def anywhere(*arrays):
    return [(pl.ANY, a) for a in arrays]


def fetch(sources, targets, sems):
    copies = [
        pltpu.make_async_copy(a, b, sems.at[i]) for i, (a, b) in enumerate(zip(sources, targets))
    ]
    for copy in copies:
        copy.start()
    return copies


def exchange(value, mask, row_total):
    return lax.ppermute(value, "row", [(i, i ^ mask) for i in range(row_total)])


def shift(value, step, col_total):
    return lax.ppermute(value, "col", [(i, (i + step) % col_total) for i in range(col_total)])


def flip(value, mask, col_total):
    return lax.ppermute(value, "col", [(i, i ^ mask) for i in range(col_total)])


class Shape:
    def __init__(self, rows, cols, panel, cached, width):
        self.R, self.C = rows, cols
        self.ws, self.slots, self.B = panel.shape
        self.W = width
        self.RC = cached.shape[0]
        self.CC = cached.shape[3]
        self.Q = rows // cols
        self.payload = self.slots * 2 * self.ws
        self.share = self.B // cols
        self.chips = rows // 2
        self.eight = self.ws // rows
        self.live = self.slots * self.B
        self.parts = self.W // self.B
        self.part = self.payload // 2
        self.block = self.part + self.ws // 2 + 8


def pack(s, *refs):
    sources, (kept, sent, mine, parents, children, *targets, sems) = refs[:6], refs[6:]
    for copy in fetch(sources, targets, sems):
        copy.wait()
    blocks, psize, csize, parent, child, top = targets
    row = lax.axis_index("row")
    side = lax.div(lax.rem(row, s.C), s.C // 2)
    lane = lax.broadcasted_iota(jnp.int32, (s.ws, s.B), 1)
    for slot in range(s.slots):
        base = slot * 2 * s.ws
        for which, panel, sizes, half in ((0, parent, psize, parents), (1, child, csize, children)):
            live = jnp.where(lane < sizes[slot], panel[slot], 0.0)
            mine[base + which * s.ws : base + (which + 1) * s.ws, :] = live
            half[slot * s.ws : (slot + 1) * s.ws, :] = live
    columns = pl.ds(pl.multiple_of(lax.div(row, s.C) * s.B, s.B), s.B)
    row8 = lax.broadcasted_iota(jnp.int32, (8, s.B), 0)
    ids = jnp.zeros((8, s.B), f32)
    for slot in range(s.slots):
        ids = jnp.where(row8 == slot, blocks[slot].astype(f32), ids)
    quarter = s.ws // 2
    for out, at in ((kept, side), (sent, 1 - side)):

        @pl.when(at == 0)
        def _():
            out[: s.part, :] = parents[...]

        @pl.when(at == 1)
        def _():
            out[: s.part, :] = children[...]

        rows = pl.ds(pl.multiple_of(at * quarter, quarter), quarter)
        out[s.part : s.part + quarter, :] = top[rows, columns]
        out[s.part + quarter :, :] = ids


def route(s, kept, got, first, second, sems):
    side = lax.div(lax.rem(lax.axis_index("row"), s.C), s.C // 2)
    high = lax.div(lax.axis_index("col"), s.C // 2)
    own = high == side

    @pl.when(own)
    def _():
        for copy in fetch((kept, got), (first, second), sems):
            copy.wait()

    @pl.when(jnp.logical_not(own))
    def _():
        for copy in fetch((got, kept), (first, second), sems):
            copy.wait()


def join(s, first, second, *refs):
    out = refs[-1 - (len(refs) - 1) // 2]
    out[: s.block, :] = first[...]
    out[s.block :, :] = second[...]


def order(s, *refs):
    pass


def split_live(s, cached, blocks, high, low, held, numbers, sems):
    copy = pltpu.make_async_copy(blocks, numbers, sems.at[0])
    copy.start()
    copy.wait()
    size = s.B * s.CC
    copies = []
    for slot in range(s.slots):
        p = lax.div(jnp.maximum(numbers[slot], 0), s.R)
        source = cached.at[pl.ds(pl.multiple_of(p * size, size), size), :]
        copy = pltpu.make_async_copy(source, held.at[pl.ds(slot * size, size), :], sems.at[1 + slot])
        copy.start()
        copies.append(copy)
    for slot in range(s.slots):
        copies[slot].wait()
        rows = slice(slot * s.B, (slot + 1) * s.B)
        for m in range(s.CC):
            h, l = split(held[pl.ds(slot * size + m, s.B, stride=s.CC), :])
            high[rows, m * s.B : (m + 1) * s.B] = h
            low[rows, m * s.B : (m + 1) * s.B] = l


def shares_of(s, pd, sh, sl, *refs):
    panels, refs = refs[: s.R], refs[s.R :]
    shares, refs = refs[: s.C], refs[s.C :]
    gh, gl, th, tl, ih, il, base, extra, xh, xl, total, top = refs
    row, col = lax.axis_index("row"), lax.axis_index("col")
    places = []
    for owner in range(s.Q):
        for slot in range(s.slots):
            at = s.block - 8 + slot
            number = jnp.max(panels[owner * s.C][at : at + 1, :]).astype(jnp.int32)
            places.append(jnp.where(number < 0, s.CC, lax.div(jnp.maximum(number, 0), s.C)))
    for m in range(s.CC):
        taken = places[0] == m
        for place in places[1:]:
            taken = jnp.logical_or(taken, place == m)

        @pl.when(jnp.logical_not(taken))
        def _():
            xh[m] = jnp.zeros((2 * s.W, s.B), bf16)
            xl[m] = jnp.zeros((2 * s.W, s.B), bf16)

    high, quarter = lax.div(col, s.C // 2), s.ws // 2
    for mask in range(s.R):
        sender = jnp.bitwise_xor(row, mask)
        owner, inside = lax.div(sender, s.C), lax.rem(sender, s.C)
        side, low = lax.div(inside, s.C // 2), lax.rem(inside, s.C // 2)
        lanes = pl.ds(pl.multiple_of(owner * s.B, s.B), s.B)
        for turn in range(2):
            source = jnp.bitwise_xor(high, turn) * (s.C // 2) + low
            begin = turn * s.block
            rows = pl.ds(pl.multiple_of(side * s.W + source * s.ws, s.ws), s.ws)
            for slot in range(s.slots):
                place = places[mask // s.C * s.slots + slot]
                start = begin + slot * s.ws
                up, down = split(panels[mask][start : start + s.ws, :])
                xh[place, rows, :] = up
                xl[place, rows, :] = down
            start = begin + s.part
            rows = pl.ds(pl.multiple_of(source * s.ws + side * quarter, quarter), quarter)
            top[rows, lanes] = panels[mask][start : start + quarter, :]
    right = tuple(jnp.concatenate([x[i] for i in range(s.CC)], axis=1) for x in (xh, xl))
    total[...] = dot3((sh[...], sl[...]), right, NT)
    gh[...], gl[...] = split(total[...])
    for mask in range(s.C):
        target = jnp.bitwise_xor(col, mask)
        for slot in range(s.slots):
            start = pl.multiple_of(slot * s.B + target * s.share, s.share)
            rows = slice(slot * s.share, (slot + 1) * s.share)
            shares[mask][rows, :] = total[pl.ds(start, s.share), :]
    th[...], tl[...] = split(top[...])
    ih[...], il[...] = split(top[...].T)
    lead = dot3(split(pd[...]), (th[...], tl[...]), NN)
    base[...] = -lead
    own = top[pl.ds(pl.multiple_of(col * s.ws, s.ws), s.ws), :]
    extra[...] = dot3(split(own), split(lead * (1.0 / s.R)), TN)


def collect(s, *refs):
    owned, (lh, ll) = refs[: s.C], refs[s.C + 2 : s.C + 4]
    col = lax.axis_index("col")
    for mask in range(s.C):
        source = jnp.bitwise_xor(col, mask)
        for slot in range(s.slots):
            for which in range(2):
                start = (slot * 2 + which) * s.ws
                rows = pl.ds(pl.multiple_of(which * s.W + source * s.ws, s.ws), s.ws)
                lanes = slice(slot * s.B, (slot + 1) * s.B)
                lh[rows, lanes], ll[rows, lanes] = split(owned[mask][start : start + s.ws, :])


def products(s, gh, gl, th, tl, ih, il, extra, lh, ll, keep, send, both):
    core = lax.rem(lax.axis_index("row"), 2)
    W = s.W
    first = dot3((lh[...], ll[...]), (gh[:, :W], gl[:, :W]), NN)
    d = dot3((lh[W:, :], ll[W:, :]), (gh[:, W:], gl[:, W:]), NN)
    second = dot3(split(first), (th[...], tl[...]), NN)
    third = dot3((ih[...], il[...]), split(second[:W]), NN)
    both[0:W, :] = first[:W]
    both[W : 2 * W, :] = first[W:].T - second[:W]
    cross = second[W:]
    both[2 * W :, :] = d - cross - cross.T + third + extra[...]
    n = s.eight
    for out, swap in ((keep, 0), (send, 1)):
        offset = jnp.bitwise_xor(core, swap) * (s.ws // 2)
        for chip in range(s.chips):
            for source in range(s.C):
                for kind in range(3):
                    at = pl.multiple_of(kind * W + source * s.ws + chip * n + offset, n)
                    to = ((chip * s.C + source) * 3 + kind) * n
                    out[to : to + n, :] = both[pl.ds(at, n), :]


def add_chips(s, kept, got, share, *outs):
    outs = outs[: s.chips]
    size = s.C * 3 * s.eight
    chip = lax.div(lax.axis_index("row"), 2)
    for mask in range(s.chips):
        rows = pl.ds(pl.multiple_of(jnp.bitwise_xor(chip, mask) * size, size), size)
        outs[mask][...] = kept[rows, :] + got[rows, :]


def add_cols(s, *refs):
    terms, outs, total = refs[: s.chips], refs[s.chips : -1], refs[-1]
    size = 3 * s.eight
    col = lax.axis_index("col")
    value = terms[0][...]
    for term in terms[1:]:
        value = value + term[...]
    total[...] = value
    for step in range(s.C):
        rows = pl.ds(pl.multiple_of(lax.rem(col + step, s.C) * size, size), size)
        outs[step][...] = total[rows, :]


def plus(s, *refs):
    count = len(refs) // 3
    for one, two, out in zip(refs[:count], refs[count : 2 * count], refs[2 * count :]):
        out[...] = one[...] + two[...]


def add_all(s, *refs):
    terms, out = refs[:-1], refs[-1]
    value = terms[0][...]
    for term in terms[1:]:
        value = value + term[...]
    out[...] = value


def finish(s, pd, cd, base, *refs):
    parts, outs = refs[: s.R], refs[s.R :]
    row = lax.axis_index("row")
    n = s.eight
    starts = (pd, base, cd)
    for mask in range(s.R):
        source = jnp.bitwise_xor(row, mask)
        at = lax.rem(source, 2) * (s.ws // 2) + lax.div(source, 2) * n
        rows = pl.ds(pl.multiple_of(at, n), n)
        for kind in range(3):
            outs[kind][rows, :] = starts[kind][rows, :] + parts[mask][kind * n : (kind + 1) * n, :]


def rows_out(s, blocks, psize, csize, th, tl, *refs):
    terms, (parent, child) = refs[:-2], refs[-2:]
    value = terms[0][...]
    for term in terms[1:]:
        value = value + term[...]
    first = lax.axis_index("col") * s.share
    index = lax.broadcasted_iota(jnp.int32, (s.share, s.W), 0) + first
    plive = jnp.concatenate([index < psize[k] for k in range(s.slots)], axis=0)
    clive = jnp.concatenate([index < csize[k] for k in range(s.slots)], axis=0)
    y = jnp.where(plive, -value[:, : s.W], 0.0)
    carried = dot3(split(y), (th[...], tl[...]), NN)
    z = jnp.where(clive, -(value[:, s.W :] + carried), 0.0)
    parent[...] = jnp.zeros_like(parent)
    child[...] = jnp.zeros_like(child)
    for slot in range(s.slots):

        @pl.when(blocks[slot] >= 0)
        def _():
            at = lax.div(blocks[slot], s.R) * s.share
            rows = pl.ds(pl.multiple_of(at, s.share), s.share)
            parent[rows, :] = y[slot * s.share : (slot + 1) * s.share, :]
            child[rows, :] = z[slot * s.share : (slot + 1) * s.share, :]


def column_perm(s, turn):
    half, pairs = s.C // 2, []
    for q in range(s.Q):
        for at in range(s.C):
            for c in range(s.C):
                to = (turn ^ c // half) * half + at % half
                row = q * s.C + at // half * half + c % half
                pairs.append(((q * s.C + at) * s.C + c, row * s.C + to))
    return pairs


def fast_body(
    cached_inverse,
    parent_panel,
    parent_blocks,
    parent_sizes,
    parent_diagonal,
    child_panel,
    child_top,
    child_blocks,
    child_sizes,
    child_diagonal,
):
    R, C = lax.axis_size("row"), lax.axis_size("col")
    B = cached_inverse.shape[2]
    s = Shape(R, C, parent_panel, cached_inverse, parent_diagonal.shape[1])
    W, ws, live = s.W, s.ws, s.live
    cached = cached_inverse.reshape(-1, B)
    bind = lambda kernel: functools.partial(kernel, s)
    numbers = pltpu.SMEM((s.slots,), jnp.int32)
    by_slot = (s.slots, ws, B)
    with jax.named_scope("pack"):
        kept, sent, mine, parents, children = call(
            bind(pack),
            anywhere(
                parent_blocks,
                parent_sizes,
                child_sizes,
                jnp.transpose(parent_panel, (1, 0, 2)),
                jnp.transpose(child_panel, (1, 0, 2)),
                child_top,
            ),
            [(s.block, B)] * 2 + [(s.payload, B)] + [(s.part, B)] * 2,
            [numbers] * 3
            + [pltpu.VMEM(by_slot, f32)] * 2
            + [pltpu.VMEM((ws, W), f32), pltpu.SemaphoreType.DMA((6,))],
            limit=None,
        )
    with jax.named_scope("to_column"):
        got = exchange(sent, C // 2, R)
        pieces = call(
            bind(route),
            anywhere(kept, got),
            [(s.block, B)] * 2,
            [pltpu.SemaphoreType.DMA((2,))],
        )
        pieces = [
            lax.ppermute(pieces[turn], ("row", "col"), column_perm(s, turn)) for turn in range(2)
        ]
    with jax.named_scope("split_live"):
        sh, sl = call(
            bind(split_live),
            anywhere(cached, parent_blocks),
            [((live, s.CC * B), bf16)] * 2,
            [pltpu.VMEM((s.slots * B * s.CC, B), f32), numbers]
            + [pltpu.SemaphoreType.DMA((1 + s.slots,))],
        )
    with jax.named_scope("owned"):
        near = flip(mine, 1, C)
        held, mask = {0: mine}, C // 2
        while mask > 1:
            held.update({m ^ mask: flip(held[m], mask, C) for m in list(held)})
            mask //= 2
        owned = {0: mine, 1: near}
        for m in range(2, C, 2):
            (owned[m],) = call(bind(order), (), (), passed=(held[m],), ahead=8e9)
            owned[m + 1] = flip(owned[m], 1, C)
    with jax.named_scope("join"):
        own, owned[1], sh, sl = call(
            bind(join), vmem(*pieces), [(2 * s.block, B)], passed=(owned[1], sh, sl)
        )
    with jax.named_scope("panels"):
        panels = {0: own}
        for mask in range(2, R, 2):
            panels[mask] = exchange(own, mask, R)
        for mask in range(0, R, 2):
            panels[mask + 1] = exchange(panels[mask], 1, R)
    with jax.named_scope("shares_of"):
        pair = lambda rows, cols: [((rows, cols), bf16)] * 2
        *shares, gh, gl, th, tl, ih, il, base, extra = call(
            bind(shares_of),
            vmem(parent_diagonal, sh, sl, *[panels[m] for m in range(R)]),
            [(s.slots * s.share, 2 * W)] * C
            + pair(live, 2 * W)
            + pair(W, W)
            + pair(W, W)
            + [(ws, W), (W, W)],
            [pltpu.VMEM((s.CC + 1, 2 * W, B), bf16)] * 2
            + [pltpu.VMEM((live, 2 * W), f32), pltpu.VMEM((W, W), f32)],
        )
    with jax.named_scope("products"):
        lh, ll, gh, gl = call(
            bind(collect),
            vmem(*[owned[m] for m in range(C)]),
            pair(2 * W, live),
            ahead=3e9,
            passed=(gh, gl),
        )
        keep, send = call(
            bind(products),
            vmem(gh, gl, th, tl, ih, il, extra, lh, ll),
            [(3 * W // 2, W)] * 2,
            [pltpu.VMEM((3 * W, W), f32)],
        )
    with jax.named_scope("sum_core"):
        got = exchange(send, 1, R)
    with jax.named_scope("sum_shares"):
        arrived, mask = [shares[0]], 1
        while mask < C:
            far = list(range(3 * mask, C, 2 * mask))
            if far:
                come = [flip(shares[m], mask, C) for m in far]
                to = [m ^ mask for m in far]
                added = call(
                    bind(plus),
                    vmem(*[shares[m] for m in to], *come),
                    [shares[0].shape] * len(far),
                    ahead=6e9,
                )
                for m, value in zip(to, added):
                    shares[m] = value
            mask *= 2
    with jax.named_scope("sum_chips"):
        *mine, shares[2] = call(
            bind(add_chips),
            vmem(keep, got),
            [(C * 3 * s.eight, W)] * s.chips,
            passed=(shares[2],),
        )
        mine = [mine[0]] + [exchange(mine[m], 2 * m, R) for m in range(1, s.chips)]

    with jax.named_scope("sum_shares"):
        mask = 1
        while mask < C:
            arrived.append(flip(shares[mask], mask, C))
            mask *= 2
    with jax.named_scope("sum_cols"):
        scr = [pltpu.VMEM((C * 3 * s.eight, W), f32)]
        cols = call(bind(add_cols), vmem(*mine), [(3 * s.eight, W)] * C, scr)
        cols = [cols[0]] + [shift(cols[k], k, C) for k in range(1, C)]
    with jax.named_scope("spread"):
        (done,) = call(bind(add_all), vmem(*cols), [(3 * s.eight, W)])
        parts = {0: done}
        for mask in range(2, R, 2):
            parts[mask] = exchange(done, mask, R)
    with jax.named_scope("rows_out"):
        parent_rows, child_rows = call(
            bind(rows_out),
            smem(parent_blocks, parent_sizes, child_sizes) + vmem(th, tl, *arrived),
            [(s.RC * s.share, W)] * 2,
        )
    with jax.named_scope("spread"):
        parts[R - 2], parent_rows, child_rows = call(
            bind(order), (), (), passed=(parts[R - 2], parent_rows, child_rows)
        )
        for mask in range(0, R, 2):
            parts[mask + 1] = exchange(parts[mask], 1, R)
    with jax.named_scope("finish"):
        parent_diag, child_upper, child_diag = call(
            bind(finish),
            vmem(parent_diagonal, child_diagonal, base, *[parts[m] for m in range(R)]),
            [(ws, W)] * 3,
        )
    shape = (s.RC, 1, s.share, W)
    return (
        parent_rows.reshape(shape),
        parent_diag,
        child_rows.reshape(shape),
        child_upper,
        child_diag,
    )


highest = lax.Precision.HIGHEST


def from_root(value, axis, source):
    kept = jnp.where(lax.axis_index(axis) == source, value, 0).astype(value.dtype)
    return lax.psum(kept, axis)


def live_rows(sizes, block_rows):
    return (jnp.arange(block_rows, dtype=jnp.int32)[None, :] < sizes[:, None]).astype(jnp.float32)


def own_share(widened, blocks, row_live, row_index, row_total, col_index, row_share, local_rows):
    wanted = jnp.arange(local_rows, dtype=jnp.int32) * row_total + row_index
    onehot = (blocks[None, :] == wanted[:, None]).astype(jnp.float32)
    sliced = lax.dynamic_slice_in_dim(widened, col_index * row_share, row_share, 2)
    own_rows = jnp.einsum("rk,wkb->rbw", onehot, sliced, precision=highest)
    live_part = lax.dynamic_slice_in_dim(row_live, col_index * row_share, row_share, 1)
    row_alive = jnp.einsum("rk,kb->rb", onehot, live_part, precision=highest)
    return (own_rows, row_alive)


def add_columns(column_dense, widened, blocks, col_index, col_total):
    wanted = jnp.arange(column_dense.shape[0], dtype=jnp.int32) * col_total + col_index
    onehot = (blocks[None, :] == wanted[:, None]).astype(jnp.float32)
    return column_dense + jnp.einsum("ck,wky->cwy", onehot, widened, precision=highest)


def column_panel(widened, blocks, col_index, col_total, row_total, col_blocks):
    column_dense = jnp.zeros((col_blocks, widened.shape[0], widened.shape[2]), jnp.float32)
    for repeat in range(row_total // col_total):
        sender = col_index + repeat * col_total
        heard_panel, heard_blocks = (
            from_root(widened, "row", sender),
            from_root(blocks, "row", sender),
        )
        column_dense = add_columns(column_dense, heard_panel, heard_blocks, col_index, col_total)
    return column_dense


def child_panels(
    child_panel, child_top, child_live, child_blocks, col_index, col_total, row_total, col_blocks
):
    wide_child, top_full = (
        lax.all_gather(child_panel, "col", axis=0, tiled=True),
        lax.all_gather(child_top, "col", axis=0, tiled=True),
    )
    child_full = wide_child * child_live[None, :, :]
    child_dense = column_panel(
        child_full, child_blocks, col_index, col_total, row_total, col_blocks
    )
    return (child_full, child_dense, top_full)


def apply_inverse(cached, column_dense):
    summed = lax.psum_scatter(
        jnp.einsum(
            "rxcy,cwy->xrw",
            cached,
            column_dense,
            precision=highest,
            preferred_element_type=jnp.float32,
        ),
        "col",
        scatter_dimension=0,
        tiled=True,
    )
    return jnp.transpose(summed, (1, 0, 2))


def diagonal_sum(partial_rows, panel_width, col_share, col_index):
    entire = lax.psum(partial_rows(0, panel_width), ("row", "col"))
    return lax.dynamic_slice_in_dim(entire, col_index * col_share, col_share, 0)


def body(
    cached_inverse,
    parent_panel,
    parent_blocks,
    parent_sizes,
    parent_diagonal,
    child_panel,
    child_top,
    child_blocks,
    child_sizes,
    child_diagonal,
):
    row_total = lax.axis_size("row")
    col_total = lax.axis_size("col")
    row_index = lax.axis_index("row")
    col_index = lax.axis_index("col")
    local_rows = cached_inverse.shape[0]
    block_rows = cached_inverse.shape[2]
    col_blocks = cached_inverse.shape[3]
    cached = cached_inverse.reshape(local_rows, block_rows, col_blocks, block_rows)
    panel_width = parent_diagonal.shape[1]
    row_share = block_rows // col_total
    col_share = panel_width // col_total
    parent_live = live_rows(parent_sizes, block_rows)
    child_live = live_rows(child_sizes, block_rows)
    wide_parent = lax.all_gather(parent_panel, "col", axis=0, tiled=True)
    parent_full = wide_parent * parent_live[None, :, :]
    parent_dense = column_panel(
        parent_full, parent_blocks, col_index, col_total, row_total, col_blocks
    )
    child_full, child_dense, top_full = child_panels(
        child_panel,
        child_top,
        child_live,
        child_blocks,
        col_index,
        col_total,
        row_total,
        col_blocks,
    )
    parent_own, parent_alive = own_share(
        parent_full,
        parent_blocks,
        parent_live,
        row_index,
        row_total,
        col_index,
        row_share,
        local_rows,
    )
    both_local = apply_inverse(cached, jnp.concatenate([parent_dense, child_dense], axis=1))
    parent_local = -both_local[:, :, :panel_width] * parent_alive[:, :, None]
    child_own, child_alive = own_share(
        child_full, child_blocks, child_live, row_index, row_total, col_index, row_share, local_rows
    )
    carried = jnp.einsum("rbw,wv->rbv", parent_local, top_full, precision=highest)
    child_local = -(both_local[:, :, panel_width:] + carried) * child_alive[:, :, None]

    def stacked_terms(offset, amount):
        first_part = jnp.einsum("rbw,rbv->wv", parent_own, parent_local, precision=highest)
        second_part = jnp.einsum("rbw,rbv->wv", parent_local, child_own, precision=highest)
        third_part = jnp.einsum("rbc,rbv->cv", child_own, child_local, precision=highest)
        return jnp.concatenate([first_part, second_part, third_part], axis=1)

    stacked_sum = diagonal_sum(stacked_terms, panel_width, col_share, col_index)
    parent_diag = parent_diagonal - stacked_sum[:, :panel_width]
    child_upper = -(
        jnp.dot(parent_diag, top_full, precision=highest, preferred_element_type=jnp.float32)
        + stacked_sum[:, panel_width : 2 * panel_width]
    )
    upper_whole = lax.all_gather(child_upper, "col", axis=0, tiled=True)
    top_columns = lax.dynamic_slice_in_dim(top_full, col_index * col_share, col_share, 1)
    child_diag = (
        child_diagonal
        - jnp.dot(top_columns.T, upper_whole, precision=highest, preferred_element_type=jnp.float32)
        - stacked_sum[:, 2 * panel_width :]
    )
    return (
        parent_local[:, None, :, :],
        parent_diag,
        child_local[:, None, :, :],
        child_upper,
        child_diag,
    )


def fits(rows, cols, panel, cached, width):
    s = Shape(rows, cols, panel, cached, width)
    return (
        rows & (rows - 1) == 0
        and cols & (cols - 1) == 0
        and rows % cols == 0
        and cols > 2
        and s.Q == 2
        and width == 2 * s.B
        and s.ws % 16 == 0
        and s.share % 16 == 0
        and s.ws % rows == 0
        and s.eight % 8 == 0
        and width % s.B == 0
    )


def chosen(*args):
    sizes = lax.axis_size("row"), lax.axis_size("col")
    ok = fits(*sizes, args[1], args[0], args[4].shape[1])
    return (fast_body if ok else body)(*args)


def solution(mesh):
    in_specs = (
        P(None, "row", None, None, "col", None),
        P("col", "row", None),
        P("row"),
        P("row"),
        P("col", None),
        P("col", "row", None),
        P("col", None),
        P("row"),
        P("row"),
        P("col", None),
    )
    out_specs = (
        P(None, "row", "col", None),
        P("col", None),
        P(None, "row", "col", None),
        P("col", None),
        P("col", None),
    )
    return jax.shard_map(chosen, mesh=mesh, in_specs=in_specs, out_specs=out_specs, check_vma=False)
```

```python
import functools

import jax
import jax.numpy as jnp
from jax import lax
from jax.experimental import pallas as pl
from jax.experimental.pallas import tpu as pltpu
from jax.sharding import PartitionSpec as P

f32 = jnp.float32
bf16 = jnp.bfloat16

NN = (((1,), (0,)), ((), ()))
NT = (((1,), (1,)), ((), ()))
TN = (((0,), (0,)), ((), ()))


def split(value):
    high = value.astype(bf16)
    return high, (value - high.astype(f32)).astype(bf16)


def dot3(left, right, dims):
    (lh, ll), (rh, rl) = left, right
    on_left, on_right = dims[0][0][0], dims[0][1][0]
    return lax.dot_general(
        jnp.concatenate([lh, lh, ll], axis=on_left),
        jnp.concatenate([rh, rl, rh], axis=on_right),
        dims,
        preferred_element_type=f32,
    )


def call(kernel, inputs, outs, scratch=(), ahead=0, limit=40, passed=()):
    alias = {len(inputs) + i: len(outs) + i for i in range(len(passed))}
    spaces = [pltpu.VMEM] * len(outs) + [pl.ANY] * len(passed)
    inputs = list(inputs) + [(pl.ANY, a) for a in passed]
    outs = list(outs) + [(a.shape, a.dtype) for a in passed]
    arrays = [a for _, a in inputs]
    shapes = [jax.ShapeDtypeStruct(*(o if isinstance(o[0], tuple) else (o, f32))) for o in outs]
    nbytes = sum(a.size * a.dtype.itemsize for a in arrays + shapes)
    return pl.pallas_call(
        kernel,
        out_shape=shapes,
        in_specs=[pl.BlockSpec(memory_space=space) for space, _ in inputs],
        out_specs=[pl.BlockSpec(memory_space=space) for space in spaces],
        scratch_shapes=list(scratch),
        input_output_aliases=alias,
        compiler_params=pltpu.CompilerParams(vmem_limit_bytes=limit and limit * 1024 * 1024),
        cost_estimate=pl.CostEstimate(flops=int(ahead), bytes_accessed=nbytes, transcendentals=0),
    )(*arrays)


def vmem(*arrays):
    return [(pltpu.VMEM, a) for a in arrays]


def smem(*arrays):
    return [(pltpu.SMEM, a) for a in arrays]


def anywhere(*arrays):
    return [(pl.ANY, a) for a in arrays]


def fetch(sources, targets, sems):
    copies = [
        pltpu.make_async_copy(a, b, sems.at[i]) for i, (a, b) in enumerate(zip(sources, targets))
    ]
    for copy in copies:
        copy.start()
    return copies


def exchange(value, mask, row_total):
    return lax.ppermute(value, "row", [(i, i ^ mask) for i in range(row_total)])


def shift(value, step, col_total):
    return lax.ppermute(value, "col", [(i, (i + step) % col_total) for i in range(col_total)])


def flip(value, mask, col_total):
    return lax.ppermute(value, "col", [(i, i ^ mask) for i in range(col_total)])


class Shape:
    def __init__(self, rows, cols, panel, cached, width):
        self.R, self.C = rows, cols
        self.ws, self.slots, self.B = panel.shape
        self.W = width
        self.RC = cached.shape[0]
        self.CC = cached.shape[3]
        self.Q = rows // cols
        self.payload = self.slots * 2 * self.ws
        self.share = self.B // cols
        self.chips = rows // 2
        self.eight = self.ws // rows
        self.live = self.slots * self.B
        self.parts = self.W // self.B
        self.part = self.payload // 2
        self.block = self.part + self.ws // 2 + 8


def pack(s, *refs):
    sources, (kept, sent, mine, parents, children, *targets, sems) = refs[:6], refs[6:]
    for copy in fetch(sources, targets, sems):
        copy.wait()
    blocks, psize, csize, parent, child, top = targets
    row = lax.axis_index("row")
    side = lax.div(lax.rem(row, s.C), s.C // 2)
    lane = lax.broadcasted_iota(jnp.int32, (s.ws, s.B), 1)
    for slot in range(s.slots):
        base = slot * 2 * s.ws
        for which, panel, sizes, half in ((0, parent, psize, parents), (1, child, csize, children)):
            live = jnp.where(lane < sizes[slot], panel[slot], 0.0)
            mine[base + which * s.ws : base + (which + 1) * s.ws, :] = live
            half[slot * s.ws : (slot + 1) * s.ws, :] = live
    columns = pl.ds(pl.multiple_of(lax.div(row, s.C) * s.B, s.B), s.B)
    row8 = lax.broadcasted_iota(jnp.int32, (8, s.B), 0)
    ids = jnp.zeros((8, s.B), f32)
    for slot in range(s.slots):
        ids = jnp.where(row8 == slot, blocks[slot].astype(f32), ids)
    quarter = s.ws // 2
    for out, at in ((kept, side), (sent, 1 - side)):

        @pl.when(at == 0)
        def _():
            out[: s.part, :] = parents[...]

        @pl.when(at == 1)
        def _():
            out[: s.part, :] = children[...]

        rows = pl.ds(pl.multiple_of(at * quarter, quarter), quarter)
        out[s.part : s.part + quarter, :] = top[rows, columns]
        out[s.part + quarter :, :] = ids


def keep(s, source, target, sems):
    for copy in fetch((source,), (target,), sems):
        copy.wait()


def route(s, kept, got, first, second, sems):
    side = lax.div(lax.rem(lax.axis_index("row"), s.C), s.C // 2)
    high = lax.div(lax.axis_index("col"), s.C // 2)
    own = high == side

    @pl.when(own)
    def _():
        for copy in fetch((kept, got), (first, second), sems):
            copy.wait()

    @pl.when(jnp.logical_not(own))
    def _():
        for copy in fetch((got, kept), (first, second), sems):
            copy.wait()


def join(s, first, second, *refs):
    out = refs[-1 - (len(refs) - 1) // 2]
    out[: s.block, :] = first[...]
    out[s.block :, :] = second[...]


def order(s, *refs):
    pass


def split_live(s, cached, blocks, high, low, held, numbers, sems):
    copy = pltpu.make_async_copy(blocks, numbers, sems.at[0])
    copy.start()
    copy.wait()
    size = s.B * s.CC
    copies = []
    for slot in range(s.slots):
        p = lax.div(jnp.maximum(numbers[slot], 0), s.R)
        source = cached.at[pl.ds(pl.multiple_of(p * size, size), size), :]
        copy = pltpu.make_async_copy(source, held.at[pl.ds(slot * size, size), :], sems.at[1 + slot])
        copy.start()
        copies.append(copy)
    for slot in range(s.slots):
        copies[slot].wait()
        rows = slice(slot * s.B, (slot + 1) * s.B)
        for m in range(s.CC):
            h, l = split(held[pl.ds(slot * size + m, s.B, stride=s.CC), :])
            high[rows, m * s.B : (m + 1) * s.B] = h
            low[rows, m * s.B : (m + 1) * s.B] = l


def shares_of(s, pd, sh, sl, *refs):
    panels, refs = refs[: s.R], refs[s.R :]
    shares, refs = refs[: s.C], refs[s.C :]
    gh, gl, th, tl, ih, il, base, extra, xh, xl, total, top = refs
    row, col = lax.axis_index("row"), lax.axis_index("col")
    places = []
    for owner in range(s.Q):
        for slot in range(s.slots):
            at = s.block - 8 + slot
            number = jnp.max(panels[owner * s.C][at : at + 1, :]).astype(jnp.int32)
            places.append(jnp.where(number < 0, s.CC, lax.div(jnp.maximum(number, 0), s.C)))
    for m in range(s.CC):
        taken = places[0] == m
        for place in places[1:]:
            taken = jnp.logical_or(taken, place == m)

        @pl.when(jnp.logical_not(taken))
        def _():
            xh[m] = jnp.zeros((2 * s.W, s.B), bf16)
            xl[m] = jnp.zeros((2 * s.W, s.B), bf16)

    high, quarter = lax.div(col, s.C // 2), s.ws // 2
    for mask in range(s.R):
        sender = jnp.bitwise_xor(row, mask)
        owner, inside = lax.div(sender, s.C), lax.rem(sender, s.C)
        side, low = lax.div(inside, s.C // 2), lax.rem(inside, s.C // 2)
        lanes = pl.ds(pl.multiple_of(owner * s.B, s.B), s.B)
        for turn in range(2):
            source = jnp.bitwise_xor(high, turn) * (s.C // 2) + low
            begin = turn * s.block
            rows = pl.ds(pl.multiple_of(side * s.W + source * s.ws, s.ws), s.ws)
            for slot in range(s.slots):
                place = places[mask // s.C * s.slots + slot]
                start = begin + slot * s.ws
                up, down = split(panels[mask][start : start + s.ws, :])
                xh[place, rows, :] = up
                xl[place, rows, :] = down
            start = begin + s.part
            rows = pl.ds(pl.multiple_of(source * s.ws + side * quarter, quarter), quarter)
            top[rows, lanes] = panels[mask][start : start + quarter, :]
    right = tuple(jnp.concatenate([x[i] for i in range(s.CC)], axis=1) for x in (xh, xl))
    total[...] = dot3((sh[...], sl[...]), right, NT)
    gh[...], gl[...] = split(total[...])
    for mask in range(s.C):
        target = jnp.bitwise_xor(col, mask)
        for slot in range(s.slots):
            start = pl.multiple_of(slot * s.B + target * s.share, s.share)
            rows = slice(slot * s.share, (slot + 1) * s.share)
            shares[mask][rows, :] = total[pl.ds(start, s.share), :]
    th[...], tl[...] = split(top[...])
    ih[...], il[...] = split(top[...].T)
    lead = dot3(split(pd[...]), (th[...], tl[...]), NN)
    base[...] = -lead
    own = top[pl.ds(pl.multiple_of(col * s.ws, s.ws), s.ws), :]
    extra[...] = dot3(split(own), split(lead * (1.0 / s.R)), TN)


def collect(s, *refs):
    owned, (lh, ll) = refs[: s.C], refs[s.C + 2 : s.C + 4]
    col = lax.axis_index("col")
    for mask in range(s.C):
        source = jnp.bitwise_xor(col, mask)
        for slot in range(s.slots):
            for which in range(2):
                start = (slot * 2 + which) * s.ws
                rows = pl.ds(pl.multiple_of(which * s.W + source * s.ws, s.ws), s.ws)
                lanes = slice(slot * s.B, (slot + 1) * s.B)
                lh[rows, lanes], ll[rows, lanes] = split(owned[mask][start : start + s.ws, :])


def products(s, gh, gl, th, tl, ih, il, extra, lh, ll, keep, send, both):
    core = lax.rem(lax.axis_index("row"), 2)
    W = s.W
    first = dot3((lh[...], ll[...]), (gh[:, :W], gl[:, :W]), NN)
    d = dot3((lh[W:, :], ll[W:, :]), (gh[:, W:], gl[:, W:]), NN)
    second = dot3(split(first), (th[...], tl[...]), NN)
    third = dot3((ih[...], il[...]), split(second[:W]), NN)
    both[0:W, :] = first[:W]
    both[W : 2 * W, :] = first[W:].T - second[:W]
    cross = second[W:]
    both[2 * W :, :] = d - cross - cross.T + third + extra[...]
    n = s.eight
    for out, swap in ((keep, 0), (send, 1)):
        offset = jnp.bitwise_xor(core, swap) * (s.ws // 2)
        for chip in range(s.chips):
            for source in range(s.C):
                for kind in range(3):
                    at = pl.multiple_of(kind * W + source * s.ws + chip * n + offset, n)
                    to = ((chip * s.C + source) * 3 + kind) * n
                    out[to : to + n, :] = both[pl.ds(at, n), :]


def add_chips(s, kept, got, share, *outs):
    outs = outs[: s.chips]
    size = s.C * 3 * s.eight
    chip = lax.div(lax.axis_index("row"), 2)
    for mask in range(s.chips):
        rows = pl.ds(pl.multiple_of(jnp.bitwise_xor(chip, mask) * size, size), size)
        outs[mask][...] = kept[rows, :] + got[rows, :]


def add_cols(s, *refs):
    terms, outs, total = refs[: s.chips], refs[s.chips : -1], refs[-1]
    size = 3 * s.eight
    col = lax.axis_index("col")
    value = terms[0][...]
    for term in terms[1:]:
        value = value + term[...]
    total[...] = value
    for step in range(s.C):
        rows = pl.ds(pl.multiple_of(lax.rem(col + step, s.C) * size, size), size)
        outs[step][...] = total[rows, :]


def plus(s, *refs):
    count = len(refs) // 3
    for one, two, out in zip(refs[:count], refs[count : 2 * count], refs[2 * count :]):
        out[...] = one[...] + two[...]


def add_all(s, *refs):
    terms, out = refs[:-1], refs[-1]
    value = terms[0][...]
    for term in terms[1:]:
        value = value + term[...]
    out[...] = value


def finish(s, pd, cd, base, *refs):
    parts, outs = refs[: s.R], refs[s.R :]
    row = lax.axis_index("row")
    n = s.eight
    starts = (pd, base, cd)
    for mask in range(s.R):
        source = jnp.bitwise_xor(row, mask)
        at = lax.rem(source, 2) * (s.ws // 2) + lax.div(source, 2) * n
        rows = pl.ds(pl.multiple_of(at, n), n)
        for kind in range(3):
            outs[kind][rows, :] = starts[kind][rows, :] + parts[mask][kind * n : (kind + 1) * n, :]


def rows_out(s, blocks, psize, csize, th, tl, *refs):
    terms, (parent, child) = refs[:-2], refs[-2:]
    value = terms[0][...]
    for term in terms[1:]:
        value = value + term[...]
    first = lax.axis_index("col") * s.share
    index = lax.broadcasted_iota(jnp.int32, (s.share, s.W), 0) + first
    plive = jnp.concatenate([index < psize[k] for k in range(s.slots)], axis=0)
    clive = jnp.concatenate([index < csize[k] for k in range(s.slots)], axis=0)
    y = jnp.where(plive, -value[:, : s.W], 0.0)
    carried = dot3(split(y), (th[...], tl[...]), NN)
    z = jnp.where(clive, -(value[:, s.W :] + carried), 0.0)
    parent[...] = jnp.zeros_like(parent)
    child[...] = jnp.zeros_like(child)
    for slot in range(s.slots):

        @pl.when(blocks[slot] >= 0)
        def _():
            at = lax.div(blocks[slot], s.R) * s.share
            rows = pl.ds(pl.multiple_of(at, s.share), s.share)
            parent[rows, :] = y[slot * s.share : (slot + 1) * s.share, :]
            child[rows, :] = z[slot * s.share : (slot + 1) * s.share, :]


def column_perm(s, turn):
    half, pairs = s.C // 2, []
    for q in range(s.Q):
        for at in range(s.C):
            for c in range(s.C):
                to = (turn ^ c // half) * half + at % half
                row = q * s.C + at // half * half + c % half
                pairs.append(((q * s.C + at) * s.C + c, row * s.C + to))
    return pairs


def fast_body(
    cached_inverse,
    parent_panel,
    parent_blocks,
    parent_sizes,
    parent_diagonal,
    child_panel,
    child_top,
    child_blocks,
    child_sizes,
    child_diagonal,
):
    R, C = lax.axis_size("row"), lax.axis_size("col")
    B = cached_inverse.shape[2]
    s = Shape(R, C, parent_panel, cached_inverse, parent_diagonal.shape[1])
    W, ws, live = s.W, s.ws, s.live
    cached = cached_inverse.reshape(-1, B)
    bind = lambda kernel: functools.partial(kernel, s)
    numbers = pltpu.SMEM((s.slots,), jnp.int32)
    by_slot = (s.slots, ws, B)
    with jax.named_scope("pack"):
        kept, sent, mine, parents, children = call(
            bind(pack),
            anywhere(
                parent_blocks,
                parent_sizes,
                child_sizes,
                jnp.transpose(parent_panel, (1, 0, 2)),
                jnp.transpose(child_panel, (1, 0, 2)),
                child_top,
            ),
            [(s.block, B)] * 2 + [(s.payload, B)] + [(s.part, B)] * 2,
            [numbers] * 3
            + [pltpu.VMEM(by_slot, f32)] * 2
            + [pltpu.VMEM((ws, W), f32), pltpu.SemaphoreType.DMA((6,))],
            limit=None,
        )
    with jax.named_scope("to_column"):
        got = exchange(sent, C // 2, R)
        (kept,) = call(
            bind(keep), anywhere(kept), [(s.block, B)], [pltpu.SemaphoreType.DMA((1,))]
        )
        pieces = call(
            bind(route),
            anywhere(kept, got),
            [(s.block, B)] * 2,
            [pltpu.SemaphoreType.DMA((2,))],
        )
        pieces = [
            lax.ppermute(pieces[turn], ("row", "col"), column_perm(s, turn)) for turn in range(2)
        ]
    with jax.named_scope("split_live"):
        sh, sl = call(
            bind(split_live),
            anywhere(cached, parent_blocks),
            [((live, s.CC * B), bf16)] * 2,
            [pltpu.VMEM((s.slots * B * s.CC, B), f32), numbers]
            + [pltpu.SemaphoreType.DMA((1 + s.slots,))],
        )
    with jax.named_scope("owned"):
        near = flip(mine, 1, C)
        held, mask = {0: mine}, C // 2
        while mask > 1:
            held.update({m ^ mask: flip(held[m], mask, C) for m in list(held)})
            mask //= 2
        owned = {0: mine, 1: near}
        for m in range(2, C, 2):
            (owned[m],) = call(bind(order), (), (), passed=(held[m],), ahead=8e9)
            owned[m + 1] = flip(owned[m], 1, C)
    with jax.named_scope("join"):
        own, owned[1], sh, sl = call(
            bind(join), vmem(*pieces), [(2 * s.block, B)], passed=(owned[1], sh, sl)
        )
    with jax.named_scope("panels"):
        panels = {0: own}
        for mask in range(2, R, 2):
            panels[mask] = exchange(own, mask, R)
        for mask in range(0, R, 2):
            panels[mask + 1] = exchange(panels[mask], 1, R)
    with jax.named_scope("shares_of"):
        pair = lambda rows, cols: [((rows, cols), bf16)] * 2
        *shares, gh, gl, th, tl, ih, il, base, extra = call(
            bind(shares_of),
            vmem(parent_diagonal, sh, sl, *[panels[m] for m in range(R)]),
            [(s.slots * s.share, 2 * W)] * C
            + pair(live, 2 * W)
            + pair(W, W)
            + pair(W, W)
            + [(ws, W), (W, W)],
            [pltpu.VMEM((s.CC + 1, 2 * W, B), bf16)] * 2
            + [pltpu.VMEM((live, 2 * W), f32), pltpu.VMEM((W, W), f32)],
        )
    with jax.named_scope("products"):
        lh, ll, gh, gl = call(
            bind(collect),
            vmem(*[owned[m] for m in range(C)]),
            pair(2 * W, live),
            ahead=3e9,
            passed=(gh, gl),
        )
        stays, send = call(
            bind(products),
            vmem(gh, gl, th, tl, ih, il, extra, lh, ll),
            [(3 * W // 2, W)] * 2,
            [pltpu.VMEM((3 * W, W), f32)],
        )
    with jax.named_scope("sum_core"):
        got = exchange(send, 1, R)
    with jax.named_scope("sum_shares"):
        arrived, mask = [shares[0]], 1
        while mask < C:
            far = list(range(3 * mask, C, 2 * mask))
            if far:
                come = [flip(shares[m], mask, C) for m in far]
                to = [m ^ mask for m in far]
                added = call(
                    bind(plus),
                    vmem(*[shares[m] for m in to], *come),
                    [shares[0].shape] * len(far),
                    ahead=6e9,
                )
                for m, value in zip(to, added):
                    shares[m] = value
            mask *= 2
    with jax.named_scope("sum_chips"):
        *mine, shares[2] = call(
            bind(add_chips),
            vmem(stays, got),
            [(C * 3 * s.eight, W)] * s.chips,
            passed=(shares[2],),
        )
        mine = [mine[0]] + [exchange(mine[m], 2 * m, R) for m in range(1, s.chips)]

    with jax.named_scope("sum_shares"):
        mask = 1
        while mask < C:
            arrived.append(flip(shares[mask], mask, C))
            mask *= 2
    with jax.named_scope("sum_cols"):
        scr = [pltpu.VMEM((C * 3 * s.eight, W), f32)]
        cols = call(bind(add_cols), vmem(*mine), [(3 * s.eight, W)] * C, scr)
        cols = [cols[0]] + [shift(cols[k], k, C) for k in range(1, C)]
    with jax.named_scope("spread"):
        (done,) = call(bind(add_all), vmem(*cols), [(3 * s.eight, W)])
        parts = {0: done}
        for mask in range(2, R, 2):
            parts[mask] = exchange(done, mask, R)
    with jax.named_scope("rows_out"):
        parent_rows, child_rows = call(
            bind(rows_out),
            smem(parent_blocks, parent_sizes, child_sizes) + vmem(th, tl, *arrived),
            [(s.RC * s.share, W)] * 2,
        )
    with jax.named_scope("spread"):
        parts[R - 2], parent_rows, child_rows = call(
            bind(order), (), (), passed=(parts[R - 2], parent_rows, child_rows)
        )
        for mask in range(0, R, 2):
            parts[mask + 1] = exchange(parts[mask], 1, R)
    with jax.named_scope("finish"):
        parent_diag, child_upper, child_diag = call(
            bind(finish),
            vmem(parent_diagonal, child_diagonal, base, *[parts[m] for m in range(R)]),
            [(ws, W)] * 3,
        )
    shape = (s.RC, 1, s.share, W)
    return (
        parent_rows.reshape(shape),
        parent_diag,
        child_rows.reshape(shape),
        child_upper,
        child_diag,
    )


highest = lax.Precision.HIGHEST


def from_root(value, axis, source):
    kept = jnp.where(lax.axis_index(axis) == source, value, 0).astype(value.dtype)
    return lax.psum(kept, axis)


def live_rows(sizes, block_rows):
    return (jnp.arange(block_rows, dtype=jnp.int32)[None, :] < sizes[:, None]).astype(jnp.float32)


def own_share(widened, blocks, row_live, row_index, row_total, col_index, row_share, local_rows):
    wanted = jnp.arange(local_rows, dtype=jnp.int32) * row_total + row_index
    onehot = (blocks[None, :] == wanted[:, None]).astype(jnp.float32)
    sliced = lax.dynamic_slice_in_dim(widened, col_index * row_share, row_share, 2)
    own_rows = jnp.einsum("rk,wkb->rbw", onehot, sliced, precision=highest)
    live_part = lax.dynamic_slice_in_dim(row_live, col_index * row_share, row_share, 1)
    row_alive = jnp.einsum("rk,kb->rb", onehot, live_part, precision=highest)
    return (own_rows, row_alive)


def add_columns(column_dense, widened, blocks, col_index, col_total):
    wanted = jnp.arange(column_dense.shape[0], dtype=jnp.int32) * col_total + col_index
    onehot = (blocks[None, :] == wanted[:, None]).astype(jnp.float32)
    return column_dense + jnp.einsum("ck,wky->cwy", onehot, widened, precision=highest)


def column_panel(widened, blocks, col_index, col_total, row_total, col_blocks):
    column_dense = jnp.zeros((col_blocks, widened.shape[0], widened.shape[2]), jnp.float32)
    for repeat in range(row_total // col_total):
        sender = col_index + repeat * col_total
        heard_panel, heard_blocks = (
            from_root(widened, "row", sender),
            from_root(blocks, "row", sender),
        )
        column_dense = add_columns(column_dense, heard_panel, heard_blocks, col_index, col_total)
    return column_dense


def child_panels(
    child_panel, child_top, child_live, child_blocks, col_index, col_total, row_total, col_blocks
):
    wide_child, top_full = (
        lax.all_gather(child_panel, "col", axis=0, tiled=True),
        lax.all_gather(child_top, "col", axis=0, tiled=True),
    )
    child_full = wide_child * child_live[None, :, :]
    child_dense = column_panel(
        child_full, child_blocks, col_index, col_total, row_total, col_blocks
    )
    return (child_full, child_dense, top_full)


def apply_inverse(cached, column_dense):
    summed = lax.psum_scatter(
        jnp.einsum(
            "rxcy,cwy->xrw",
            cached,
            column_dense,
            precision=highest,
            preferred_element_type=jnp.float32,
        ),
        "col",
        scatter_dimension=0,
        tiled=True,
    )
    return jnp.transpose(summed, (1, 0, 2))


def diagonal_sum(partial_rows, panel_width, col_share, col_index):
    entire = lax.psum(partial_rows(0, panel_width), ("row", "col"))
    return lax.dynamic_slice_in_dim(entire, col_index * col_share, col_share, 0)


def body(
    cached_inverse,
    parent_panel,
    parent_blocks,
    parent_sizes,
    parent_diagonal,
    child_panel,
    child_top,
    child_blocks,
    child_sizes,
    child_diagonal,
):
    row_total = lax.axis_size("row")
    col_total = lax.axis_size("col")
    row_index = lax.axis_index("row")
    col_index = lax.axis_index("col")
    local_rows = cached_inverse.shape[0]
    block_rows = cached_inverse.shape[2]
    col_blocks = cached_inverse.shape[3]
    cached = cached_inverse.reshape(local_rows, block_rows, col_blocks, block_rows)
    panel_width = parent_diagonal.shape[1]
    row_share = block_rows // col_total
    col_share = panel_width // col_total
    parent_live = live_rows(parent_sizes, block_rows)
    child_live = live_rows(child_sizes, block_rows)
    wide_parent = lax.all_gather(parent_panel, "col", axis=0, tiled=True)
    parent_full = wide_parent * parent_live[None, :, :]
    parent_dense = column_panel(
        parent_full, parent_blocks, col_index, col_total, row_total, col_blocks
    )
    child_full, child_dense, top_full = child_panels(
        child_panel,
        child_top,
        child_live,
        child_blocks,
        col_index,
        col_total,
        row_total,
        col_blocks,
    )
    parent_own, parent_alive = own_share(
        parent_full,
        parent_blocks,
        parent_live,
        row_index,
        row_total,
        col_index,
        row_share,
        local_rows,
    )
    both_local = apply_inverse(cached, jnp.concatenate([parent_dense, child_dense], axis=1))
    parent_local = -both_local[:, :, :panel_width] * parent_alive[:, :, None]
    child_own, child_alive = own_share(
        child_full, child_blocks, child_live, row_index, row_total, col_index, row_share, local_rows
    )
    carried = jnp.einsum("rbw,wv->rbv", parent_local, top_full, precision=highest)
    child_local = -(both_local[:, :, panel_width:] + carried) * child_alive[:, :, None]

    def stacked_terms(offset, amount):
        first_part = jnp.einsum("rbw,rbv->wv", parent_own, parent_local, precision=highest)
        second_part = jnp.einsum("rbw,rbv->wv", parent_local, child_own, precision=highest)
        third_part = jnp.einsum("rbc,rbv->cv", child_own, child_local, precision=highest)
        return jnp.concatenate([first_part, second_part, third_part], axis=1)

    stacked_sum = diagonal_sum(stacked_terms, panel_width, col_share, col_index)
    parent_diag = parent_diagonal - stacked_sum[:, :panel_width]
    child_upper = -(
        jnp.dot(parent_diag, top_full, precision=highest, preferred_element_type=jnp.float32)
        + stacked_sum[:, panel_width : 2 * panel_width]
    )
    upper_whole = lax.all_gather(child_upper, "col", axis=0, tiled=True)
    top_columns = lax.dynamic_slice_in_dim(top_full, col_index * col_share, col_share, 1)
    child_diag = (
        child_diagonal
        - jnp.dot(top_columns.T, upper_whole, precision=highest, preferred_element_type=jnp.float32)
        - stacked_sum[:, 2 * panel_width :]
    )
    return (
        parent_local[:, None, :, :],
        parent_diag,
        child_local[:, None, :, :],
        child_upper,
        child_diag,
    )


def fits(rows, cols, panel, cached, width):
    s = Shape(rows, cols, panel, cached, width)
    return (
        rows & (rows - 1) == 0
        and cols & (cols - 1) == 0
        and rows % cols == 0
        and cols > 2
        and s.Q == 2
        and width == 2 * s.B
        and s.ws % 16 == 0
        and s.share % 16 == 0
        and s.ws % rows == 0
        and s.eight % 8 == 0
        and width % s.B == 0
    )


def chosen(*args):
    sizes = lax.axis_size("row"), lax.axis_size("col")
    ok = fits(*sizes, args[1], args[0], args[4].shape[1])
    return (fast_body if ok else body)(*args)


def solution(mesh):
    in_specs = (
        P(None, "row", None, None, "col", None),
        P("col", "row", None),
        P("row"),
        P("row"),
        P("col", None),
        P("col", "row", None),
        P("col", None),
        P("row"),
        P("row"),
        P("col", None),
    )
    out_specs = (
        P(None, "row", "col", None),
        P("col", None),
        P(None, "row", "col", None),
        P("col", None),
        P("col", None),
    )
    return jax.shard_map(chosen, mesh=mesh, in_specs=in_specs, out_specs=out_specs, check_vma=False)
```

```python
import functools

import jax
import jax.numpy as jnp
from jax import lax
from jax.experimental import pallas as pl
from jax.experimental.pallas import tpu as pltpu
from jax.sharding import PartitionSpec as P

f32 = jnp.float32
bf16 = jnp.bfloat16

NN = (((1,), (0,)), ((), ()))
NT = (((1,), (1,)), ((), ()))
TN = (((0,), (0,)), ((), ()))


def split(value):
    high = value.astype(bf16)
    return high, (value - high.astype(f32)).astype(bf16)


def dot3(left, right, dims):
    (lh, ll), (rh, rl) = left, right
    on_left, on_right = dims[0][0][0], dims[0][1][0]
    return lax.dot_general(
        jnp.concatenate([lh, lh, ll], axis=on_left),
        jnp.concatenate([rh, rl, rh], axis=on_right),
        dims,
        preferred_element_type=f32,
    )


def call(kernel, inputs, outs, scratch=(), ahead=0, limit=40, passed=()):
    alias = {len(inputs) + i: len(outs) + i for i in range(len(passed))}
    spaces = [pltpu.VMEM] * len(outs) + [pl.ANY] * len(passed)
    inputs = list(inputs) + [(pl.ANY, a) for a in passed]
    outs = list(outs) + [(a.shape, a.dtype) for a in passed]
    arrays = [a for _, a in inputs]
    shapes = [jax.ShapeDtypeStruct(*(o if isinstance(o[0], tuple) else (o, f32))) for o in outs]
    nbytes = sum(a.size * a.dtype.itemsize for a in arrays + shapes)
    return pl.pallas_call(
        kernel,
        out_shape=shapes,
        in_specs=[pl.BlockSpec(memory_space=space) for space, _ in inputs],
        out_specs=[pl.BlockSpec(memory_space=space) for space in spaces],
        scratch_shapes=list(scratch),
        input_output_aliases=alias,
        compiler_params=pltpu.CompilerParams(vmem_limit_bytes=limit and limit * 1024 * 1024),
        cost_estimate=pl.CostEstimate(flops=int(ahead), bytes_accessed=nbytes, transcendentals=0),
    )(*arrays)


def vmem(*arrays):
    return [(pltpu.VMEM, a) for a in arrays]


def smem(*arrays):
    return [(pltpu.SMEM, a) for a in arrays]


def anywhere(*arrays):
    return [(pl.ANY, a) for a in arrays]


def fetch(sources, targets, sems):
    copies = [
        pltpu.make_async_copy(a, b, sems.at[i]) for i, (a, b) in enumerate(zip(sources, targets))
    ]
    for copy in copies:
        copy.start()
    return copies


def exchange(value, mask, row_total):
    return lax.ppermute(value, "row", [(i, i ^ mask) for i in range(row_total)])


def shift(value, step, col_total):
    return lax.ppermute(value, "col", [(i, (i + step) % col_total) for i in range(col_total)])


def flip(value, mask, col_total):
    return lax.ppermute(value, "col", [(i, i ^ mask) for i in range(col_total)])


class Shape:
    def __init__(self, rows, cols, panel, cached, width):
        self.R, self.C = rows, cols
        self.ws, self.slots, self.B = panel.shape
        self.W = width
        self.RC = cached.shape[0]
        self.CC = cached.shape[3]
        self.Q = rows // cols
        self.payload = self.slots * 2 * self.ws
        self.share = self.B // cols
        self.chips = rows // 2
        self.eight = self.ws // rows
        self.live = self.slots * self.B
        self.parts = self.W // self.B
        self.part = self.payload // 2
        self.block = self.part + self.ws // 2 + 8


def pack(s, *refs):
    sources, (kept, sent, mine, *targets, sems) = refs[:6], refs[6:]
    for copy in fetch(sources, targets, sems):
        copy.wait()
    blocks, psize, csize, parent, child, top = targets
    row = lax.axis_index("row")
    side = lax.div(lax.rem(row, s.C), s.C // 2)
    lane = lax.broadcasted_iota(jnp.int32, (s.ws, s.B), 1)
    for slot in range(s.slots):
        base = slot * 2 * s.ws
        for which, panel, sizes in ((0, parent, psize), (1, child, csize)):
            live = jnp.where(lane < sizes[slot], panel[slot], 0.0)
            mine[base + which * s.ws : base + (which + 1) * s.ws, :] = live
    columns = pl.ds(pl.multiple_of(lax.div(row, s.C) * s.B, s.B), s.B)
    row8 = lax.broadcasted_iota(jnp.int32, (8, s.B), 0)
    ids = jnp.zeros((8, s.B), f32)
    for slot in range(s.slots):
        ids = jnp.where(row8 == slot, blocks[slot].astype(f32), ids)
    quarter = s.ws // 2
    for out, at in ((kept, side), (sent, 1 - side)):
        for slot in range(s.slots):
            rows = pl.ds(pl.multiple_of((slot * 2 + at) * s.ws, s.ws), s.ws)
            out[slot * s.ws : (slot + 1) * s.ws, :] = mine[rows, :]
        rows = pl.ds(pl.multiple_of(at * quarter, quarter), quarter)
        out[s.part : s.part + quarter, :] = top[rows, columns]
        out[s.part + quarter :, :] = ids


def keep(s, source, target, sems):
    for copy in fetch((source,), (target,), sems):
        copy.wait()


def route(s, kept, got, first, second, sems):
    side = lax.div(lax.rem(lax.axis_index("row"), s.C), s.C // 2)
    high = lax.div(lax.axis_index("col"), s.C // 2)
    own = high == side

    @pl.when(own)
    def _():
        for copy in fetch((kept, got), (first, second), sems):
            copy.wait()

    @pl.when(jnp.logical_not(own))
    def _():
        for copy in fetch((got, kept), (first, second), sems):
            copy.wait()


def join(s, first, second, *refs):
    out = refs[-1 - (len(refs) - 1) // 2]
    out[: s.block, :] = first[...]
    out[s.block :, :] = second[...]


def order(s, *refs):
    pass


def split_live(s, cached, blocks, after, high, low, held, numbers, sems):
    copy = pltpu.make_async_copy(blocks, numbers, sems.at[0])
    copy.start()
    copy.wait()
    size = s.B * s.CC
    copies = []
    for slot in range(s.slots):
        p = lax.div(jnp.maximum(numbers[slot], 0), s.R)
        source = cached.at[pl.ds(pl.multiple_of(p * size, size), size), :]
        copy = pltpu.make_async_copy(source, held.at[pl.ds(slot * size, size), :], sems.at[1 + slot])
        copy.start()
        copies.append(copy)
    for slot in range(s.slots):
        copies[slot].wait()
        rows = slice(slot * s.B, (slot + 1) * s.B)
        for m in range(s.CC):
            h, l = split(held[pl.ds(slot * size + m, s.B, stride=s.CC), :])
            high[rows, m * s.B : (m + 1) * s.B] = h
            low[rows, m * s.B : (m + 1) * s.B] = l


def shares_of(s, pd, sh, sl, *refs):
    panels, refs = refs[: s.R], refs[s.R :]
    shares, refs = refs[: s.C], refs[s.C :]
    gh, gl, th, tl, ih, il, base, extra, xh, xl, total, top = refs
    row, col = lax.axis_index("row"), lax.axis_index("col")
    places = []
    for owner in range(s.Q):
        for slot in range(s.slots):
            at = s.block - 8 + slot
            number = jnp.max(panels[owner * s.C][at : at + 1, :]).astype(jnp.int32)
            places.append(jnp.where(number < 0, s.CC, lax.div(jnp.maximum(number, 0), s.C)))
    for m in range(s.CC):
        taken = places[0] == m
        for place in places[1:]:
            taken = jnp.logical_or(taken, place == m)

        @pl.when(jnp.logical_not(taken))
        def _():
            xh[m] = jnp.zeros((2 * s.W, s.B), bf16)
            xl[m] = jnp.zeros((2 * s.W, s.B), bf16)

    high, quarter = lax.div(col, s.C // 2), s.ws // 2
    for mask in range(s.R):
        sender = jnp.bitwise_xor(row, mask)
        owner, inside = lax.div(sender, s.C), lax.rem(sender, s.C)
        side, low = lax.div(inside, s.C // 2), lax.rem(inside, s.C // 2)
        lanes = pl.ds(pl.multiple_of(owner * s.B, s.B), s.B)
        for turn in range(2):
            source = jnp.bitwise_xor(high, turn) * (s.C // 2) + low
            begin = turn * s.block
            rows = pl.ds(pl.multiple_of(side * s.W + source * s.ws, s.ws), s.ws)
            for slot in range(s.slots):
                place = places[mask // s.C * s.slots + slot]
                start = begin + slot * s.ws
                up, down = split(panels[mask][start : start + s.ws, :])
                xh[place, rows, :] = up
                xl[place, rows, :] = down
            start = begin + s.part
            rows = pl.ds(pl.multiple_of(source * s.ws + side * quarter, quarter), quarter)
            top[rows, lanes] = panels[mask][start : start + quarter, :]
    right = tuple(jnp.concatenate([x[i] for i in range(s.CC)], axis=1) for x in (xh, xl))
    total[...] = dot3((sh[...], sl[...]), right, NT)
    gh[...], gl[...] = split(total[...])
    for mask in range(s.C):
        target = jnp.bitwise_xor(col, mask)
        for slot in range(s.slots):
            start = pl.multiple_of(slot * s.B + target * s.share, s.share)
            rows = slice(slot * s.share, (slot + 1) * s.share)
            shares[mask][rows, :] = total[pl.ds(start, s.share), :]
    th[...], tl[...] = split(top[...])
    ih[...], il[...] = split(top[...].T)
    lead = dot3(split(pd[...]), (th[...], tl[...]), NN)
    base[...] = -lead
    own = top[pl.ds(pl.multiple_of(col * s.ws, s.ws), s.ws), :]
    extra[...] = dot3(split(own), split(lead * (1.0 / s.R)), TN)


def collect(s, *refs):
    owned, (lh, ll) = refs[: s.C], refs[s.C + 2 : s.C + 4]
    col = lax.axis_index("col")
    for mask in range(s.C):
        source = jnp.bitwise_xor(col, mask)
        for slot in range(s.slots):
            for which in range(2):
                start = (slot * 2 + which) * s.ws
                rows = pl.ds(pl.multiple_of(which * s.W + source * s.ws, s.ws), s.ws)
                lanes = slice(slot * s.B, (slot + 1) * s.B)
                lh[rows, lanes], ll[rows, lanes] = split(owned[mask][start : start + s.ws, :])


def products(s, gh, gl, th, tl, ih, il, extra, lh, ll, keep, send, both):
    core = lax.rem(lax.axis_index("row"), 2)
    W = s.W
    first = dot3((lh[...], ll[...]), (gh[:, :W], gl[:, :W]), NN)
    d = dot3((lh[W:, :], ll[W:, :]), (gh[:, W:], gl[:, W:]), NN)
    second = dot3(split(first), (th[...], tl[...]), NN)
    third = dot3((ih[...], il[...]), split(second[:W]), NN)
    both[0:W, :] = first[:W]
    both[W : 2 * W, :] = first[W:].T - second[:W]
    cross = second[W:]
    both[2 * W :, :] = d - cross - cross.T + third + extra[...]
    n = s.eight
    for out, swap in ((keep, 0), (send, 1)):
        offset = jnp.bitwise_xor(core, swap) * (s.ws // 2)
        for chip in range(s.chips):
            for source in range(s.C):
                for kind in range(3):
                    at = pl.multiple_of(kind * W + source * s.ws + chip * n + offset, n)
                    to = ((chip * s.C + source) * 3 + kind) * n
                    out[to : to + n, :] = both[pl.ds(at, n), :]


def add_chips(s, kept, got, share, *outs):
    outs = outs[: s.chips]
    size = s.C * 3 * s.eight
    chip = lax.div(lax.axis_index("row"), 2)
    for mask in range(s.chips):
        rows = pl.ds(pl.multiple_of(jnp.bitwise_xor(chip, mask) * size, size), size)
        outs[mask][...] = kept[rows, :] + got[rows, :]


def add_cols(s, *refs):
    terms, outs, total = refs[: s.chips], refs[s.chips : -1], refs[-1]
    size = 3 * s.eight
    col = lax.axis_index("col")
    value = terms[0][...]
    for term in terms[1:]:
        value = value + term[...]
    total[...] = value
    for step in range(s.C):
        rows = pl.ds(pl.multiple_of(lax.rem(col + step, s.C) * size, size), size)
        outs[step][...] = total[rows, :]


def plus(s, *refs):
    count = len(refs) // 3
    for one, two, out in zip(refs[:count], refs[count : 2 * count], refs[2 * count :]):
        out[...] = one[...] + two[...]


def add_all(s, *refs):
    terms, out = refs[:-1], refs[-1]
    value = terms[0][...]
    for term in terms[1:]:
        value = value + term[...]
    out[...] = value


def finish(s, pd, cd, base, *refs):
    parts, outs = refs[: s.R], refs[s.R :]
    row = lax.axis_index("row")
    n = s.eight
    starts = (pd, base, cd)
    for mask in range(s.R):
        source = jnp.bitwise_xor(row, mask)
        at = lax.rem(source, 2) * (s.ws // 2) + lax.div(source, 2) * n
        rows = pl.ds(pl.multiple_of(at, n), n)
        for kind in range(3):
            outs[kind][rows, :] = starts[kind][rows, :] + parts[mask][kind * n : (kind + 1) * n, :]


def rows_out(s, blocks, psize, csize, th, tl, *refs):
    terms, (parent, child) = refs[:-2], refs[-2:]
    value = terms[0][...]
    for term in terms[1:]:
        value = value + term[...]
    first = lax.axis_index("col") * s.share
    index = lax.broadcasted_iota(jnp.int32, (s.share, s.W), 0) + first
    plive = jnp.concatenate([index < psize[k] for k in range(s.slots)], axis=0)
    clive = jnp.concatenate([index < csize[k] for k in range(s.slots)], axis=0)
    y = jnp.where(plive, -value[:, : s.W], 0.0)
    carried = dot3(split(y), (th[...], tl[...]), NN)
    z = jnp.where(clive, -(value[:, s.W :] + carried), 0.0)
    parent[...] = jnp.zeros_like(parent)
    child[...] = jnp.zeros_like(child)
    for slot in range(s.slots):

        @pl.when(blocks[slot] >= 0)
        def _():
            at = lax.div(blocks[slot], s.R) * s.share
            rows = pl.ds(pl.multiple_of(at, s.share), s.share)
            parent[rows, :] = y[slot * s.share : (slot + 1) * s.share, :]
            child[rows, :] = z[slot * s.share : (slot + 1) * s.share, :]


def column_perm(s, turn):
    half, pairs = s.C // 2, []
    for q in range(s.Q):
        for at in range(s.C):
            for c in range(s.C):
                to = (turn ^ c // half) * half + at % half
                row = q * s.C + at // half * half + c % half
                pairs.append(((q * s.C + at) * s.C + c, row * s.C + to))
    return pairs


def fast_body(
    cached_inverse,
    parent_panel,
    parent_blocks,
    parent_sizes,
    parent_diagonal,
    child_panel,
    child_top,
    child_blocks,
    child_sizes,
    child_diagonal,
):
    R, C = lax.axis_size("row"), lax.axis_size("col")
    B = cached_inverse.shape[2]
    s = Shape(R, C, parent_panel, cached_inverse, parent_diagonal.shape[1])
    W, ws, live = s.W, s.ws, s.live
    cached = cached_inverse.reshape(-1, B)
    bind = lambda kernel: functools.partial(kernel, s)
    numbers = pltpu.SMEM((s.slots,), jnp.int32)
    by_slot = (s.slots, ws, B)
    with jax.named_scope("pack"):
        kept, sent, mine = call(
            bind(pack),
            anywhere(
                parent_blocks,
                parent_sizes,
                child_sizes,
                jnp.transpose(parent_panel, (1, 0, 2)),
                jnp.transpose(child_panel, (1, 0, 2)),
                child_top,
            ),
            [(s.block, B)] * 2 + [(s.payload, B)],
            [numbers] * 3
            + [pltpu.VMEM(by_slot, f32)] * 2
            + [pltpu.VMEM((ws, W), f32), pltpu.SemaphoreType.DMA((6,))],
            limit=None,
        )
    with jax.named_scope("to_column"):
        got = exchange(sent, C // 2, R)
        (kept,) = call(
            bind(keep), anywhere(kept), [(s.block, B)], [pltpu.SemaphoreType.DMA((1,))]
        )
        pieces = call(
            bind(route),
            anywhere(kept, got),
            [(s.block, B)] * 2,
            [pltpu.SemaphoreType.DMA((2,))],
        )
        pieces = [
            lax.ppermute(pieces[turn], ("row", "col"), column_perm(s, turn)) for turn in range(2)
        ]
    with jax.named_scope("owned"):
        near = flip(mine, 1, C)
        held, mask = {0: mine}, C // 2
        while mask > 1:
            held.update({m ^ mask: flip(held[m], mask, C) for m in list(held)})
            mask //= 2
        owned = {0: mine, 1: near}
        for m in range(2, C, 2):
            (owned[m],) = call(bind(order), (), (), passed=(held[m],), ahead=8e9)
            owned[m + 1] = flip(owned[m], 1, C)
    with jax.named_scope("join"):
        own, owned[1] = call(bind(join), vmem(*pieces), [(2 * s.block, B)], passed=(owned[1],))
    with jax.named_scope("split_live"):
        sh, sl = call(
            bind(split_live),
            anywhere(cached, parent_blocks, own),
            [((live, s.CC * B), bf16)] * 2,
            [pltpu.VMEM((s.slots * B * s.CC, B), f32), numbers]
            + [pltpu.SemaphoreType.DMA((1 + s.slots,))],
        )
    with jax.named_scope("panels"):
        panels = {0: own}
        for mask in range(2, R, 2):
            panels[mask] = exchange(own, mask, R)
        panels[C], sh, sl = call(bind(order), (), (), passed=(panels[C], sh, sl))
        for mask in range(0, R, 2):
            panels[mask + 1] = exchange(panels[mask], 1, R)
    with jax.named_scope("shares_of"):
        pair = lambda rows, cols: [((rows, cols), bf16)] * 2
        *shares, gh, gl, th, tl, ih, il, base, extra = call(
            bind(shares_of),
            vmem(parent_diagonal, sh, sl, *[panels[m] for m in range(R)]),
            [(s.slots * s.share, 2 * W)] * C
            + pair(live, 2 * W)
            + pair(W, W)
            + pair(W, W)
            + [(ws, W), (W, W)],
            [pltpu.VMEM((s.CC + 1, 2 * W, B), bf16)] * 2
            + [pltpu.VMEM((live, 2 * W), f32), pltpu.VMEM((W, W), f32)],
        )
    with jax.named_scope("products"):
        lh, ll, gh, gl = call(
            bind(collect),
            vmem(*[owned[m] for m in range(C)]),
            pair(2 * W, live),
            ahead=3e9,
            passed=(gh, gl),
        )
        stays, send = call(
            bind(products),
            vmem(gh, gl, th, tl, ih, il, extra, lh, ll),
            [(3 * W // 2, W)] * 2,
            [pltpu.VMEM((3 * W, W), f32)],
        )
    with jax.named_scope("sum_core"):
        got = exchange(send, 1, R)
    with jax.named_scope("sum_shares"):
        arrived, mask = [shares[0]], 1
        while mask < C:
            far = list(range(3 * mask, C, 2 * mask))
            if far:
                come = [flip(shares[m], mask, C) for m in far]
                to = [m ^ mask for m in far]
                added = call(
                    bind(plus),
                    vmem(*[shares[m] for m in to], *come),
                    [shares[0].shape] * len(far),
                    ahead=6e9,
                )
                for m, value in zip(to, added):
                    shares[m] = value
            mask *= 2
    with jax.named_scope("sum_chips"):
        *mine, shares[2] = call(
            bind(add_chips),
            vmem(stays, got),
            [(C * 3 * s.eight, W)] * s.chips,
            passed=(shares[2],),
        )
        mine = [mine[0]] + [exchange(mine[m], 2 * m, R) for m in range(1, s.chips)]

    with jax.named_scope("sum_shares"):
        mask = 1
        while mask < C:
            arrived.append(flip(shares[mask], mask, C))
            mask *= 2
    with jax.named_scope("sum_cols"):
        scr = [pltpu.VMEM((C * 3 * s.eight, W), f32)]
        cols = call(bind(add_cols), vmem(*mine), [(3 * s.eight, W)] * C, scr)
        cols = [cols[0]] + [shift(cols[k], k, C) for k in range(1, C)]
    with jax.named_scope("spread"):
        (done,) = call(bind(add_all), vmem(*cols), [(3 * s.eight, W)])
        parts = {0: done}
        for mask in range(2, R, 2):
            parts[mask] = exchange(done, mask, R)
    with jax.named_scope("rows_out"):
        parent_rows, child_rows = call(
            bind(rows_out),
            smem(parent_blocks, parent_sizes, child_sizes) + vmem(th, tl, *arrived),
            [(s.RC * s.share, W)] * 2,
        )
    with jax.named_scope("spread"):
        parts[R - 2], parent_rows, child_rows = call(
            bind(order), (), (), passed=(parts[R - 2], parent_rows, child_rows)
        )
        for mask in range(0, R, 2):
            parts[mask + 1] = exchange(parts[mask], 1, R)
    with jax.named_scope("finish"):
        parent_diag, child_upper, child_diag = call(
            bind(finish),
            vmem(parent_diagonal, child_diagonal, base, *[parts[m] for m in range(R)]),
            [(ws, W)] * 3,
        )
    shape = (s.RC, 1, s.share, W)
    return (
        parent_rows.reshape(shape),
        parent_diag,
        child_rows.reshape(shape),
        child_upper,
        child_diag,
    )


highest = lax.Precision.HIGHEST


def from_root(value, axis, source):
    kept = jnp.where(lax.axis_index(axis) == source, value, 0).astype(value.dtype)
    return lax.psum(kept, axis)


def live_rows(sizes, block_rows):
    return (jnp.arange(block_rows, dtype=jnp.int32)[None, :] < sizes[:, None]).astype(jnp.float32)


def own_share(widened, blocks, row_live, row_index, row_total, col_index, row_share, local_rows):
    wanted = jnp.arange(local_rows, dtype=jnp.int32) * row_total + row_index
    onehot = (blocks[None, :] == wanted[:, None]).astype(jnp.float32)
    sliced = lax.dynamic_slice_in_dim(widened, col_index * row_share, row_share, 2)
    own_rows = jnp.einsum("rk,wkb->rbw", onehot, sliced, precision=highest)
    live_part = lax.dynamic_slice_in_dim(row_live, col_index * row_share, row_share, 1)
    row_alive = jnp.einsum("rk,kb->rb", onehot, live_part, precision=highest)
    return (own_rows, row_alive)


def add_columns(column_dense, widened, blocks, col_index, col_total):
    wanted = jnp.arange(column_dense.shape[0], dtype=jnp.int32) * col_total + col_index
    onehot = (blocks[None, :] == wanted[:, None]).astype(jnp.float32)
    return column_dense + jnp.einsum("ck,wky->cwy", onehot, widened, precision=highest)


def column_panel(widened, blocks, col_index, col_total, row_total, col_blocks):
    column_dense = jnp.zeros((col_blocks, widened.shape[0], widened.shape[2]), jnp.float32)
    for repeat in range(row_total // col_total):
        sender = col_index + repeat * col_total
        heard_panel, heard_blocks = (
            from_root(widened, "row", sender),
            from_root(blocks, "row", sender),
        )
        column_dense = add_columns(column_dense, heard_panel, heard_blocks, col_index, col_total)
    return column_dense


def child_panels(
    child_panel, child_top, child_live, child_blocks, col_index, col_total, row_total, col_blocks
):
    wide_child, top_full = (
        lax.all_gather(child_panel, "col", axis=0, tiled=True),
        lax.all_gather(child_top, "col", axis=0, tiled=True),
    )
    child_full = wide_child * child_live[None, :, :]
    child_dense = column_panel(
        child_full, child_blocks, col_index, col_total, row_total, col_blocks
    )
    return (child_full, child_dense, top_full)


def apply_inverse(cached, column_dense):
    summed = lax.psum_scatter(
        jnp.einsum(
            "rxcy,cwy->xrw",
            cached,
            column_dense,
            precision=highest,
            preferred_element_type=jnp.float32,
        ),
        "col",
        scatter_dimension=0,
        tiled=True,
    )
    return jnp.transpose(summed, (1, 0, 2))


def diagonal_sum(partial_rows, panel_width, col_share, col_index):
    entire = lax.psum(partial_rows(0, panel_width), ("row", "col"))
    return lax.dynamic_slice_in_dim(entire, col_index * col_share, col_share, 0)


def body(
    cached_inverse,
    parent_panel,
    parent_blocks,
    parent_sizes,
    parent_diagonal,
    child_panel,
    child_top,
    child_blocks,
    child_sizes,
    child_diagonal,
):
    row_total = lax.axis_size("row")
    col_total = lax.axis_size("col")
    row_index = lax.axis_index("row")
    col_index = lax.axis_index("col")
    local_rows = cached_inverse.shape[0]
    block_rows = cached_inverse.shape[2]
    col_blocks = cached_inverse.shape[3]
    cached = cached_inverse.reshape(local_rows, block_rows, col_blocks, block_rows)
    panel_width = parent_diagonal.shape[1]
    row_share = block_rows // col_total
    col_share = panel_width // col_total
    parent_live = live_rows(parent_sizes, block_rows)
    child_live = live_rows(child_sizes, block_rows)
    wide_parent = lax.all_gather(parent_panel, "col", axis=0, tiled=True)
    parent_full = wide_parent * parent_live[None, :, :]
    parent_dense = column_panel(
        parent_full, parent_blocks, col_index, col_total, row_total, col_blocks
    )
    child_full, child_dense, top_full = child_panels(
        child_panel,
        child_top,
        child_live,
        child_blocks,
        col_index,
        col_total,
        row_total,
        col_blocks,
    )
    parent_own, parent_alive = own_share(
        parent_full,
        parent_blocks,
        parent_live,
        row_index,
        row_total,
        col_index,
        row_share,
        local_rows,
    )
    both_local = apply_inverse(cached, jnp.concatenate([parent_dense, child_dense], axis=1))
    parent_local = -both_local[:, :, :panel_width] * parent_alive[:, :, None]
    child_own, child_alive = own_share(
        child_full, child_blocks, child_live, row_index, row_total, col_index, row_share, local_rows
    )
    carried = jnp.einsum("rbw,wv->rbv", parent_local, top_full, precision=highest)
    child_local = -(both_local[:, :, panel_width:] + carried) * child_alive[:, :, None]

    def stacked_terms(offset, amount):
        first_part = jnp.einsum("rbw,rbv->wv", parent_own, parent_local, precision=highest)
        second_part = jnp.einsum("rbw,rbv->wv", parent_local, child_own, precision=highest)
        third_part = jnp.einsum("rbc,rbv->cv", child_own, child_local, precision=highest)
        return jnp.concatenate([first_part, second_part, third_part], axis=1)

    stacked_sum = diagonal_sum(stacked_terms, panel_width, col_share, col_index)
    parent_diag = parent_diagonal - stacked_sum[:, :panel_width]
    child_upper = -(
        jnp.dot(parent_diag, top_full, precision=highest, preferred_element_type=jnp.float32)
        + stacked_sum[:, panel_width : 2 * panel_width]
    )
    upper_whole = lax.all_gather(child_upper, "col", axis=0, tiled=True)
    top_columns = lax.dynamic_slice_in_dim(top_full, col_index * col_share, col_share, 1)
    child_diag = (
        child_diagonal
        - jnp.dot(top_columns.T, upper_whole, precision=highest, preferred_element_type=jnp.float32)
        - stacked_sum[:, 2 * panel_width :]
    )
    return (
        parent_local[:, None, :, :],
        parent_diag,
        child_local[:, None, :, :],
        child_upper,
        child_diag,
    )


def fits(rows, cols, panel, cached, width):
    s = Shape(rows, cols, panel, cached, width)
    return (
        rows & (rows - 1) == 0
        and cols & (cols - 1) == 0
        and rows % cols == 0
        and cols > 2
        and s.Q == 2
        and width == 2 * s.B
        and s.ws % 16 == 0
        and s.share % 16 == 0
        and s.ws % rows == 0
        and s.eight % 8 == 0
        and width % s.B == 0
    )


def chosen(*args):
    sizes = lax.axis_size("row"), lax.axis_size("col")
    ok = fits(*sizes, args[1], args[0], args[4].shape[1])
    return (fast_body if ok else body)(*args)


def solution(mesh):
    in_specs = (
        P(None, "row", None, None, "col", None),
        P("col", "row", None),
        P("row"),
        P("row"),
        P("col", None),
        P("col", "row", None),
        P("col", None),
        P("row"),
        P("row"),
        P("col", None),
    )
    out_specs = (
        P(None, "row", "col", None),
        P("col", None),
        P(None, "row", "col", None),
        P("col", None),
        P("col", None),
    )
    return jax.shard_map(chosen, mesh=mesh, in_specs=in_specs, out_specs=out_specs, check_vma=False)
```

```python
import functools

import jax
import jax.numpy as jnp
from jax import lax
from jax.experimental import pallas as pl
from jax.experimental.pallas import tpu as pltpu
from jax.sharding import PartitionSpec as P

f32 = jnp.float32
bf16 = jnp.bfloat16

NN = (((1,), (0,)), ((), ()))
NT = (((1,), (1,)), ((), ()))
TN = (((0,), (0,)), ((), ()))


def split(value):
    high = value.astype(bf16)
    return high, (value - high.astype(f32)).astype(bf16)


def dot3(left, right, dims):
    (lh, ll), (rh, rl) = left, right
    on_left, on_right = dims[0][0][0], dims[0][1][0]
    return lax.dot_general(
        jnp.concatenate([lh, lh, ll], axis=on_left),
        jnp.concatenate([rh, rl, rh], axis=on_right),
        dims,
        preferred_element_type=f32,
    )


def call(kernel, inputs, outs, scratch=(), ahead=0, limit=40, passed=()):
    alias = {len(inputs) + i: len(outs) + i for i in range(len(passed))}
    spaces = [pltpu.VMEM] * len(outs) + [pl.ANY] * len(passed)
    inputs = list(inputs) + [(pl.ANY, a) for a in passed]
    outs = list(outs) + [(a.shape, a.dtype) for a in passed]
    arrays = [a for _, a in inputs]
    shapes = [jax.ShapeDtypeStruct(*(o if isinstance(o[0], tuple) else (o, f32))) for o in outs]
    nbytes = sum(a.size * a.dtype.itemsize for a in arrays + shapes)
    return pl.pallas_call(
        kernel,
        out_shape=shapes,
        in_specs=[pl.BlockSpec(memory_space=space) for space, _ in inputs],
        out_specs=[pl.BlockSpec(memory_space=space) for space in spaces],
        scratch_shapes=list(scratch),
        input_output_aliases=alias,
        compiler_params=pltpu.CompilerParams(vmem_limit_bytes=limit and limit * 1024 * 1024),
        cost_estimate=pl.CostEstimate(flops=int(ahead), bytes_accessed=nbytes, transcendentals=0),
    )(*arrays)


def vmem(*arrays):
    return [(pltpu.VMEM, a) for a in arrays]


def smem(*arrays):
    return [(pltpu.SMEM, a) for a in arrays]


def anywhere(*arrays):
    return [(pl.ANY, a) for a in arrays]


def fetch(sources, targets, sems):
    copies = [
        pltpu.make_async_copy(a, b, sems.at[i]) for i, (a, b) in enumerate(zip(sources, targets))
    ]
    for copy in copies:
        copy.start()
    return copies


def exchange(value, mask, row_total):
    return lax.ppermute(value, "row", [(i, i ^ mask) for i in range(row_total)])


def shift(value, step, col_total):
    return lax.ppermute(value, "col", [(i, (i + step) % col_total) for i in range(col_total)])


def flip(value, mask, col_total):
    return lax.ppermute(value, "col", [(i, i ^ mask) for i in range(col_total)])


class Shape:
    def __init__(self, rows, cols, panel, cached, width):
        self.R, self.C = rows, cols
        self.ws, self.slots, self.B = panel.shape
        self.W = width
        self.RC = cached.shape[0]
        self.CC = cached.shape[3]
        self.Q = rows // cols
        self.payload = self.slots * 2 * self.ws
        self.share = self.B // cols
        self.chips = rows // 2
        self.eight = self.ws // rows
        self.live = self.slots * self.B
        self.parts = self.W // self.B
        self.part = self.payload // 2
        self.block = self.part + self.ws // 2 + 8


def pack(s, *refs):
    sources, (kept, sent, mine, *targets, sems) = refs[:6], refs[6:]
    for copy in fetch(sources, targets, sems):
        copy.wait()
    blocks, psize, csize, parent, child, top = targets
    row = lax.axis_index("row")
    side = lax.div(lax.rem(row, s.C), s.C // 2)
    lane = lax.broadcasted_iota(jnp.int32, (s.ws, s.B), 1)
    for slot in range(s.slots):
        base = slot * 2 * s.ws
        for which, panel, sizes in ((0, parent, psize), (1, child, csize)):
            live = jnp.where(lane < sizes[slot], panel[slot], 0.0)
            mine[base + which * s.ws : base + (which + 1) * s.ws, :] = live
    columns = pl.ds(pl.multiple_of(lax.div(row, s.C) * s.B, s.B), s.B)
    row8 = lax.broadcasted_iota(jnp.int32, (8, s.B), 0)
    ids = jnp.zeros((8, s.B), f32)
    for slot in range(s.slots):
        ids = jnp.where(row8 == slot, blocks[slot].astype(f32), ids)
    quarter = s.ws // 2
    for out, at in ((kept, side), (sent, 1 - side)):
        for slot in range(s.slots):
            rows = pl.ds(pl.multiple_of((slot * 2 + at) * s.ws, s.ws), s.ws)
            out[slot * s.ws : (slot + 1) * s.ws, :] = mine[rows, :]
        rows = pl.ds(pl.multiple_of(at * quarter, quarter), quarter)
        out[s.part : s.part + quarter, :] = top[rows, columns]
        out[s.part + quarter :, :] = ids


def keep(s, source, target, sems):
    for copy in fetch((source,), (target,), sems):
        copy.wait()


def route(s, kept, got, first, second, sems):
    side = lax.div(lax.rem(lax.axis_index("row"), s.C), s.C // 2)
    high = lax.div(lax.axis_index("col"), s.C // 2)
    own = high == side

    @pl.when(own)
    def _():
        for copy in fetch((kept, got), (first, second), sems):
            copy.wait()

    @pl.when(jnp.logical_not(own))
    def _():
        for copy in fetch((got, kept), (first, second), sems):
            copy.wait()


def join(s, first, second, *refs):
    out = refs[-1 - (len(refs) - 1) // 2]
    out[: s.block, :] = first[...]
    out[s.block :, :] = second[...]


def order(s, *refs):
    pass


def split_live(s, cached, blocks, after, high, low, held, numbers, sems):
    copy = pltpu.make_async_copy(blocks, numbers, sems.at[0])
    copy.start()
    copy.wait()
    size = s.B * s.CC
    copies = []
    for slot in range(s.slots):
        p = lax.div(jnp.maximum(numbers[slot], 0), s.R)
        source = cached.at[pl.ds(pl.multiple_of(p * size, size), size), :]
        copy = pltpu.make_async_copy(source, held.at[pl.ds(slot * size, size), :], sems.at[1 + slot])
        copy.start()
        copies.append(copy)
    for slot in range(s.slots):
        copies[slot].wait()
        rows = slice(slot * s.B, (slot + 1) * s.B)
        for m in range(s.CC):
            h, l = split(held[pl.ds(slot * size + m, s.B, stride=s.CC), :])
            high[rows, m * s.B : (m + 1) * s.B] = h
            low[rows, m * s.B : (m + 1) * s.B] = l


def shares_of(s, pd, sh, sl, *refs):
    panels, refs = refs[: s.R], refs[s.R :]
    shares, refs = refs[: s.C], refs[s.C :]
    gh, gl, th, tl, ih, il, base, extra, xh, xl, total, top = refs
    row, col = lax.axis_index("row"), lax.axis_index("col")
    places = []
    for owner in range(s.Q):
        for slot in range(s.slots):
            at = s.block - 8 + slot
            number = jnp.max(panels[owner * s.C][at : at + 1, :]).astype(jnp.int32)
            places.append(jnp.where(number < 0, s.CC, lax.div(jnp.maximum(number, 0), s.C)))
    for m in range(s.CC):
        taken = places[0] == m
        for place in places[1:]:
            taken = jnp.logical_or(taken, place == m)

        @pl.when(jnp.logical_not(taken))
        def _():
            xh[m] = jnp.zeros((2 * s.W, s.B), bf16)
            xl[m] = jnp.zeros((2 * s.W, s.B), bf16)

    high, quarter = lax.div(col, s.C // 2), s.ws // 2
    for mask in range(s.R):
        sender = jnp.bitwise_xor(row, mask)
        owner, inside = lax.div(sender, s.C), lax.rem(sender, s.C)
        side, low = lax.div(inside, s.C // 2), lax.rem(inside, s.C // 2)
        lanes = pl.ds(pl.multiple_of(owner * s.B, s.B), s.B)
        for turn in range(2):
            source = jnp.bitwise_xor(high, turn) * (s.C // 2) + low
            begin = turn * s.block
            rows = pl.ds(pl.multiple_of(side * s.W + source * s.ws, s.ws), s.ws)
            for slot in range(s.slots):
                place = places[mask // s.C * s.slots + slot]
                start = begin + slot * s.ws
                up, down = split(panels[mask][start : start + s.ws, :])
                xh[place, rows, :] = up
                xl[place, rows, :] = down
            start = begin + s.part
            rows = pl.ds(pl.multiple_of(source * s.ws + side * quarter, quarter), quarter)
            top[rows, lanes] = panels[mask][start : start + quarter, :]
    right = tuple(jnp.concatenate([x[i] for i in range(s.CC)], axis=1) for x in (xh, xl))
    total[...] = dot3((sh[...], sl[...]), right, NT)
    gh[...], gl[...] = split(total[...])
    for mask in range(s.C):
        target = jnp.bitwise_xor(col, mask)
        for slot in range(s.slots):
            start = pl.multiple_of(slot * s.B + target * s.share, s.share)
            rows = slice(slot * s.share, (slot + 1) * s.share)
            shares[mask][rows, :] = total[pl.ds(start, s.share), :]
    th[...], tl[...] = split(top[...])
    ih[...], il[...] = split(top[...].T)
    lead = dot3(split(pd[...]), (th[...], tl[...]), NN)
    base[...] = -lead
    own = top[pl.ds(pl.multiple_of(col * s.ws, s.ws), s.ws), :]
    extra[...] = dot3(split(own), split(lead * (1.0 / s.R)), TN)


def collect(s, *refs):
    owned, (lh, ll) = refs[: s.C], refs[s.C + 2 : s.C + 4]
    col = lax.axis_index("col")
    for mask in range(s.C):
        source = jnp.bitwise_xor(col, mask)
        for slot in range(s.slots):
            for which in range(2):
                start = (slot * 2 + which) * s.ws
                rows = pl.ds(pl.multiple_of(which * s.W + source * s.ws, s.ws), s.ws)
                lanes = slice(slot * s.B, (slot + 1) * s.B)
                lh[rows, lanes], ll[rows, lanes] = split(owned[mask][start : start + s.ws, :])


def products(s, gh, gl, th, tl, ih, il, extra, lh, ll, keep, send, both):
    core = lax.rem(lax.axis_index("row"), 2)
    W = s.W
    first = dot3((lh[...], ll[...]), (gh[:, :W], gl[:, :W]), NN)
    d = dot3((lh[W:, :], ll[W:, :]), (gh[:, W:], gl[:, W:]), NN)
    second = dot3(split(first), (th[...], tl[...]), NN)
    third = dot3((ih[...], il[...]), split(second[:W]), NN)
    both[0:W, :] = first[:W]
    both[W : 2 * W, :] = first[W:].T - second[:W]
    cross = second[W:]
    both[2 * W :, :] = d - cross - cross.T + third + extra[...]
    n = s.eight
    for out, swap in ((keep, 0), (send, 1)):
        offset = jnp.bitwise_xor(core, swap) * (s.ws // 2)
        for chip in range(s.chips):
            for source in range(s.C):
                for kind in range(3):
                    at = pl.multiple_of(kind * W + source * s.ws + chip * n + offset, n)
                    to = ((chip * s.C + source) * 3 + kind) * n
                    out[to : to + n, :] = both[pl.ds(at, n), :]


def add_chips(s, kept, got, share, *outs):
    outs = outs[: s.chips]
    size = s.C * 3 * s.eight
    chip = lax.div(lax.axis_index("row"), 2)
    for mask in range(s.chips):
        rows = pl.ds(pl.multiple_of(jnp.bitwise_xor(chip, mask) * size, size), size)
        outs[mask][...] = kept[rows, :] + got[rows, :]


def add_cols(s, *refs):
    terms, outs, total = refs[: s.chips], refs[s.chips : -1], refs[-1]
    size = 3 * s.eight
    col = lax.axis_index("col")
    value = terms[0][...]
    for term in terms[1:]:
        value = value + term[...]
    total[...] = value
    for step in range(s.C):
        rows = pl.ds(pl.multiple_of(lax.rem(col + step, s.C) * size, size), size)
        outs[step][...] = total[rows, :]


def plus(s, *refs):
    count = len(refs) // 3
    for one, two, out in zip(refs[:count], refs[count : 2 * count], refs[2 * count :]):
        out[...] = one[...] + two[...]


def add_all(s, *refs):
    terms, out = refs[: s.C], refs[s.C + 2]
    value = terms[0][...]
    for term in terms[1:]:
        value = value + term[...]
    out[...] = value


def finish(s, pd, cd, base, *refs):
    parts, outs = refs[: s.R], refs[s.R :]
    row = lax.axis_index("row")
    n = s.eight
    starts = (pd, base, cd)
    for mask in range(s.R):
        source = jnp.bitwise_xor(row, mask)
        at = lax.rem(source, 2) * (s.ws // 2) + lax.div(source, 2) * n
        rows = pl.ds(pl.multiple_of(at, n), n)
        for kind in range(3):
            outs[kind][rows, :] = starts[kind][rows, :] + parts[mask][kind * n : (kind + 1) * n, :]


def rows_out(s, blocks, psize, csize, th, tl, *refs):
    terms, (parent, child) = refs[:-2], refs[-2:]
    value = terms[0][...]
    for term in terms[1:]:
        value = value + term[...]
    first = lax.axis_index("col") * s.share
    index = lax.broadcasted_iota(jnp.int32, (s.share, s.W), 0) + first
    plive = jnp.concatenate([index < psize[k] for k in range(s.slots)], axis=0)
    clive = jnp.concatenate([index < csize[k] for k in range(s.slots)], axis=0)
    y = jnp.where(plive, -value[:, : s.W], 0.0)
    carried = dot3(split(y), (th[...], tl[...]), NN)
    z = jnp.where(clive, -(value[:, s.W :] + carried), 0.0)
    parent[...] = jnp.zeros_like(parent)
    child[...] = jnp.zeros_like(child)
    for slot in range(s.slots):

        @pl.when(blocks[slot] >= 0)
        def _():
            at = lax.div(blocks[slot], s.R) * s.share
            rows = pl.ds(pl.multiple_of(at, s.share), s.share)
            parent[rows, :] = y[slot * s.share : (slot + 1) * s.share, :]
            child[rows, :] = z[slot * s.share : (slot + 1) * s.share, :]


def column_perm(s, turn):
    half, pairs = s.C // 2, []
    for q in range(s.Q):
        for at in range(s.C):
            for c in range(s.C):
                to = (turn ^ c // half) * half + at % half
                row = q * s.C + at // half * half + c % half
                pairs.append(((q * s.C + at) * s.C + c, row * s.C + to))
    return pairs


def fast_body(
    cached_inverse,
    parent_panel,
    parent_blocks,
    parent_sizes,
    parent_diagonal,
    child_panel,
    child_top,
    child_blocks,
    child_sizes,
    child_diagonal,
):
    R, C = lax.axis_size("row"), lax.axis_size("col")
    B = cached_inverse.shape[2]
    s = Shape(R, C, parent_panel, cached_inverse, parent_diagonal.shape[1])
    W, ws, live = s.W, s.ws, s.live
    cached = cached_inverse.reshape(-1, B)
    bind = lambda kernel: functools.partial(kernel, s)
    numbers = pltpu.SMEM((s.slots,), jnp.int32)
    by_slot = (s.slots, ws, B)
    with jax.named_scope("pack"):
        kept, sent, mine = call(
            bind(pack),
            anywhere(
                parent_blocks,
                parent_sizes,
                child_sizes,
                jnp.transpose(parent_panel, (1, 0, 2)),
                jnp.transpose(child_panel, (1, 0, 2)),
                child_top,
            ),
            [(s.block, B)] * 2 + [(s.payload, B)],
            [numbers] * 3
            + [pltpu.VMEM(by_slot, f32)] * 2
            + [pltpu.VMEM((ws, W), f32), pltpu.SemaphoreType.DMA((6,))],
            limit=None,
        )
    with jax.named_scope("to_column"):
        got = exchange(sent, C // 2, R)
        (kept,) = call(
            bind(keep), anywhere(kept), [(s.block, B)], [pltpu.SemaphoreType.DMA((1,))]
        )
        pieces = call(
            bind(route),
            anywhere(kept, got),
            [(s.block, B)] * 2,
            [pltpu.SemaphoreType.DMA((2,))],
        )
        pieces = [
            lax.ppermute(pieces[turn], ("row", "col"), column_perm(s, turn)) for turn in range(2)
        ]
    with jax.named_scope("owned"):
        near = flip(mine, 1, C)
        held, mask = {0: mine}, C // 2
        while mask > 1:
            held.update({m ^ mask: flip(held[m], mask, C) for m in list(held)})
            mask //= 2
        owned = {0: mine, 1: near}
        for m in range(2, C, 2):
            (owned[m],) = call(bind(order), (), (), passed=(held[m],), ahead=8e9)
            owned[m + 1] = flip(owned[m], 1, C)
    with jax.named_scope("join"):
        own, owned[1] = call(bind(join), vmem(*pieces), [(2 * s.block, B)], passed=(owned[1],))
    with jax.named_scope("split_live"):
        sh, sl = call(
            bind(split_live),
            anywhere(cached, parent_blocks, own),
            [((live, s.CC * B), bf16)] * 2,
            [pltpu.VMEM((s.slots * B * s.CC, B), f32), numbers]
            + [pltpu.SemaphoreType.DMA((1 + s.slots,))],
        )
    with jax.named_scope("panels"):
        panels = {0: own}
        for mask in range(2, R, 2):
            panels[mask] = exchange(own, mask, R)
        panels[C], sh, sl = call(bind(order), (), (), passed=(panels[C], sh, sl))
        for mask in range(0, R, 2):
            panels[mask + 1] = exchange(panels[mask], 1, R)
    with jax.named_scope("shares_of"):
        pair = lambda rows, cols: [((rows, cols), bf16)] * 2
        *shares, gh, gl, th, tl, ih, il, base, extra = call(
            bind(shares_of),
            vmem(parent_diagonal, sh, sl, *[panels[m] for m in range(R)]),
            [(s.slots * s.share, 2 * W)] * C
            + pair(live, 2 * W)
            + pair(W, W)
            + pair(W, W)
            + [(ws, W), (W, W)],
            [pltpu.VMEM((s.CC + 1, 2 * W, B), bf16)] * 2
            + [pltpu.VMEM((live, 2 * W), f32), pltpu.VMEM((W, W), f32)],
        )
    with jax.named_scope("products"):
        lh, ll, gh, gl = call(
            bind(collect),
            vmem(*[owned[m] for m in range(C)]),
            pair(2 * W, live),
            ahead=3e9,
            passed=(gh, gl),
        )
        stays, send = call(
            bind(products),
            vmem(gh, gl, th, tl, ih, il, extra, lh, ll),
            [(3 * W // 2, W)] * 2,
            [pltpu.VMEM((3 * W, W), f32)],
        )
    with jax.named_scope("sum_core"):
        got = exchange(send, 1, R)
    with jax.named_scope("sum_shares"):
        arrived, mask = [shares[0]], 1
        while mask < C:
            far = list(range(3 * mask, C, 2 * mask))
            if far:
                come = [flip(shares[m], mask, C) for m in far]
                to = [m ^ mask for m in far]
                added = call(
                    bind(plus),
                    vmem(*[shares[m] for m in to], *come),
                    [shares[0].shape] * len(far),
                    ahead=6e9,
                )
                for m, value in zip(to, added):
                    shares[m] = value
            mask *= 2
    with jax.named_scope("sum_chips"):
        *mine, shares[2] = call(
            bind(add_chips),
            vmem(stays, got),
            [(C * 3 * s.eight, W)] * s.chips,
            passed=(shares[2],),
        )
        mine = [mine[0]] + [exchange(mine[m], 2 * m, R) for m in range(s.chips - 1, 0, -1)]

    with jax.named_scope("sum_shares"):
        mask = 1
        while mask < C:
            arrived.append(flip(shares[mask], mask, C))
            mask *= 2
    with jax.named_scope("sum_cols"):
        scr = [pltpu.VMEM((C * 3 * s.eight, W), f32)]
        cols = call(bind(add_cols), vmem(*mine), [(3 * s.eight, W)] * C, scr)
        cols = [cols[0]] + [shift(cols[k], k, C) for k in range(1, C)]
    with jax.named_scope("rows_out"):
        parent_rows, child_rows = call(
            bind(rows_out),
            smem(parent_blocks, parent_sizes, child_sizes) + vmem(th, tl, *arrived),
            [(s.RC * s.share, W)] * 2,
        )
    with jax.named_scope("spread"):
        done, parent_rows, child_rows = call(
            bind(add_all), vmem(*cols), [(3 * s.eight, W)], passed=(parent_rows, child_rows)
        )
        parts = {0: done}
        for mask in range(R - 2, 0, -2):
            parts[mask] = exchange(done, mask, R)
    with jax.named_scope("spread"):
        for mask in range(0, R, 2):
            parts[mask + 1] = exchange(parts[mask], 1, R)
    with jax.named_scope("finish"):
        parent_diag, child_upper, child_diag = call(
            bind(finish),
            vmem(parent_diagonal, child_diagonal, base, *[parts[m] for m in range(R)]),
            [(ws, W)] * 3,
        )
    shape = (s.RC, 1, s.share, W)
    return (
        parent_rows.reshape(shape),
        parent_diag,
        child_rows.reshape(shape),
        child_upper,
        child_diag,
    )


highest = lax.Precision.HIGHEST


def from_root(value, axis, source):
    kept = jnp.where(lax.axis_index(axis) == source, value, 0).astype(value.dtype)
    return lax.psum(kept, axis)


def live_rows(sizes, block_rows):
    return (jnp.arange(block_rows, dtype=jnp.int32)[None, :] < sizes[:, None]).astype(jnp.float32)


def own_share(widened, blocks, row_live, row_index, row_total, col_index, row_share, local_rows):
    wanted = jnp.arange(local_rows, dtype=jnp.int32) * row_total + row_index
    onehot = (blocks[None, :] == wanted[:, None]).astype(jnp.float32)
    sliced = lax.dynamic_slice_in_dim(widened, col_index * row_share, row_share, 2)
    own_rows = jnp.einsum("rk,wkb->rbw", onehot, sliced, precision=highest)
    live_part = lax.dynamic_slice_in_dim(row_live, col_index * row_share, row_share, 1)
    row_alive = jnp.einsum("rk,kb->rb", onehot, live_part, precision=highest)
    return (own_rows, row_alive)


def add_columns(column_dense, widened, blocks, col_index, col_total):
    wanted = jnp.arange(column_dense.shape[0], dtype=jnp.int32) * col_total + col_index
    onehot = (blocks[None, :] == wanted[:, None]).astype(jnp.float32)
    return column_dense + jnp.einsum("ck,wky->cwy", onehot, widened, precision=highest)


def column_panel(widened, blocks, col_index, col_total, row_total, col_blocks):
    column_dense = jnp.zeros((col_blocks, widened.shape[0], widened.shape[2]), jnp.float32)
    for repeat in range(row_total // col_total):
        sender = col_index + repeat * col_total
        heard_panel, heard_blocks = (
            from_root(widened, "row", sender),
            from_root(blocks, "row", sender),
        )
        column_dense = add_columns(column_dense, heard_panel, heard_blocks, col_index, col_total)
    return column_dense


def child_panels(
    child_panel, child_top, child_live, child_blocks, col_index, col_total, row_total, col_blocks
):
    wide_child, top_full = (
        lax.all_gather(child_panel, "col", axis=0, tiled=True),
        lax.all_gather(child_top, "col", axis=0, tiled=True),
    )
    child_full = wide_child * child_live[None, :, :]
    child_dense = column_panel(
        child_full, child_blocks, col_index, col_total, row_total, col_blocks
    )
    return (child_full, child_dense, top_full)


def apply_inverse(cached, column_dense):
    summed = lax.psum_scatter(
        jnp.einsum(
            "rxcy,cwy->xrw",
            cached,
            column_dense,
            precision=highest,
            preferred_element_type=jnp.float32,
        ),
        "col",
        scatter_dimension=0,
        tiled=True,
    )
    return jnp.transpose(summed, (1, 0, 2))


def diagonal_sum(partial_rows, panel_width, col_share, col_index):
    entire = lax.psum(partial_rows(0, panel_width), ("row", "col"))
    return lax.dynamic_slice_in_dim(entire, col_index * col_share, col_share, 0)


def body(
    cached_inverse,
    parent_panel,
    parent_blocks,
    parent_sizes,
    parent_diagonal,
    child_panel,
    child_top,
    child_blocks,
    child_sizes,
    child_diagonal,
):
    row_total = lax.axis_size("row")
    col_total = lax.axis_size("col")
    row_index = lax.axis_index("row")
    col_index = lax.axis_index("col")
    local_rows = cached_inverse.shape[0]
    block_rows = cached_inverse.shape[2]
    col_blocks = cached_inverse.shape[3]
    cached = cached_inverse.reshape(local_rows, block_rows, col_blocks, block_rows)
    panel_width = parent_diagonal.shape[1]
    row_share = block_rows // col_total
    col_share = panel_width // col_total
    parent_live = live_rows(parent_sizes, block_rows)
    child_live = live_rows(child_sizes, block_rows)
    wide_parent = lax.all_gather(parent_panel, "col", axis=0, tiled=True)
    parent_full = wide_parent * parent_live[None, :, :]
    parent_dense = column_panel(
        parent_full, parent_blocks, col_index, col_total, row_total, col_blocks
    )
    child_full, child_dense, top_full = child_panels(
        child_panel,
        child_top,
        child_live,
        child_blocks,
        col_index,
        col_total,
        row_total,
        col_blocks,
    )
    parent_own, parent_alive = own_share(
        parent_full,
        parent_blocks,
        parent_live,
        row_index,
        row_total,
        col_index,
        row_share,
        local_rows,
    )
    both_local = apply_inverse(cached, jnp.concatenate([parent_dense, child_dense], axis=1))
    parent_local = -both_local[:, :, :panel_width] * parent_alive[:, :, None]
    child_own, child_alive = own_share(
        child_full, child_blocks, child_live, row_index, row_total, col_index, row_share, local_rows
    )
    carried = jnp.einsum("rbw,wv->rbv", parent_local, top_full, precision=highest)
    child_local = -(both_local[:, :, panel_width:] + carried) * child_alive[:, :, None]

    def stacked_terms(offset, amount):
        first_part = jnp.einsum("rbw,rbv->wv", parent_own, parent_local, precision=highest)
        second_part = jnp.einsum("rbw,rbv->wv", parent_local, child_own, precision=highest)
        third_part = jnp.einsum("rbc,rbv->cv", child_own, child_local, precision=highest)
        return jnp.concatenate([first_part, second_part, third_part], axis=1)

    stacked_sum = diagonal_sum(stacked_terms, panel_width, col_share, col_index)
    parent_diag = parent_diagonal - stacked_sum[:, :panel_width]
    child_upper = -(
        jnp.dot(parent_diag, top_full, precision=highest, preferred_element_type=jnp.float32)
        + stacked_sum[:, panel_width : 2 * panel_width]
    )
    upper_whole = lax.all_gather(child_upper, "col", axis=0, tiled=True)
    top_columns = lax.dynamic_slice_in_dim(top_full, col_index * col_share, col_share, 1)
    child_diag = (
        child_diagonal
        - jnp.dot(top_columns.T, upper_whole, precision=highest, preferred_element_type=jnp.float32)
        - stacked_sum[:, 2 * panel_width :]
    )
    return (
        parent_local[:, None, :, :],
        parent_diag,
        child_local[:, None, :, :],
        child_upper,
        child_diag,
    )


def fits(rows, cols, panel, cached, width):
    s = Shape(rows, cols, panel, cached, width)
    return (
        rows & (rows - 1) == 0
        and cols & (cols - 1) == 0
        and rows % cols == 0
        and cols > 2
        and s.Q == 2
        and width == 2 * s.B
        and s.ws % 16 == 0
        and s.share % 16 == 0
        and s.ws % rows == 0
        and s.eight % 8 == 0
        and width % s.B == 0
    )


def chosen(*args):
    sizes = lax.axis_size("row"), lax.axis_size("col")
    ok = fits(*sizes, args[1], args[0], args[4].shape[1])
    return (fast_body if ok else body)(*args)


def solution(mesh):
    in_specs = (
        P(None, "row", None, None, "col", None),
        P("col", "row", None),
        P("row"),
        P("row"),
        P("col", None),
        P("col", "row", None),
        P("col", None),
        P("row"),
        P("row"),
        P("col", None),
    )
    out_specs = (
        P(None, "row", "col", None),
        P("col", None),
        P(None, "row", "col", None),
        P("col", None),
        P("col", None),
    )
    return jax.shard_map(chosen, mesh=mesh, in_specs=in_specs, out_specs=out_specs, check_vma=False)
```

```python
import functools

import jax
import jax.numpy as jnp
from jax import lax
from jax.experimental import pallas as pl
from jax.experimental.pallas import tpu as pltpu
from jax.sharding import PartitionSpec as P

f32 = jnp.float32
bf16 = jnp.bfloat16

NN = (((1,), (0,)), ((), ()))
NT = (((1,), (1,)), ((), ()))
TN = (((0,), (0,)), ((), ()))


def split(value):
    high = value.astype(bf16)
    return high, (value - high.astype(f32)).astype(bf16)


def dot3(left, right, dims):
    (lh, ll), (rh, rl) = left, right
    on_left, on_right = dims[0][0][0], dims[0][1][0]
    return lax.dot_general(
        jnp.concatenate([lh, lh, ll], axis=on_left),
        jnp.concatenate([rh, rl, rh], axis=on_right),
        dims,
        preferred_element_type=f32,
    )


def call(kernel, inputs, outs, scratch=(), ahead=0, limit=40, passed=()):
    alias = {len(inputs) + i: len(outs) + i for i in range(len(passed))}
    spaces = [pltpu.VMEM] * len(outs) + [pl.ANY] * len(passed)
    inputs = list(inputs) + [(pl.ANY, a) for a in passed]
    outs = list(outs) + [(a.shape, a.dtype) for a in passed]
    arrays = [a for _, a in inputs]
    shapes = [jax.ShapeDtypeStruct(*(o if isinstance(o[0], tuple) else (o, f32))) for o in outs]
    nbytes = sum(a.size * a.dtype.itemsize for a in arrays + shapes)
    return pl.pallas_call(
        kernel,
        out_shape=shapes,
        in_specs=[pl.BlockSpec(memory_space=space) for space, _ in inputs],
        out_specs=[pl.BlockSpec(memory_space=space) for space in spaces],
        scratch_shapes=list(scratch),
        input_output_aliases=alias,
        compiler_params=pltpu.CompilerParams(vmem_limit_bytes=limit and limit * 1024 * 1024),
        cost_estimate=pl.CostEstimate(flops=int(ahead), bytes_accessed=nbytes, transcendentals=0),
    )(*arrays)


def vmem(*arrays):
    return [(pltpu.VMEM, a) for a in arrays]


def smem(*arrays):
    return [(pltpu.SMEM, a) for a in arrays]


def anywhere(*arrays):
    return [(pl.ANY, a) for a in arrays]


def fetch(sources, targets, sems):
    copies = [
        pltpu.make_async_copy(a, b, sems.at[i]) for i, (a, b) in enumerate(zip(sources, targets))
    ]
    for copy in copies:
        copy.start()
    return copies


def exchange(value, mask, row_total):
    return lax.ppermute(value, "row", [(i, i ^ mask) for i in range(row_total)])


def shift(value, step, col_total):
    return lax.ppermute(value, "col", [(i, (i + step) % col_total) for i in range(col_total)])


def flip(value, mask, col_total):
    return lax.ppermute(value, "col", [(i, i ^ mask) for i in range(col_total)])


class Shape:
    def __init__(self, rows, cols, panel, cached, width):
        self.R, self.C = rows, cols
        self.ws, self.slots, self.B = panel.shape
        self.W = width
        self.RC = cached.shape[0]
        self.CC = cached.shape[3]
        self.Q = rows // cols
        self.payload = self.slots * 2 * self.ws
        self.share = self.B // cols
        self.chips = rows // 2
        self.eight = self.ws // rows
        self.live = self.slots * self.B
        self.parts = self.W // self.B
        self.part = self.payload // 2
        self.block = self.part + self.ws // 2 + 8


def pack(s, *refs):
    sources, (kept, sent, mine, *targets, sems) = refs[:6], refs[6:]
    for copy in fetch(sources, targets, sems):
        copy.wait()
    blocks, psize, csize, parent, child, top = targets
    row = lax.axis_index("row")
    side = lax.div(lax.rem(row, s.C), s.C // 2)
    lane = lax.broadcasted_iota(jnp.int32, (s.ws, s.B), 1)
    for slot in range(s.slots):
        base = slot * 2 * s.ws
        for which, panel, sizes in ((0, parent, psize), (1, child, csize)):
            live = jnp.where(lane < sizes[slot], panel[slot], 0.0)
            mine[base + which * s.ws : base + (which + 1) * s.ws, :] = live
    columns = pl.ds(pl.multiple_of(lax.div(row, s.C) * s.B, s.B), s.B)
    row8 = lax.broadcasted_iota(jnp.int32, (8, s.B), 0)
    ids = jnp.zeros((8, s.B), f32)
    for slot in range(s.slots):
        ids = jnp.where(row8 == slot, blocks[slot].astype(f32), ids)
    quarter = s.ws // 2
    for out, at in ((kept, side), (sent, 1 - side)):
        for slot in range(s.slots):
            rows = pl.ds(pl.multiple_of((slot * 2 + at) * s.ws, s.ws), s.ws)
            out[slot * s.ws : (slot + 1) * s.ws, :] = mine[rows, :]
        rows = pl.ds(pl.multiple_of(at * quarter, quarter), quarter)
        out[s.part : s.part + quarter, :] = top[rows, columns]
        out[s.part + quarter :, :] = ids


def keep(s, source, target, sems):
    for copy in fetch((source,), (target,), sems):
        copy.wait()


def route(s, kept, got, first, second, sems):
    side = lax.div(lax.rem(lax.axis_index("row"), s.C), s.C // 2)
    high = lax.div(lax.axis_index("col"), s.C // 2)
    own = high == side

    @pl.when(own)
    def _():
        for copy in fetch((kept, got), (first, second), sems):
            copy.wait()

    @pl.when(jnp.logical_not(own))
    def _():
        for copy in fetch((got, kept), (first, second), sems):
            copy.wait()


def join(s, first, second, *refs):
    out = refs[-1 - (len(refs) - 1) // 2]
    out[: s.block, :] = first[...]
    out[s.block :, :] = second[...]


def order(s, *refs):
    pass


def split_live(s, cached, blocks, after, high, low, held, numbers, sems):
    copy = pltpu.make_async_copy(blocks, numbers, sems.at[0])
    copy.start()
    copy.wait()
    size = s.B * s.CC
    copies = []
    for slot in range(s.slots):
        p = lax.div(jnp.maximum(numbers[slot], 0), s.R)
        source = cached.at[pl.ds(pl.multiple_of(p * size, size), size), :]
        copy = pltpu.make_async_copy(source, held.at[pl.ds(slot * size, size), :], sems.at[1 + slot])
        copy.start()
        copies.append(copy)
    for slot in range(s.slots):
        copies[slot].wait()
        rows = slice(slot * s.B, (slot + 1) * s.B)
        for m in range(s.CC):
            h, l = split(held[pl.ds(slot * size + m, s.B, stride=s.CC), :])
            high[rows, m * s.B : (m + 1) * s.B] = h
            low[rows, m * s.B : (m + 1) * s.B] = l


def shares_of(s, sh, sl, *refs):
    panels, refs = refs[: s.R], refs[s.R :]
    shares, refs = refs[: s.C], refs[s.C :]
    gh, gl, top, xh, xl, total = refs
    row, col = lax.axis_index("row"), lax.axis_index("col")
    places = []
    for owner in range(s.Q):
        for slot in range(s.slots):
            at = s.block - 8 + slot
            number = jnp.max(panels[owner * s.C][at : at + 1, :]).astype(jnp.int32)
            places.append(jnp.where(number < 0, s.CC, lax.div(jnp.maximum(number, 0), s.C)))
    for m in range(s.CC):
        taken = places[0] == m
        for place in places[1:]:
            taken = jnp.logical_or(taken, place == m)

        @pl.when(jnp.logical_not(taken))
        def _():
            xh[m] = jnp.zeros((2 * s.W, s.B), bf16)
            xl[m] = jnp.zeros((2 * s.W, s.B), bf16)

    high, quarter = lax.div(col, s.C // 2), s.ws // 2
    for mask in range(s.R):
        sender = jnp.bitwise_xor(row, mask)
        owner, inside = lax.div(sender, s.C), lax.rem(sender, s.C)
        side, low = lax.div(inside, s.C // 2), lax.rem(inside, s.C // 2)
        lanes = pl.ds(pl.multiple_of(owner * s.B, s.B), s.B)
        for turn in range(2):
            source = jnp.bitwise_xor(high, turn) * (s.C // 2) + low
            begin = turn * s.block
            rows = pl.ds(pl.multiple_of(side * s.W + source * s.ws, s.ws), s.ws)
            for slot in range(s.slots):
                place = places[mask // s.C * s.slots + slot]
                start = begin + slot * s.ws
                up, down = split(panels[mask][start : start + s.ws, :])
                xh[place, rows, :] = up
                xl[place, rows, :] = down
            start = begin + s.part
            rows = pl.ds(pl.multiple_of(source * s.ws + side * quarter, quarter), quarter)
            top[rows, lanes] = panels[mask][start : start + quarter, :]
    right = tuple(jnp.concatenate([x[i] for i in range(s.CC)], axis=1) for x in (xh, xl))
    total[...] = dot3((sh[...], sl[...]), right, NT)
    gh[...], gl[...] = split(total[...])
    for mask in range(s.C):
        target = jnp.bitwise_xor(col, mask)
        for slot in range(s.slots):
            start = pl.multiple_of(slot * s.B + target * s.share, s.share)
            rows = slice(slot * s.share, (slot + 1) * s.share)
            shares[mask][rows, :] = total[pl.ds(start, s.share), :]


def tops(s, pd, top, th, tl, ih, il, base, extra):
    col = lax.axis_index("col")
    th[...], tl[...] = split(top[...])
    ih[...], il[...] = split(top[...].T)
    lead = dot3(split(pd[...]), (th[...], tl[...]), NN)
    base[...] = -lead
    own = top[pl.ds(pl.multiple_of(col * s.ws, s.ws), s.ws), :]
    extra[...] = dot3(split(own), split(lead * (1.0 / s.R)), TN)


def collect(s, *refs):
    owned, (lh, ll) = refs[: s.C], refs[s.C + 2 : s.C + 4]
    col = lax.axis_index("col")
    for mask in range(s.C):
        source = jnp.bitwise_xor(col, mask)
        for slot in range(s.slots):
            for which in range(2):
                start = (slot * 2 + which) * s.ws
                rows = pl.ds(pl.multiple_of(which * s.W + source * s.ws, s.ws), s.ws)
                lanes = slice(slot * s.B, (slot + 1) * s.B)
                lh[rows, lanes], ll[rows, lanes] = split(owned[mask][start : start + s.ws, :])


def products(s, gh, gl, th, tl, ih, il, extra, lh, ll, keep, send, both):
    core = lax.rem(lax.axis_index("row"), 2)
    W = s.W
    first = dot3((lh[...], ll[...]), (gh[:, :W], gl[:, :W]), NN)
    d = dot3((lh[W:, :], ll[W:, :]), (gh[:, W:], gl[:, W:]), NN)
    second = dot3(split(first), (th[...], tl[...]), NN)
    third = dot3((ih[...], il[...]), split(second[:W]), NN)
    both[0:W, :] = first[:W]
    both[W : 2 * W, :] = first[W:].T - second[:W]
    cross = second[W:]
    both[2 * W :, :] = d - cross - cross.T + third + extra[...]
    n = s.eight
    for out, swap in ((keep, 0), (send, 1)):
        offset = jnp.bitwise_xor(core, swap) * (s.ws // 2)
        for chip in range(s.chips):
            for source in range(s.C):
                for kind in range(3):
                    at = pl.multiple_of(kind * W + source * s.ws + chip * n + offset, n)
                    to = ((chip * s.C + source) * 3 + kind) * n
                    out[to : to + n, :] = both[pl.ds(at, n), :]


def add_chips(s, kept, got, share, *outs):
    outs = outs[: s.chips]
    size = s.C * 3 * s.eight
    chip = lax.div(lax.axis_index("row"), 2)
    for mask in range(s.chips):
        rows = pl.ds(pl.multiple_of(jnp.bitwise_xor(chip, mask) * size, size), size)
        outs[mask][...] = kept[rows, :] + got[rows, :]


def add_cols(s, *refs):
    terms, outs, total = refs[: s.chips], refs[s.chips : -1], refs[-1]
    size = 3 * s.eight
    col = lax.axis_index("col")
    value = terms[0][...]
    for term in terms[1:]:
        value = value + term[...]
    total[...] = value
    for step in range(s.C):
        rows = pl.ds(pl.multiple_of(lax.rem(col + step, s.C) * size, size), size)
        outs[step][...] = total[rows, :]


def plus(s, *refs):
    count = len(refs) // 3
    for one, two, out in zip(refs[:count], refs[count : 2 * count], refs[2 * count :]):
        out[...] = one[...] + two[...]


def add_all(s, *refs):
    terms, out = refs[: s.C], refs[s.C + 2]
    value = terms[0][...]
    for term in terms[1:]:
        value = value + term[...]
    out[...] = value


def finish(s, pd, cd, base, *refs):
    parts, outs = refs[: s.R], refs[s.R :]
    row = lax.axis_index("row")
    n = s.eight
    starts = (pd, base, cd)
    for mask in range(s.R):
        source = jnp.bitwise_xor(row, mask)
        at = lax.rem(source, 2) * (s.ws // 2) + lax.div(source, 2) * n
        rows = pl.ds(pl.multiple_of(at, n), n)
        for kind in range(3):
            outs[kind][rows, :] = starts[kind][rows, :] + parts[mask][kind * n : (kind + 1) * n, :]


def rows_out(s, blocks, psize, csize, th, tl, *refs):
    terms, (parent, child) = refs[:-2], refs[-2:]
    value = terms[0][...]
    for term in terms[1:]:
        value = value + term[...]
    first = lax.axis_index("col") * s.share
    index = lax.broadcasted_iota(jnp.int32, (s.share, s.W), 0) + first
    plive = jnp.concatenate([index < psize[k] for k in range(s.slots)], axis=0)
    clive = jnp.concatenate([index < csize[k] for k in range(s.slots)], axis=0)
    y = jnp.where(plive, -value[:, : s.W], 0.0)
    carried = dot3(split(y), (th[...], tl[...]), NN)
    z = jnp.where(clive, -(value[:, s.W :] + carried), 0.0)
    parent[...] = jnp.zeros_like(parent)
    child[...] = jnp.zeros_like(child)
    for slot in range(s.slots):

        @pl.when(blocks[slot] >= 0)
        def _():
            at = lax.div(blocks[slot], s.R) * s.share
            rows = pl.ds(pl.multiple_of(at, s.share), s.share)
            parent[rows, :] = y[slot * s.share : (slot + 1) * s.share, :]
            child[rows, :] = z[slot * s.share : (slot + 1) * s.share, :]


def column_perm(s, turn):
    half, pairs = s.C // 2, []
    for q in range(s.Q):
        for at in range(s.C):
            for c in range(s.C):
                to = (turn ^ c // half) * half + at % half
                row = q * s.C + at // half * half + c % half
                pairs.append(((q * s.C + at) * s.C + c, row * s.C + to))
    return pairs


def fast_body(
    cached_inverse,
    parent_panel,
    parent_blocks,
    parent_sizes,
    parent_diagonal,
    child_panel,
    child_top,
    child_blocks,
    child_sizes,
    child_diagonal,
):
    R, C = lax.axis_size("row"), lax.axis_size("col")
    B = cached_inverse.shape[2]
    s = Shape(R, C, parent_panel, cached_inverse, parent_diagonal.shape[1])
    W, ws, live = s.W, s.ws, s.live
    cached = cached_inverse.reshape(-1, B)
    bind = lambda kernel: functools.partial(kernel, s)
    numbers = pltpu.SMEM((s.slots,), jnp.int32)
    by_slot = (s.slots, ws, B)
    with jax.named_scope("pack"):
        kept, sent, mine = call(
            bind(pack),
            anywhere(
                parent_blocks,
                parent_sizes,
                child_sizes,
                jnp.transpose(parent_panel, (1, 0, 2)),
                jnp.transpose(child_panel, (1, 0, 2)),
                child_top,
            ),
            [(s.block, B)] * 2 + [(s.payload, B)],
            [numbers] * 3
            + [pltpu.VMEM(by_slot, f32)] * 2
            + [pltpu.VMEM((ws, W), f32), pltpu.SemaphoreType.DMA((6,))],
            limit=None,
        )
    with jax.named_scope("to_column"):
        got = exchange(sent, C // 2, R)
        (kept,) = call(
            bind(keep), anywhere(kept), [(s.block, B)], [pltpu.SemaphoreType.DMA((1,))]
        )
        pieces = call(
            bind(route),
            anywhere(kept, got),
            [(s.block, B)] * 2,
            [pltpu.SemaphoreType.DMA((2,))],
        )
        pieces = [
            lax.ppermute(pieces[turn], ("row", "col"), column_perm(s, turn)) for turn in range(2)
        ]
    with jax.named_scope("owned"):
        near = flip(mine, 1, C)
        held, mask = {0: mine}, C // 2
        while mask > 1:
            held.update({m ^ mask: flip(held[m], mask, C) for m in list(held)})
            mask //= 2
        owned = {0: mine, 1: near}
        for m in range(2, C, 2):
            (owned[m],) = call(bind(order), (), (), passed=(held[m],), ahead=8e9)
            owned[m + 1] = flip(owned[m], 1, C)
    with jax.named_scope("join"):
        own, owned[1] = call(bind(join), vmem(*pieces), [(2 * s.block, B)], passed=(owned[1],))
    with jax.named_scope("split_live"):
        sh, sl = call(
            bind(split_live),
            anywhere(cached, parent_blocks, own),
            [((live, s.CC * B), bf16)] * 2,
            [pltpu.VMEM((s.slots * B * s.CC, B), f32), numbers]
            + [pltpu.SemaphoreType.DMA((1 + s.slots,))],
        )
    with jax.named_scope("panels"):
        panels = {0: own}
        for mask in range(2, R, 2):
            panels[mask] = exchange(own, mask, R)
        panels[C], sh, sl = call(bind(order), (), (), passed=(panels[C], sh, sl))
        for mask in range(0, R, 2):
            panels[mask + 1] = exchange(panels[mask], 1, R)
    with jax.named_scope("shares_of"):
        pair = lambda rows, cols: [((rows, cols), bf16)] * 2
        *shares, gh, gl, top = call(
            bind(shares_of),
            vmem(sh, sl, *[panels[m] for m in range(R)]),
            [(s.slots * s.share, 2 * W)] * C
            + pair(live, 2 * W)
            + [(W, W)],
            [pltpu.VMEM((s.CC + 1, 2 * W, B), bf16)] * 2
            + [pltpu.VMEM((live, 2 * W), f32)],
        )
    with jax.named_scope("tops"):
        th, tl, ih, il, base, extra = call(
            bind(tops),
            vmem(parent_diagonal, top),
            pair(W, W) + pair(W, W) + [(ws, W), (W, W)],
        )
    with jax.named_scope("products"):
        lh, ll, gh, gl = call(
            bind(collect),
            vmem(*[owned[m] for m in range(C)]),
            pair(2 * W, live),
            ahead=3e9,
            passed=(gh, gl),
        )
        stays, send = call(
            bind(products),
            vmem(gh, gl, th, tl, ih, il, extra, lh, ll),
            [(3 * W // 2, W)] * 2,
            [pltpu.VMEM((3 * W, W), f32)],
        )
    with jax.named_scope("sum_core"):
        got = exchange(send, 1, R)
    with jax.named_scope("sum_shares"):
        arrived, mask = [shares[0]], 1
        while mask < C:
            far = list(range(3 * mask, C, 2 * mask))
            if far:
                come = [flip(shares[m], mask, C) for m in far]
                to = [m ^ mask for m in far]
                added = call(
                    bind(plus),
                    vmem(*[shares[m] for m in to], *come),
                    [shares[0].shape] * len(far),
                    ahead=6e9,
                )
                for m, value in zip(to, added):
                    shares[m] = value
            mask *= 2
    with jax.named_scope("sum_chips"):
        *mine, shares[2] = call(
            bind(add_chips),
            vmem(stays, got),
            [(C * 3 * s.eight, W)] * s.chips,
            passed=(shares[2],),
        )
        mine = [mine[0]] + [exchange(mine[m], 2 * m, R) for m in range(s.chips - 1, 0, -1)]

    with jax.named_scope("sum_shares"):
        mask = 1
        while mask < C:
            arrived.append(flip(shares[mask], mask, C))
            mask *= 2
    with jax.named_scope("sum_cols"):
        scr = [pltpu.VMEM((C * 3 * s.eight, W), f32)]
        cols = call(bind(add_cols), vmem(*mine), [(3 * s.eight, W)] * C, scr)
        cols = [cols[0]] + [shift(cols[k], k, C) for k in range(1, C)]
    with jax.named_scope("rows_out"):
        parent_rows, child_rows = call(
            bind(rows_out),
            smem(parent_blocks, parent_sizes, child_sizes) + vmem(th, tl, *arrived),
            [(s.RC * s.share, W)] * 2,
        )
    with jax.named_scope("spread"):
        done, parent_rows, child_rows = call(
            bind(add_all), vmem(*cols), [(3 * s.eight, W)], passed=(parent_rows, child_rows)
        )
        parts = {0: done}
        for mask in range(R - 2, 0, -2):
            parts[mask] = exchange(done, mask, R)
    with jax.named_scope("spread"):
        for mask in range(0, R, 2):
            parts[mask + 1] = exchange(parts[mask], 1, R)
    with jax.named_scope("finish"):
        parent_diag, child_upper, child_diag = call(
            bind(finish),
            vmem(parent_diagonal, child_diagonal, base, *[parts[m] for m in range(R)]),
            [(ws, W)] * 3,
        )
    shape = (s.RC, 1, s.share, W)
    return (
        parent_rows.reshape(shape),
        parent_diag,
        child_rows.reshape(shape),
        child_upper,
        child_diag,
    )


highest = lax.Precision.HIGHEST


def from_root(value, axis, source):
    kept = jnp.where(lax.axis_index(axis) == source, value, 0).astype(value.dtype)
    return lax.psum(kept, axis)


def live_rows(sizes, block_rows):
    return (jnp.arange(block_rows, dtype=jnp.int32)[None, :] < sizes[:, None]).astype(jnp.float32)


def own_share(widened, blocks, row_live, row_index, row_total, col_index, row_share, local_rows):
    wanted = jnp.arange(local_rows, dtype=jnp.int32) * row_total + row_index
    onehot = (blocks[None, :] == wanted[:, None]).astype(jnp.float32)
    sliced = lax.dynamic_slice_in_dim(widened, col_index * row_share, row_share, 2)
    own_rows = jnp.einsum("rk,wkb->rbw", onehot, sliced, precision=highest)
    live_part = lax.dynamic_slice_in_dim(row_live, col_index * row_share, row_share, 1)
    row_alive = jnp.einsum("rk,kb->rb", onehot, live_part, precision=highest)
    return (own_rows, row_alive)


def add_columns(column_dense, widened, blocks, col_index, col_total):
    wanted = jnp.arange(column_dense.shape[0], dtype=jnp.int32) * col_total + col_index
    onehot = (blocks[None, :] == wanted[:, None]).astype(jnp.float32)
    return column_dense + jnp.einsum("ck,wky->cwy", onehot, widened, precision=highest)


def column_panel(widened, blocks, col_index, col_total, row_total, col_blocks):
    column_dense = jnp.zeros((col_blocks, widened.shape[0], widened.shape[2]), jnp.float32)
    for repeat in range(row_total // col_total):
        sender = col_index + repeat * col_total
        heard_panel, heard_blocks = (
            from_root(widened, "row", sender),
            from_root(blocks, "row", sender),
        )
        column_dense = add_columns(column_dense, heard_panel, heard_blocks, col_index, col_total)
    return column_dense


def child_panels(
    child_panel, child_top, child_live, child_blocks, col_index, col_total, row_total, col_blocks
):
    wide_child, top_full = (
        lax.all_gather(child_panel, "col", axis=0, tiled=True),
        lax.all_gather(child_top, "col", axis=0, tiled=True),
    )
    child_full = wide_child * child_live[None, :, :]
    child_dense = column_panel(
        child_full, child_blocks, col_index, col_total, row_total, col_blocks
    )
    return (child_full, child_dense, top_full)


def apply_inverse(cached, column_dense):
    summed = lax.psum_scatter(
        jnp.einsum(
            "rxcy,cwy->xrw",
            cached,
            column_dense,
            precision=highest,
            preferred_element_type=jnp.float32,
        ),
        "col",
        scatter_dimension=0,
        tiled=True,
    )
    return jnp.transpose(summed, (1, 0, 2))


def diagonal_sum(partial_rows, panel_width, col_share, col_index):
    entire = lax.psum(partial_rows(0, panel_width), ("row", "col"))
    return lax.dynamic_slice_in_dim(entire, col_index * col_share, col_share, 0)


def body(
    cached_inverse,
    parent_panel,
    parent_blocks,
    parent_sizes,
    parent_diagonal,
    child_panel,
    child_top,
    child_blocks,
    child_sizes,
    child_diagonal,
):
    row_total = lax.axis_size("row")
    col_total = lax.axis_size("col")
    row_index = lax.axis_index("row")
    col_index = lax.axis_index("col")
    local_rows = cached_inverse.shape[0]
    block_rows = cached_inverse.shape[2]
    col_blocks = cached_inverse.shape[3]
    cached = cached_inverse.reshape(local_rows, block_rows, col_blocks, block_rows)
    panel_width = parent_diagonal.shape[1]
    row_share = block_rows // col_total
    col_share = panel_width // col_total
    parent_live = live_rows(parent_sizes, block_rows)
    child_live = live_rows(child_sizes, block_rows)
    wide_parent = lax.all_gather(parent_panel, "col", axis=0, tiled=True)
    parent_full = wide_parent * parent_live[None, :, :]
    parent_dense = column_panel(
        parent_full, parent_blocks, col_index, col_total, row_total, col_blocks
    )
    child_full, child_dense, top_full = child_panels(
        child_panel,
        child_top,
        child_live,
        child_blocks,
        col_index,
        col_total,
        row_total,
        col_blocks,
    )
    parent_own, parent_alive = own_share(
        parent_full,
        parent_blocks,
        parent_live,
        row_index,
        row_total,
        col_index,
        row_share,
        local_rows,
    )
    both_local = apply_inverse(cached, jnp.concatenate([parent_dense, child_dense], axis=1))
    parent_local = -both_local[:, :, :panel_width] * parent_alive[:, :, None]
    child_own, child_alive = own_share(
        child_full, child_blocks, child_live, row_index, row_total, col_index, row_share, local_rows
    )
    carried = jnp.einsum("rbw,wv->rbv", parent_local, top_full, precision=highest)
    child_local = -(both_local[:, :, panel_width:] + carried) * child_alive[:, :, None]

    def stacked_terms(offset, amount):
        first_part = jnp.einsum("rbw,rbv->wv", parent_own, parent_local, precision=highest)
        second_part = jnp.einsum("rbw,rbv->wv", parent_local, child_own, precision=highest)
        third_part = jnp.einsum("rbc,rbv->cv", child_own, child_local, precision=highest)
        return jnp.concatenate([first_part, second_part, third_part], axis=1)

    stacked_sum = diagonal_sum(stacked_terms, panel_width, col_share, col_index)
    parent_diag = parent_diagonal - stacked_sum[:, :panel_width]
    child_upper = -(
        jnp.dot(parent_diag, top_full, precision=highest, preferred_element_type=jnp.float32)
        + stacked_sum[:, panel_width : 2 * panel_width]
    )
    upper_whole = lax.all_gather(child_upper, "col", axis=0, tiled=True)
    top_columns = lax.dynamic_slice_in_dim(top_full, col_index * col_share, col_share, 1)
    child_diag = (
        child_diagonal
        - jnp.dot(top_columns.T, upper_whole, precision=highest, preferred_element_type=jnp.float32)
        - stacked_sum[:, 2 * panel_width :]
    )
    return (
        parent_local[:, None, :, :],
        parent_diag,
        child_local[:, None, :, :],
        child_upper,
        child_diag,
    )


def fits(rows, cols, panel, cached, width):
    s = Shape(rows, cols, panel, cached, width)
    return (
        rows & (rows - 1) == 0
        and cols & (cols - 1) == 0
        and rows % cols == 0
        and cols > 2
        and s.Q == 2
        and width == 2 * s.B
        and s.ws % 16 == 0
        and s.share % 16 == 0
        and s.ws % rows == 0
        and s.eight % 8 == 0
        and width % s.B == 0
    )


def chosen(*args):
    sizes = lax.axis_size("row"), lax.axis_size("col")
    ok = fits(*sizes, args[1], args[0], args[4].shape[1])
    return (fast_body if ok else body)(*args)


def solution(mesh):
    in_specs = (
        P(None, "row", None, None, "col", None),
        P("col", "row", None),
        P("row"),
        P("row"),
        P("col", None),
        P("col", "row", None),
        P("col", None),
        P("row"),
        P("row"),
        P("col", None),
    )
    out_specs = (
        P(None, "row", "col", None),
        P("col", None),
        P(None, "row", "col", None),
        P("col", None),
        P("col", None),
    )
    return jax.shard_map(chosen, mesh=mesh, in_specs=in_specs, out_specs=out_specs, check_vma=False)
```
